128 devices in a mesh: gx: 16 (over x, z), gy: 8 (over y, core).
Axes of the slice: x: 4, y: 4, z: 4, core: 2. Of those that a mesh axis runs over, the one named last changes fastest.
Arguments:
- features: bfloat16 [128, 32, 32, 256], P(None, 'gx', 'gy'), may hold values from -6 to 6
- labels: int32 [32, 32, 256], P('gx', 'gy'), may hold values from 0 to 3
- w_down: bfloat16 [2, 2, 2, 256, 128], replicated, may hold values from -0.1875 to 0.1875
- w_mid: bfloat16 [3, 3, 3, 256, 256], replicated, may hold values from -0.078125 to 0.078125
- w_up: bfloat16 [4, 4, 4, 128, 256], replicated, may hold values from -0.125 to 0.125
- w_head: bfloat16 [4, 128], replicated, may hold values from -0.5 to 0.5
Outputs:
- feature_grad: bfloat16 [128, 32, 32, 256], P(None, 'gx', 'gy')
- mid_weight_grad: bfloat16 [3, 3, 3, 256, 256], replicated
- up_weight_grad: bfloat16 [4, 4, 4, 128, 256], replicated
The draws below stay inside these ranges and needn't reach their ends.
All inputs are finite; a program needn't handle non-finite values.
Results may differ from the reference program's by a relative error of at most 0.0085.
Values may be sent and summed in bfloat16 or wider, within the bound.
A program may use at most 128 MiB of HBM per device.

```python
import math
import jax
import jax.numpy as jnp

C4 = 128
C5 = 256
KC = 4
NZ4 = 256
NX4 = 32
NY4 = 32


def place_ends(values, stream_key, least, largest):
    shape = values.shape
    place = [jax.random.randint(jax.random.fold_in(stream_key, axis), (), 0, shape[axis]) for axis in range(len(shape))]
    values = values.at[tuple(place)].set(least)
    longest = shape.index(max(shape))
    place[longest] = (place[longest] + 1) % shape[longest]
    return values.at[tuple(place)].set(largest)


def levels(own_key, shape, cuts, least, largest):
    gain, own = 1.0, jax.random.fold_in(own_key, 6)
    for axis_at, blocks in cuts:
        heights = jnp.exp(jax.random.uniform(jax.random.fold_in(own, axis_at), (blocks,), jnp.float32, least / len(cuts), largest / len(cuts)))
        gain = gain * jnp.repeat(heights, shape[axis_at] // blocks).reshape([-1 if axis == axis_at else 1 for axis in range(len(shape))])
    return gain


def noise(rng, dims, deviation, reach, split=(), kind=jnp.bfloat16):
    drawn = jax.random.normal(rng, dims, jnp.float32) * deviation
    if len(split) > 0:
        drawn = levels(rng, dims, split, -0.22, 0.18) * drawn
    return jnp.clip(drawn, min=-reach, max=reach).astype(kind)


def setup_inputs(seed: int = 0) -> dict:
    key_of = jax.random.split(jax.random.key(seed), 7)
    features = noise(key_of[0], (C4, NX4, NY4, NZ4), 1.0, 6.0, ((1, 16), (2, 8)))
    labels = place_ends(jax.random.randint(key_of[1], (NX4, NY4, NZ4), 0, KC), jax.random.fold_in(key_of[1], 1), 0, KC - 1).astype(jnp.int32)
    w_down = noise(key_of[2], (2, 2, 2, C5, C4), (8 * C4) ** -0.5, 0.1875)
    w_mid = noise(key_of[3], (3, 3, 3, C5, C5), (27 * C5) ** -0.5, 0.078125)
    w_up = noise(key_of[4], (4, 4, 4, C4, C5), (8 * C5) ** -0.5, 0.125)
    w_head = noise(key_of[5], (KC, C4), C4 ** -0.5, 0.5)
    return {"features": features, "labels": labels, "w_down": w_down, "w_mid": w_mid, "w_up": w_up, "w_head": w_head}


def silu_slope(value):
    gate = jax.nn.sigmoid(value)
    return gate * (1.0 + value * (1.0 - gate))

def alternate(blocks):
    layers = []
    for a in (0, 1):
        planes = []
        for b in (0, 1):
            planes.append(jnp.stack([blocks[a, b, 0], blocks[a, b, 1]], axis=4))
        layers.append(jnp.stack(planes, axis=3))
    whole = jnp.stack(layers, axis=2)
    return whole.reshape(whole.shape[0], 2 * whole.shape[1], 2 * whole.shape[3], 2 * whole.shape[5])

def apply_taps(weight, field):
    return jnp.einsum('oi,ixyz->oxyz', weight.astype(jnp.float32), field.astype(jnp.float32))

def apply_back(weight, field):
    return jnp.einsum('oi,oxyz->ixyz', weight.astype(jnp.float32), field.astype(jnp.float32))

def outer_sum(left, right):
    return jnp.einsum('oxyz,ixyz->oi', left.astype(jnp.float32), right.astype(jnp.float32))

def reference(features, labels, w_down, w_mid, w_up, w_head):
    sx, sy, sz = (NX4 // 2, NY4 // 2, NZ4 // 2)
    down_pre = jnp.zeros((C5, sx, sy, sz), jnp.float32)
    for a in (0, 1):
        for b in (0, 1):
            for c in (0, 1):
                down_pre = down_pre + apply_taps(w_down[a, b, c], features[:, a::2, b::2, c::2])
    low = jax.nn.silu(down_pre).astype(jnp.bfloat16)
    low_pad = jnp.pad(low, ((0, 0), (1, 1), (1, 1), (1, 1)))
    mid_pre = jnp.zeros((C5, sx, sy, sz), jnp.float32)
    for a in range(3):
        for b in range(3):
            for c in range(3):
                mid_pre = mid_pre + apply_taps(w_mid[a, b, c], low_pad[:, a:a + sx, b:b + sy, c:c + sz])
    mid = jax.nn.silu(mid_pre).astype(jnp.bfloat16)
    blocks = {}
    for a in (0, 1):
        for b in (0, 1):
            for c in (0, 1):
                total = jnp.zeros((C4, sx + 1, sy + 1, sz + 1), jnp.float32)
                for u in (0, 1):
                    for v in (0, 1):
                        for w in (0, 1):
                            part = apply_taps(w_up[2 * u + a, 2 * v + b, 2 * w + c], mid)
                            total = total + jnp.pad(part, ((0, 0), (u, 1 - u), (v, 1 - v), (w, 1 - w)))
                blocks[a, b, c] = total
    upward = alternate(blocks)[:, 1:-1, 1:-1, 1:-1]
    hidden = (upward + features.astype(jnp.float32)).astype(jnp.bfloat16)
    logits = jnp.einsum('ko,oxyz->kxyz', w_head.astype(jnp.float32), hidden.astype(jnp.float32))
    classes = jnp.arange(KC, dtype=jnp.int32)[:, None, None, None]
    target = (labels[None] == classes).astype(jnp.float32)
    logit_grad = (jax.nn.sigmoid(logits) - target).astype(jnp.bfloat16)
    hidden_grad = apply_back(w_head, logit_grad).astype(jnp.bfloat16)
    grad_pad = jnp.pad(hidden_grad, ((0, 0), (1, 1), (1, 1), (1, 1)))
    mid_grad = jnp.zeros((C5, sx, sy, sz), jnp.float32)
    up_terms = []
    for a in range(4):
        for b in range(4):
            for c in range(4):
                piece = grad_pad[:, a:a + 2 * sx:2, b:b + 2 * sy:2, c:c + 2 * sz:2]
                mid_grad = mid_grad + apply_back(w_up[a, b, c], piece)
                up_terms.append(outer_sum(piece, mid))
    scale = 1.0 / math.sqrt(sx * sy * sz)
    up_sum = jnp.stack(up_terms).reshape(4, 4, 4, C4, C5)
    mid_pre_grad = (mid_grad * silu_slope(mid_pre)).astype(jnp.bfloat16)
    back_pad = jnp.pad(mid_pre_grad, ((0, 0), (1, 1), (1, 1), (1, 1)))
    low_grad = jnp.zeros((C5, sx, sy, sz), jnp.float32)
    mid_terms = []
    for a in range(3):
        for b in range(3):
            for c in range(3):
                low_grad = low_grad + apply_back(w_mid[a, b, c], back_pad[:, 2 - a:2 - a + sx, 2 - b:2 - b + sy, 2 - c:2 - c + sz])
                mid_terms.append(outer_sum(mid_pre_grad, low_pad[:, a:a + sx, b:b + sy, c:c + sz]))
    mid_sum = jnp.stack(mid_terms).reshape(3, 3, 3, C5, C5)
    down_grad = (low_grad * silu_slope(down_pre)).astype(jnp.bfloat16)
    pieces = {}
    for a in (0, 1):
        for b in (0, 1):
            for c in (0, 1):
                pieces[a, b, c] = apply_back(w_down[a, b, c], down_grad)
    feature_grad = (alternate(pieces) + hidden_grad.astype(jnp.float32)).astype(jnp.bfloat16)
    return (feature_grad, (mid_sum * scale).astype(jnp.bfloat16), (up_sum * scale).astype(jnp.bfloat16))
```

```python
import math

import jax
import jax.numpy as jnp
from jax import lax
from jax.sharding import PartitionSpec as P


def padded(cells, sides, width):
    for axis, dim in sides:
        count = lax.axis_size(axis)
        ends = count - 1
        head = lax.slice_in_dim(cells, 0, width, axis=dim)
        tail = lax.slice_in_dim(cells, cells.shape[dim] - width, cells.shape[dim], axis=dim)
        cells = jnp.concatenate(
            [
                lax.ppermute(tail, axis, [(i, (i + 1) % count) for i in range(ends)]),
                cells,
                lax.ppermute(head, axis, [((i + 1) % count, i) for i in range(ends)]),
            ],
            axis=dim,
        )
    return cells


def shifted(block, axis, distance):
    devices = range(lax.axis_size(axis))
    route = [(i - distance, i) for i in devices if i - distance in devices]
    return lax.ppermute(block, axis, route)


def for_sending(shard):

    def short(part):
        return part.astype(jnp.bfloat16) if part.dtype == jnp.float32 else part

    return jax.tree.map(short, shard)


def silu_slope(value):
    gate = jax.nn.sigmoid(value)
    return gate * (1.0 + value * (1.0 - gate))


def stride_table(full, half, offset, kind):
    rows = lax.broadcasted_iota(jnp.int32, (full, half), 0)
    cols = lax.broadcasted_iota(jnp.int32, (full, half), 1)
    return (rows == 2 * cols + offset).astype(kind)


def shift_table(count, offset):
    rows = lax.broadcasted_iota(jnp.int32, (count, count), 0)
    cols = lax.broadcasted_iota(jnp.int32, (count, count), 1)
    return (rows == cols + offset).astype(jnp.bfloat16)


def depth_select(field, table):
    return jnp.einsum("cxyz,zk->cxyk", field, table, preferred_element_type=jnp.float32).astype(
        jnp.bfloat16
    )


def depth_spread(field, table):
    return jnp.einsum(
        "cxyk,zk->cxyz",
        field,
        table,
        preferred_element_type=jnp.float32,
        precision=lax.Precision.HIGHEST,
    )


def alternate_plane(blocks):
    layers = []
    for a in (0, 1):
        layers.append(jnp.stack([blocks[a, 0], blocks[a, 1]], axis=3))
    whole = jnp.stack(layers, axis=2)
    return whole.reshape(whole.shape[0], 2 * whole.shape[1], 2 * whole.shape[3], whole.shape[5])


def apply_taps(weight, field):
    return jnp.einsum("oi,ixyz->oxyz", weight, field, preferred_element_type=jnp.float32)


def apply_back(weight, field):
    return jnp.einsum("oi,oxyz->ixyz", weight, field, preferred_element_type=jnp.float32)


def outer_sum(left, right):
    return jnp.einsum("oxyz,ixyz->oi", left, right, preferred_element_type=jnp.float32)


def add_edges(inner, before, after, axis):
    count = inner.shape[axis]
    first = lax.slice_in_dim(inner, 0, 1, axis=axis) + before
    middle = lax.slice_in_dim(inner, 1, count - 1, axis=axis)
    last = lax.slice_in_dim(inner, count - 1, count, axis=axis) + after
    return jnp.concatenate([first, middle, last], axis=axis)


def local(features, labels, w_down, w_mid, w_up, w_head):
    chans_up, bx4, by4, nz4 = features.shape
    chans_mid = w_mid.shape[3]
    sx, sy, sz = (bx4 // 2, by4 // 2, nz4 // 2)
    down_pre = jnp.zeros((chans_mid, sx, sy, sz), jnp.float32)
    for c in (0, 1):
        depth_part = depth_select(features, stride_table(nz4, sz, c, jnp.bfloat16))
        for a in (0, 1):
            for b in (0, 1):
                down_pre = down_pre + apply_taps(w_down[a, b, c], depth_part[:, a::2, b::2])
    low = jax.nn.silu(down_pre).astype(jnp.bfloat16)
    low_halo = padded(low, (("gx", 1), ("gy", 2)), 1)
    low_moved = [depth_select(low_halo, shift_table(sz, c - 1)) for c in range(3)]
    mid_pre = jnp.zeros((chans_mid, sx, sy, sz), jnp.float32)
    for a in range(3):
        for b in range(3):
            for c in range(3):
                mid_pre = mid_pre + apply_taps(
                    w_mid[a, b, c], low_moved[c][:, a : a + sx, b : b + sy]
                )
    mid = jax.nn.silu(mid_pre).astype(jnp.bfloat16)
    spreads = [stride_table(nz4, sz, t - 1, jnp.float32) for t in range(4)]
    blocks = {}
    for a in (0, 1):
        for b in (0, 1):
            total = jnp.zeros((chans_up, sx + 1, sy + 1, nz4), jnp.float32)
            for tap_z in range(4):
                gathered = jnp.zeros((chans_up, sx + 1, sy + 1, sz), jnp.float32)
                for u in (0, 1):
                    for v in (0, 1):
                        part = apply_taps(w_up[2 * u + a, 2 * v + b, tap_z], mid)
                        gathered = gathered + jnp.pad(
                            part, ((0, 0), (u, 1 - u), (v, 1 - v), (0, 0))
                        )
                total = total + depth_spread(gathered, spreads[tap_z])
            blocks[a, b] = total
    extended = alternate_plane(blocks)
    from_before = shifted(extended[:, -1:].astype(jnp.bfloat16), "gx", 1).astype(jnp.float32)
    from_after = shifted(extended[:, :1].astype(jnp.bfloat16), "gx", -1).astype(jnp.float32)
    inner = add_edges(extended[:, 1:-1], from_before, from_after, 1)
    side_before = shifted(for_sending(inner[:, :, -1:]), "gy", 1)
    side_after = shifted(for_sending(inner[:, :, :1]), "gy", -1)
    upward = add_edges(inner[:, :, 1:-1], side_before, side_after, 2)
    hidden = (upward + features.astype(jnp.float32)).astype(jnp.bfloat16)
    logits = jnp.einsum("ko,oxyz->kxyz", w_head, hidden, preferred_element_type=jnp.float32)
    classes = jnp.arange(w_head.shape[0], dtype=jnp.int32)[:, None, None, None]
    target = (labels[None] == classes).astype(jnp.float32)
    logit_grad = (jax.nn.sigmoid(logits) - target).astype(jnp.bfloat16)
    hidden_grad = apply_back(w_head, logit_grad).astype(jnp.bfloat16)
    grad_halo = padded(hidden_grad, (("gx", 1), ("gy", 2)), 1)
    grad_depth = [
        depth_select(grad_halo, stride_table(nz4, sz, c - 1, jnp.bfloat16)) for c in range(4)
    ]
    mid_grad = jnp.zeros((chans_mid, sx, sy, sz), jnp.float32)
    up_terms = []
    for a in range(4):
        for b in range(4):
            for c in range(4):
                piece = grad_depth[c][:, a : a + 2 * sx : 2, b : b + 2 * sy : 2]
                mid_grad = mid_grad + apply_back(w_up[a, b, c], piece)
                up_terms.append(outer_sum(piece, mid))
    cells = sx * sy * sz * lax.axis_size("gx") * lax.axis_size("gy")
    scale = 1.0 / math.sqrt(cells)
    up_local = jnp.stack(up_terms).reshape(4, 4, 4, chans_up, chans_mid)
    mid_pre_grad = (mid_grad * silu_slope(mid_pre)).astype(jnp.bfloat16)
    back_halo = padded(mid_pre_grad, (("gx", 1), ("gy", 2)), 1)
    back_moved = [depth_select(back_halo, shift_table(sz, 1 - c)) for c in range(3)]
    low_grad = jnp.zeros((chans_mid, sx, sy, sz), jnp.float32)
    mid_terms = []
    for a in range(3):
        for b in range(3):
            for c in range(3):
                low_grad = low_grad + apply_back(
                    w_mid[a, b, c], back_moved[c][:, 2 - a : 2 - a + sx, 2 - b : 2 - b + sy]
                )
                mid_terms.append(outer_sum(mid_pre_grad, low_moved[c][:, a : a + sx, b : b + sy]))
    mid_local = jnp.stack(mid_terms).reshape(3, 3, 3, chans_mid, chans_mid)
    up_sum = lax.psum(up_local.astype(jnp.bfloat16), ("gx", "gy"))
    mid_sum = lax.psum(mid_local.astype(jnp.bfloat16), ("gx", "gy"))
    mid_out = (mid_sum.astype(jnp.float32) * scale).astype(jnp.bfloat16)
    up_out = (up_sum.astype(jnp.float32) * scale).astype(jnp.bfloat16)
    down_grad = (low_grad * silu_slope(down_pre)).astype(jnp.bfloat16)
    pieces = {}
    for a in (0, 1):
        for b in (0, 1):
            full_depth = jnp.zeros((chans_up, sx, sy, nz4), jnp.float32)
            for c in (0, 1):
                full_depth = full_depth + depth_spread(
                    apply_back(w_down[a, b, c], down_grad), stride_table(nz4, sz, c, jnp.float32)
                )
            pieces[a, b] = full_depth
    feature_grad = (alternate_plane(pieces) + hidden_grad.astype(jnp.float32)).astype(jnp.bfloat16)
    return (feature_grad, mid_out, up_out)


def solution(mesh):
    return jax.shard_map(
        local,
        mesh=mesh,
        in_specs=(P(None, "gx", "gy", None), P("gx", "gy", None), P(), P(), P(), P()),
        out_specs=(P(None, "gx", "gy", None), P(), P()),
        check_vma=False,
    )
```

```python
import functools
import math

import jax
import jax.numpy as jnp
from jax import lax
from jax.experimental import pallas as pl
from jax.experimental.pallas import tpu as pltpu
from jax.sharding import PartitionSpec as P

MESH = pl.DeviceIdType.MESH
ROWS = 15360
PART = ROWS // 3
UNIT = 80
STEP = 80


def my_place():
    gx, gy = lax.axis_index("gx"), lax.axis_index("gy")
    return lax.div(gx, 4), lax.div(gy, 2), lax.rem(gx, 4), lax.rem(gy, 2)


def device_at(x, y, z, core):
    return (x * 4 + z, y * 2 + core)


def moved(place, axis, distance):
    spot = list(place)
    spot[axis] = lax.rem(spot[axis] + distance, 4)
    return device_at(*spot)


def rows_at(start, count):
    return pl.ds(pl.multiple_of(start, 16), count)


def for_rows(count, body):
    def step(i, carry):
        body(i * STEP)
        return carry

    lax.fori_loop(0, count // STEP, step, 0)


def reduce_kernel(scale, part, out, work, got, half1, half2, half3, slab1, slab2, slab3,
                  sum1, sum2, res, send_sem, recv_sem):
    place = my_place()
    core = place[3]
    other = device_at(place[0], place[1], place[2], 1 - core)
    barrier = pltpu.get_barrier_semaphore()
    pl.semaphore_signal(barrier, inc=1, device_id=other, device_id_type=MESH)
    for axis in range(3):
        for distance in (1, 3):
            pl.semaphore_signal(
                barrier, inc=1, device_id=moved(place, axis, distance), device_id_type=MESH
            )
    pl.semaphore_wait(barrier, 7)

    count = [0]

    def send(src, dst, target):
        index = count[0]
        count[0] += 1
        copy = pltpu.make_async_remote_copy(
            src_ref=src, dst_ref=dst, send_sem=send_sem.at[index], recv_sem=recv_sem.at[index],
            device_id=target, device_id_type=MESH,
        )
        copy.start()
        return copy

    def local_copy(src, dst):
        index = count[0]
        count[0] += 1
        copy = pltpu.make_async_copy(src, dst, send_sem.at[index])
        copy.start()
        return copy

    def lanes(which):
        return pl.ds(pl.multiple_of(which * 128, 128), 128)

    sent = []
    first = []
    for k in range(3):
        rows = pl.ds(k * PART, PART)
        far = send(part.at[rows, lanes(1 - core)], got.at[rows], other)
        near = local_copy(part.at[rows, lanes(core)], work.at[rows])
        first.append((far, near))
        sent.append(far)

    axes = [(0, 1, 2), (1, 2, 0), (2, 0, 1)]
    sizes = [(16 * UNIT, 8 * UNIT), (4 * UNIT, 2 * UNIT), (UNIT, 48)]
    halves = (half1, half2, half3)
    slabs = (slab1, slab2, slab3)

    def spots(k, level):
        p = place[axes[k][level]]
        return p, lax.rem(p + 1, 4), lax.rem(p + 2, 4), lax.rem(p + 3, 4)

    def open_level(k, level, src, base):
        size, cut = sizes[level]
        _, up, far, down = spots(k, level)
        after = moved(place, axes[k][level], 1)
        before = moved(place, axes[k][level], 3)
        half, slab = halves[level], slabs[level]
        copies = [
            send(src.at[rows_at(base + far * size, cut)], half.at[k, 0, pl.ds(0, cut)], after),
            send(src.at[rows_at(base + far * size + cut, size - cut)],
                 half.at[k, 1, pl.ds(0, size - cut)], before),
            send(src.at[rows_at(base + up * size + cut, size - cut)],
                 slab.at[k, 0, pl.ds(cut, size - cut)], after),
            send(src.at[rows_at(base + down * size, cut)], slab.at[k, 1, pl.ds(0, cut)], before),
        ]
        sent.extend(copies)
        return copies

    def pass_on(k, level, src, base, copies):
        size, cut = sizes[level]
        _, up, _, down = spots(k, level)
        after = moved(place, axes[k][level], 1)
        before = moved(place, axes[k][level], 3)
        half, slab = halves[level], slabs[level]
        copies[0].wait_recv()
        rows = rows_at(base + up * size, cut)
        add_into(src, base + up * size, half.at[k, 0], cut)
        copies.append(send(src.at[rows], slab.at[k, 0, pl.ds(0, cut)], after))
        copies[1].wait_recv()
        rows = rows_at(base + down * size + cut, size - cut)
        add_into(src, base + down * size + cut, half.at[k, 1], size - cut)
        copies.append(send(src.at[rows], slab.at[k, 1, pl.ds(cut, size - cut)], before))
        sent.extend(copies[4:])

    def add_into(dst, start, src, total):
        step = STEP if total % STEP == 0 else 16

        def body(i, carry):
            rows = rows_at(start + i * step, step)
            dst[rows] = dst[rows] + src[rows_at(i * step, step)]
            return carry

        lax.fori_loop(0, total // step, body, 0)

    def close_level(k, level, src, base, copies, store):
        size, _ = sizes[level]
        own = spots(k, level)[0]
        for copy in copies[2:]:
            copy.wait_recv()
        slab = slabs[level]

        def body(start):
            rows = rows_at(start, STEP)
            total = src[rows_at(base + own * size + start, STEP)].astype(jnp.float32)
            total = total + slab[k, 0, rows].astype(jnp.float32)
            total = total + slab[k, 1, rows].astype(jnp.float32)
            store(start, total)

        for_rows(size, body)

    opened = []
    for k in range(3):
        far, near = first[k]
        near.wait()
        far.wait_recv()

        def add_first(start):
            rows = rows_at(k * PART + start, STEP)
            work[rows] = work[rows] + got[rows]

        for_rows(PART, add_first)
        opened.append(open_level(k, 0, work, k * PART))
    for k in range(3):
        pass_on(k, 0, work, k * PART, opened[k])
    for level, src, dst in ((0, work, sum1), (1, sum1, sum2)):
        size = sizes[level][0]
        later = []
        for k in range(3):
            base = k * 4 * size

            def store(start, total):
                dst[rows_at(k * size + start, STEP)] = total.astype(jnp.bfloat16)

            close_level(k, level, src, base, opened[k], store)
            later.append(open_level(k, level + 1, dst, k * size))
        for k in range(3):
            pass_on(k, level + 1, dst, k * size, later[k])
        opened = later

    def spot_base(k, level):
        base = k * PART
        for upper in range(level):
            base = base + place[axes[k][upper]] * sizes[upper][0]
        return base

    def open_spread(k, level):
        size, _ = sizes[level]
        rows = rows_at(spot_base(k, level) + spots(k, level)[0] * size, size)
        copies = [
            send(res.at[rows], res.at[rows], moved(place, axes[k][level], 1)),
            send(res.at[rows], res.at[rows], moved(place, axes[k][level], 3)),
        ]
        sent.extend(copies)
        return copies

    outs = []

    def hand_out(rows):
        outs.append(local_copy(res.at[rows], out.at[rows, lanes(core)]))
        far = send(res.at[rows], out.at[rows, lanes(core)], other)
        sent.append(far)
        outs.append(far)

    def pass_spread(k, level, copies):
        size, cut = sizes[level]
        base = spot_base(k, level)
        _, up, _, down = spots(k, level)
        copies[0].wait_recv()
        rows = rows_at(base + down * size, cut)
        copies.append(send(res.at[rows], res.at[rows], moved(place, axes[k][level], 1)))
        copies[1].wait_recv()
        rows = rows_at(base + up * size + cut, size - cut)
        copies.append(send(res.at[rows], res.at[rows], moved(place, axes[k][level], 3)))
        sent.extend(copies[2:])
        if level == 0:
            hand_out(rows_at(base + down * size, size))
            hand_out(rows_at(base + up * size, size))

    spread = []
    for k in range(3):

        def keep(start, total):
            rows = rows_at(spot_base(k, 2) + spots(k, 2)[0] * UNIT + start, STEP)
            res[rows] = (total * scale).astype(jnp.bfloat16)

        close_level(k, 2, sum2, k * sizes[1][0], opened[k], keep)
        spread.append(open_spread(k, 2))
    for level in (2, 1, 0):
        size, cut = sizes[level]
        for k in range(3):
            pass_spread(k, level, spread[k])
        later = []
        for k in range(3):
            for copy in spread[k][2:]:
                copy.wait_recv()
            if level > 0:
                later.append(open_spread(k, level - 1))
                if level == 1:
                    hand_out(rows_at(spot_base(k, 0) + spots(k, 0)[0] * sizes[0][0], sizes[0][0]))
            else:
                hand_out(rows_at(spot_base(k, 0) + spots(k, 0)[2] * size, size))
        spread = later
    for copy in sent:
        copy.wait_send()
    for index, copy in enumerate(outs):
        if index % 2:
            copy.wait_recv()
        else:
            copy.wait()


def reduce_all(part, scale):
    buf = lambda *shape: pltpu.VMEM(shape, jnp.bfloat16)
    n_copies = 140
    return pl.pallas_call(
        functools.partial(reduce_kernel, scale),
        out_shape=jax.ShapeDtypeStruct((ROWS, 256), jnp.bfloat16),
        in_specs=[pl.BlockSpec(memory_space=pl.ANY)],
        out_specs=pl.BlockSpec(memory_space=pl.ANY),
        scratch_shapes=[
            buf(ROWS, 128), buf(ROWS, 128),
            buf(3, 2, 8 * UNIT, 128), buf(3, 2, 2 * UNIT, 128), buf(3, 2, 48, 128),
            buf(3, 2, 16 * UNIT, 128), buf(3, 2, 4 * UNIT, 128), buf(3, 2, UNIT, 128),
            buf(3 * 16 * UNIT, 128), buf(3 * 4 * UNIT, 128),
            buf(ROWS, 128),
            pltpu.SemaphoreType.DMA((n_copies,)),
            pltpu.SemaphoreType.DMA((n_copies,)),
        ],
        compiler_params=pltpu.CompilerParams(
            collective_id=7, has_side_effects=True, vmem_limit_bytes=56 * 2**20
        ),
        cost_estimate=pl.CostEstimate(flops=10**7, bytes_accessed=16 * 10**6, transcendentals=0),
        name="sum_over_devices",
    )(part)


def padded(cells, sides, width):
    for axis, dim in sides:
        count = lax.axis_size(axis)
        ends = count - 1
        head = lax.slice_in_dim(cells, 0, width, axis=dim)
        tail = lax.slice_in_dim(cells, cells.shape[dim] - width, cells.shape[dim], axis=dim)
        cells = jnp.concatenate(
            [
                lax.ppermute(tail, axis, [(i, (i + 1) % count) for i in range(ends)]),
                cells,
                lax.ppermute(head, axis, [((i + 1) % count, i) for i in range(ends)]),
            ],
            axis=dim,
        )
    return cells


def shifted(block, axis, distance):
    devices = range(lax.axis_size(axis))
    route = [(i - distance, i) for i in devices if i - distance in devices]
    return lax.ppermute(block, axis, route)


def for_sending(shard):

    def short(part):
        return part.astype(jnp.bfloat16) if part.dtype == jnp.float32 else part

    return jax.tree.map(short, shard)


def silu_slope(value):
    gate = jax.nn.sigmoid(value)
    return gate * (1.0 + value * (1.0 - gate))


def stride_table(full, half, offset, kind):
    rows = lax.broadcasted_iota(jnp.int32, (full, half), 0)
    cols = lax.broadcasted_iota(jnp.int32, (full, half), 1)
    return (rows == 2 * cols + offset).astype(kind)


def shift_table(count, offset):
    rows = lax.broadcasted_iota(jnp.int32, (count, count), 0)
    cols = lax.broadcasted_iota(jnp.int32, (count, count), 1)
    return (rows == cols + offset).astype(jnp.bfloat16)


def depth_select(field, table):
    return jnp.einsum("cxyz,zk->cxyk", field, table, preferred_element_type=jnp.float32).astype(
        jnp.bfloat16
    )


def depth_spread(field, table):
    return jnp.einsum(
        "cxyk,zk->cxyz",
        field,
        table,
        preferred_element_type=jnp.float32,
        precision=lax.Precision.HIGHEST,
    )


def alternate_plane(blocks):
    layers = []
    for a in (0, 1):
        layers.append(jnp.stack([blocks[a, 0], blocks[a, 1]], axis=3))
    whole = jnp.stack(layers, axis=2)
    return whole.reshape(whole.shape[0], 2 * whole.shape[1], 2 * whole.shape[3], whole.shape[5])


def apply_taps(weight, field):
    return jnp.einsum("oi,ixyz->oxyz", weight, field, preferred_element_type=jnp.float32)


def apply_back(weight, field):
    return jnp.einsum("oi,oxyz->ixyz", weight, field, preferred_element_type=jnp.float32)


def outer_sum(left, right):
    return jnp.einsum("oxyz,ixyz->oi", left, right, preferred_element_type=jnp.float32)


def add_edges(inner, before, after, axis):
    count = inner.shape[axis]
    first = lax.slice_in_dim(inner, 0, 1, axis=axis) + before
    middle = lax.slice_in_dim(inner, 1, count - 1, axis=axis)
    last = lax.slice_in_dim(inner, count - 1, count, axis=axis) + after
    return jnp.concatenate([first, middle, last], axis=axis)


def local(features, labels, w_down, w_mid, w_up, w_head):
    chans_up, bx4, by4, nz4 = features.shape
    chans_mid = w_mid.shape[3]
    sx, sy, sz = (bx4 // 2, by4 // 2, nz4 // 2)
    down_pre = jnp.zeros((chans_mid, sx, sy, sz), jnp.float32)
    for c in (0, 1):
        depth_part = depth_select(features, stride_table(nz4, sz, c, jnp.bfloat16))
        for a in (0, 1):
            for b in (0, 1):
                down_pre = down_pre + apply_taps(w_down[a, b, c], depth_part[:, a::2, b::2])
    low = jax.nn.silu(down_pre).astype(jnp.bfloat16)
    low_halo = padded(low, (("gx", 1), ("gy", 2)), 1)
    low_moved = [depth_select(low_halo, shift_table(sz, c - 1)) for c in range(3)]
    mid_pre = jnp.zeros((chans_mid, sx, sy, sz), jnp.float32)
    for a in range(3):
        for b in range(3):
            for c in range(3):
                mid_pre = mid_pre + apply_taps(
                    w_mid[a, b, c], low_moved[c][:, a : a + sx, b : b + sy]
                )
    mid = jax.nn.silu(mid_pre).astype(jnp.bfloat16)
    spreads = [stride_table(nz4, sz, t - 1, jnp.float32) for t in range(4)]
    blocks = {}
    for a in (0, 1):
        for b in (0, 1):
            total = jnp.zeros((chans_up, sx + 1, sy + 1, nz4), jnp.float32)
            for tap_z in range(4):
                gathered = jnp.zeros((chans_up, sx + 1, sy + 1, sz), jnp.float32)
                for u in (0, 1):
                    for v in (0, 1):
                        part = apply_taps(w_up[2 * u + a, 2 * v + b, tap_z], mid)
                        gathered = gathered + jnp.pad(
                            part, ((0, 0), (u, 1 - u), (v, 1 - v), (0, 0))
                        )
                total = total + depth_spread(gathered, spreads[tap_z])
            blocks[a, b] = total
    extended = alternate_plane(blocks)
    from_before = shifted(extended[:, -1:].astype(jnp.bfloat16), "gx", 1).astype(jnp.float32)
    from_after = shifted(extended[:, :1].astype(jnp.bfloat16), "gx", -1).astype(jnp.float32)
    inner = add_edges(extended[:, 1:-1], from_before, from_after, 1)
    side_before = shifted(for_sending(inner[:, :, -1:]), "gy", 1)
    side_after = shifted(for_sending(inner[:, :, :1]), "gy", -1)
    upward = add_edges(inner[:, :, 1:-1], side_before, side_after, 2)
    hidden = (upward + features.astype(jnp.float32)).astype(jnp.bfloat16)
    logits = jnp.einsum("ko,oxyz->kxyz", w_head, hidden, preferred_element_type=jnp.float32)
    classes = jnp.arange(w_head.shape[0], dtype=jnp.int32)[:, None, None, None]
    target = (labels[None] == classes).astype(jnp.float32)
    logit_grad = (jax.nn.sigmoid(logits) - target).astype(jnp.bfloat16)
    hidden_grad = apply_back(w_head, logit_grad).astype(jnp.bfloat16)
    grad_halo = padded(hidden_grad, (("gx", 1), ("gy", 2)), 1)
    grad_depth = [
        depth_select(grad_halo, stride_table(nz4, sz, c - 1, jnp.bfloat16)) for c in range(4)
    ]
    mid_grad = jnp.zeros((chans_mid, sx, sy, sz), jnp.float32)
    up_terms = []
    for a in range(4):
        for b in range(4):
            for c in range(4):
                piece = grad_depth[c][:, a : a + 2 * sx : 2, b : b + 2 * sy : 2]
                mid_grad = mid_grad + apply_back(w_up[a, b, c], piece)
                up_terms.append(outer_sum(piece, mid))
    cells = sx * sy * sz * lax.axis_size("gx") * lax.axis_size("gy")
    scale = 1.0 / math.sqrt(cells)
    up_local = jnp.stack(up_terms).reshape(4, 4, 4, chans_up, chans_mid)
    mid_pre_grad = (mid_grad * silu_slope(mid_pre)).astype(jnp.bfloat16)
    back_halo = padded(mid_pre_grad, (("gx", 1), ("gy", 2)), 1)
    back_moved = [depth_select(back_halo, shift_table(sz, 1 - c)) for c in range(3)]
    low_grad = jnp.zeros((chans_mid, sx, sy, sz), jnp.float32)
    mid_terms = []
    for a in range(3):
        for b in range(3):
            for c in range(3):
                low_grad = low_grad + apply_back(
                    w_mid[a, b, c], back_moved[c][:, 2 - a : 2 - a + sx, 2 - b : 2 - b + sy]
                )
                mid_terms.append(outer_sum(mid_pre_grad, low_moved[c][:, a : a + sx, b : b + sy]))
    mid_local = jnp.stack(mid_terms).reshape(3, 3, 3, chans_mid, chans_mid)
    part = jnp.concatenate(
        [
            up_local.reshape(-1, chans_mid).astype(jnp.bfloat16),
            mid_local.reshape(-1, chans_mid).astype(jnp.bfloat16),
            jnp.zeros((256, chans_mid), jnp.bfloat16),
        ]
    )
    total = reduce_all(part, scale)
    up_rows, mid_rows = 64 * chans_up, 27 * chans_mid
    up_out = total[:up_rows].reshape(4, 4, 4, chans_up, chans_mid)
    mid_out = total[up_rows : up_rows + mid_rows].reshape(3, 3, 3, chans_mid, chans_mid)
    down_grad = (low_grad * silu_slope(down_pre)).astype(jnp.bfloat16)
    pieces = {}
    for a in (0, 1):
        for b in (0, 1):
            full_depth = jnp.zeros((chans_up, sx, sy, nz4), jnp.float32)
            for c in (0, 1):
                full_depth = full_depth + depth_spread(
                    apply_back(w_down[a, b, c], down_grad), stride_table(nz4, sz, c, jnp.float32)
                )
            pieces[a, b] = full_depth
    feature_grad = (alternate_plane(pieces) + hidden_grad.astype(jnp.float32)).astype(jnp.bfloat16)
    return (feature_grad, mid_out, up_out)


def solution(mesh):
    return jax.shard_map(
        local,
        mesh=mesh,
        in_specs=(P(None, "gx", "gy", None), P("gx", "gy", None), P(), P(), P(), P()),
        out_specs=(P(None, "gx", "gy", None), P(), P()),
        check_vma=False,
    )
```

```python
import functools
import math

import jax
import jax.numpy as jnp
from jax import lax
from jax.experimental import pallas as pl
from jax.experimental.pallas import tpu as pltpu
from jax.sharding import PartitionSpec as P

MESH = pl.DeviceIdType.MESH
ROWS = 7680
PART = ROWS // 3
SIZES = [(640, 320), (160, 80), (48, 32)]
THIRD = 4 * 48
STEP = 80


def my_place():
    gx, gy = lax.axis_index("gx"), lax.axis_index("gy")
    return lax.div(gx, 4), lax.div(gy, 2), lax.rem(gx, 4), lax.rem(gy, 2)


def device_at(x, y, z, core):
    return (x * 4 + z, y * 2 + core)


def moved(place, axis, distance):
    spot = list(place)
    spot[axis] = lax.rem(spot[axis] + distance, 4)
    return device_at(*spot)


def rows_at(start, count):
    return pl.ds(pl.multiple_of(start, 16), count)


def for_rows(count, step, body):
    def one(i, carry):
        body(i * step)
        return carry

    lax.fori_loop(0, count // step, one, 0)


def reduce_kernel(scale, part, out, work, got, half1, half2, half3, slab1, slab2, slab3,
                  sum1, sum2, piece, res, send_sem, recv_sem):
    place = my_place()
    core = place[3]
    other = device_at(place[0], place[1], place[2], 1 - core)
    barrier = pltpu.get_barrier_semaphore()
    pl.semaphore_signal(barrier, inc=1, device_id=other, device_id_type=MESH)
    for axis in range(3):
        for distance in (1, 3):
            pl.semaphore_signal(
                barrier, inc=1, device_id=moved(place, axis, distance), device_id_type=MESH
            )
    pl.semaphore_wait(barrier, 7)

    count = [0]

    def send(src, dst, target):
        index = count[0]
        count[0] += 1
        copy = pltpu.make_async_remote_copy(
            src_ref=src, dst_ref=dst, send_sem=send_sem.at[index], recv_sem=recv_sem.at[index],
            device_id=target, device_id_type=MESH,
        )
        copy.start()
        return copy

    def local_copy(src, dst):
        index = count[0]
        count[0] += 1
        copy = pltpu.make_async_copy(src, dst, send_sem.at[index])
        copy.start()
        return copy

    def lanes(which):
        return pl.ds(pl.multiple_of(which * 128, 128), 128)

    sent = []
    first = []
    for k in range(3):
        rows = pl.ds(k * PART, PART)
        far = send(part.at[rows, lanes(1 - core)], got.at[rows], other)
        near = local_copy(part.at[rows, lanes(core)], work.at[rows])
        first.append((far, near))
        sent.append(far)

    axes = [(0, 1, 2), (1, 2, 0), (2, 0, 1)]
    sizes = SIZES
    halves = (half1, half2, half3)
    slabs = (slab1, slab2, slab3)

    def spots(k, level):
        p = place[axes[k][level]]
        return p, lax.rem(p + 1, 4), lax.rem(p + 2, 4), lax.rem(p + 3, 4)

    def open_level(k, level, src, base):
        size, cut = sizes[level]
        _, up, far, down = spots(k, level)
        after = moved(place, axes[k][level], 1)
        before = moved(place, axes[k][level], 3)
        half, slab = halves[level], slabs[level]
        copies = [
            send(src.at[rows_at(base + far * size, cut)], half.at[k, 0, pl.ds(0, cut)], after),
            send(src.at[rows_at(base + far * size + cut, size - cut)],
                 half.at[k, 1, pl.ds(0, size - cut)], before),
            send(src.at[rows_at(base + up * size + cut, size - cut)],
                 slab.at[k, 0, pl.ds(cut, size - cut)], after),
            send(src.at[rows_at(base + down * size, cut)], slab.at[k, 1, pl.ds(0, cut)], before),
        ]
        sent.extend(copies)
        return copies

    def pass_on(k, level, src, base, copies):
        size, cut = sizes[level]
        _, up, _, down = spots(k, level)
        after = moved(place, axes[k][level], 1)
        before = moved(place, axes[k][level], 3)
        half, slab = halves[level], slabs[level]
        copies[0].wait_recv()
        rows = rows_at(base + up * size, cut)
        add_into(src, base + up * size, half.at[k, 0], cut)
        copies.append(send(src.at[rows], slab.at[k, 0, pl.ds(0, cut)], after))
        copies[1].wait_recv()
        rows = rows_at(base + down * size + cut, size - cut)
        add_into(src, base + down * size + cut, half.at[k, 1], size - cut)
        copies.append(send(src.at[rows], slab.at[k, 1, pl.ds(cut, size - cut)], before))
        sent.extend(copies[4:])

    def add_into(dst, start, src, total):
        step = STEP if total % STEP == 0 else 16

        def body(i, carry):
            rows = rows_at(start + i * step, step)
            dst[rows] = dst[rows] + src[rows_at(i * step, step)]
            return carry

        lax.fori_loop(0, total // step, body, 0)

    def close_level(k, level, src, base, copies, store):
        size, _ = sizes[level]
        step = 48 if level == 2 else STEP
        own = spots(k, level)[0]
        for copy in copies[2:]:
            copy.wait_recv()
        slab = slabs[level]

        def body(start):
            rows = rows_at(start, step)
            total = src[rows_at(base + own * size + start, step)].astype(jnp.float32)
            total = total + slab[k, 0, rows].astype(jnp.float32)
            total = total + slab[k, 1, rows].astype(jnp.float32)
            store(start, total)

        for_rows(size, step, body)

    opened = []
    for k in range(3):
        far, near = first[k]
        near.wait()
        far.wait_recv()

        def add_first(start):
            rows = rows_at(k * PART + start, STEP)
            work[rows] = work[rows] + got[rows]

        for_rows(PART, STEP, add_first)
        opened.append(open_level(k, 0, work, k * PART))
    for k in range(3):
        pass_on(k, 0, work, k * PART, opened[k])
    for k in range(3):
        sum2[pl.ds(k * THIRD + 160, 32)] = jnp.zeros((32, 128), jnp.bfloat16)
    for level, src, dst, src_pitch, dst_pitch in (
        (0, work, sum1, PART, 640), (1, sum1, sum2, 640, THIRD)
    ):
        later = []
        for k in range(3):

            def store(start, total):
                dst[rows_at(k * dst_pitch + start, STEP)] = total.astype(jnp.bfloat16)

            close_level(k, level, src, k * src_pitch, opened[k], store)
            later.append(open_level(k, level + 1, dst, k * dst_pitch))
        for k in range(3):
            pass_on(k, level + 1, dst, k * dst_pitch, later[k])
        opened = later

    def spread_base(k, level):
        if level == 2:
            return piece, k * THIRD
        base = k * PART
        if level == 1:
            base = base + place[axes[k][0]] * sizes[0][0]
        return res, base

    def open_spread(k, level):
        size, _ = sizes[level]
        ref, base = spread_base(k, level)
        rows = rows_at(base + spots(k, level)[0] * size, size)
        copies = [
            send(ref.at[rows], ref.at[rows], moved(place, axes[k][level], 1)),
            send(ref.at[rows], ref.at[rows], moved(place, axes[k][level], 3)),
        ]
        sent.extend(copies)
        return copies

    outs = []

    def hand_out(rows):
        outs.append(local_copy(res.at[rows], out.at[rows, lanes(core)]))
        far = send(res.at[rows], out.at[rows, lanes(core)], other)
        sent.append(far)
        outs.append(far)

    def pass_spread(k, level, copies):
        size, cut = sizes[level]
        ref, base = spread_base(k, level)
        _, up, _, down = spots(k, level)
        copies[0].wait_recv()
        rows = rows_at(base + down * size, cut)
        copies.append(send(ref.at[rows], ref.at[rows], moved(place, axes[k][level], 1)))
        copies[1].wait_recv()
        rows = rows_at(base + up * size + cut, size - cut)
        copies.append(send(ref.at[rows], ref.at[rows], moved(place, axes[k][level], 3)))
        sent.extend(copies[2:])
        if level == 0:
            hand_out(rows_at(base + down * size, size))
            hand_out(rows_at(base + up * size, size))

    spread = []
    for k in range(3):

        def keep(start, total):
            rows = rows_at(k * THIRD + spots(k, 2)[0] * 48 + start, 48)
            piece[rows] = (total * scale).astype(jnp.bfloat16)

        close_level(k, 2, sum2, k * THIRD, opened[k], keep)
        spread.append(open_spread(k, 2))
    for level in (2, 1, 0):
        size, cut = sizes[level]
        for k in range(3):
            pass_spread(k, level, spread[k])
        later = []
        for k in range(3):
            for copy in spread[k][2:]:
                copy.wait_recv()
            if level == 2:
                base = k * PART + place[axes[k][0]] * 640 + place[axes[k][1]] * 160
                res[rows_at(base, 160)] = piece[pl.ds(k * THIRD, 160)]
            if level > 0:
                later.append(open_spread(k, level - 1))
                if level == 1:
                    hand_out(rows_at(k * PART + place[axes[k][0]] * 640, 640))
            else:
                hand_out(rows_at(k * PART + spots(k, 0)[2] * size, size))
        spread = later
    for copy in sent:
        copy.wait_send()
    for index, copy in enumerate(outs):
        if index % 2:
            copy.wait_recv()
        else:
            copy.wait()


def reduce_all(part, scale):
    buf = lambda *shape: pltpu.VMEM(shape, jnp.bfloat16)
    n_copies = 140
    return pl.pallas_call(
        functools.partial(reduce_kernel, scale),
        out_shape=jax.ShapeDtypeStruct((ROWS, 256), jnp.bfloat16),
        in_specs=[pl.BlockSpec(memory_space=pl.ANY)],
        out_specs=pl.BlockSpec(memory_space=pl.ANY),
        scratch_shapes=[
            buf(ROWS, 128), buf(ROWS, 128),
            buf(3, 2, 320, 128), buf(3, 2, 80, 128), buf(3, 2, 32, 128),
            buf(3, 2, 640, 128), buf(3, 2, 160, 128), buf(3, 2, 48, 128),
            buf(3 * 640, 128), buf(3 * THIRD, 128), buf(3 * THIRD, 128),
            buf(ROWS, 128),
            pltpu.SemaphoreType.DMA((n_copies,)),
            pltpu.SemaphoreType.DMA((n_copies,)),
        ],
        compiler_params=pltpu.CompilerParams(
            collective_id=7, has_side_effects=True, vmem_limit_bytes=56 * 2**20
        ),
        cost_estimate=pl.CostEstimate(flops=10**7, bytes_accessed=16 * 10**6, transcendentals=0),
        name="sum_over_devices",
    )(part)


NEAR = [(0, 1), (0, -1), (1, 0), (-1, 0), (1, 1), (1, -1), (-1, 1), (-1, -1)]
NN = (((1,), (0,)), ((), ()))
NT = (((1,), (1,)), ((), ()))
TN = (((0,), (0,)), ((), ()))


def dot(left, right, dims=NN):
    return lax.dot_general(left, right, dims, preferred_element_type=jnp.float32)


def silu(value):
    return value * jax.nn.sigmoid(value)


def silu_slope(value):
    gate = jax.nn.sigmoid(value)
    return gate * (1.0 + value * (1.0 - gate))


def grid_of(rows, cols):
    return (
        lax.broadcasted_iota(jnp.int32, (rows, cols), 0),
        lax.broadcasted_iota(jnp.int32, (rows, cols), 1),
    )


def table(mask):
    return mask.astype(jnp.float32).astype(jnp.bfloat16)


def later_cell(block):
    lane = lax.broadcasted_iota(jnp.int32, block.shape, 1)
    return jnp.where(lane == 127, 0.0, pltpu.roll(block, 127, 1))


def earlier_cell(block):
    lane = lax.broadcasted_iota(jnp.int32, block.shape, 1)
    return jnp.where(lane == 0, 0.0, pltpu.roll(block, 1, 1))


def window_kernel(features, labels, w_down, w_head, w_mid_hbm, w_up_hbm, grad_out, part_out,
                  w_mid, w_up, low, low_moved, down_pre, mid_pre, split, head, head_t,
                  partial, arrived, logit_grad, columns, back, back_moved,
                  load_sem, send_sem, recv_sem):
    gx, gy = lax.axis_index("gx"), lax.axis_index("gy")

    def near(dx, dy):
        return (lax.rem(gx + (dx + 16), 16), lax.rem(gy + (dy + 8), 8))

    loads = [
        pltpu.make_async_copy(w_mid_hbm, w_mid, load_sem.at[0]),
        pltpu.make_async_copy(w_up_hbm, w_up, load_sem.at[1]),
    ]
    for load in loads:
        load.start()
    barrier = pltpu.get_barrier_semaphore()
    for dx, dy in NEAR:
        pl.semaphore_signal(barrier, inc=1, device_id=near(dx, dy), device_id_type=MESH)

    sent = []

    def exchange(stage, src, dst, places):
        copies = []
        for index, (dx, dy) in enumerate(NEAR):
            src_x, dst_x, src_y, dst_y = places(dx, dy)
            copy = pltpu.make_async_remote_copy(
                src_ref=src.at[src_x, src_y], dst_ref=dst.at[dst_x, dst_y],
                send_sem=send_sem.at[8 * stage + index], recv_sem=recv_sem.at[8 * stage + index],
                device_id=near(dx, dy), device_id_type=MESH,
            )
            copy.start()
            copies.append(copy)
        sent.extend(copies)
        return copies

    def finish(copies, buffer):
        for copy in copies:
            copy.wait_recv()
        wide, tall = buffer.shape[0], buffer.shape[1]

        @pl.when(gx == 0)
        def _():
            buffer[0] = jnp.zeros(buffer.shape[1:], buffer.dtype)

        @pl.when(gx == 15)
        def _():
            buffer[wide - 1] = jnp.zeros(buffer.shape[1:], buffer.dtype)

        @pl.when(gy == 0)
        def _():
            for x in range(wide):
                buffer[x, 0] = jnp.zeros(buffer.shape[2:], buffer.dtype)

        @pl.when(gy == 7)
        def _():
            for x in range(wide):
                buffer[x, tall - 1] = jnp.zeros(buffer.shape[2:], buffer.dtype)

    one = lambda i: pl.ds(i, 1)

    def brick_places(dx, dy):
        src_y = {0: pl.ds(1, 2), 1: one(2), -1: one(1)}[dy]
        dst_y = {0: pl.ds(1, 2), 1: one(0), -1: one(3)}[dy]
        return one(1), one(1 - dx), src_y, dst_y

    def upper_places(dx, dy):
        src_x = {0: pl.ds(1, 2), 1: one(2), -1: one(1)}[dx]
        dst_x = {0: pl.ds(1, 2), 1: one(0), -1: one(3)}[dx]
        src_y = {0: pl.ds(1, 4), 1: one(4), -1: one(1)}[dy]
        dst_y = {0: pl.ds(1, 4), 1: one(0), -1: one(5)}[dy]
        return src_x, dst_x, src_y, dst_y

    def spill_places(dx, dy):
        src_x = {0: pl.ds(1, 2), 1: one(3), -1: one(0)}[dx]
        src_y = {0: pl.ds(1, 4), 1: one(5), -1: one(0)}[dy]
        _, dst_x, _, dst_y = upper_places(dx, dy)
        return src_x, dst_x, src_y, dst_y

    lanes = lambda i: pl.ds(i * 128, 128)
    rows, cols = grid_of(256, 256)
    apart = table(rows == jnp.where(cols < 128, 2 * cols, 2 * cols - 255))
    split[...] = dot(features[...], apart).astype(jnp.bfloat16)
    total = jnp.zeros((256, 256), jnp.float32)
    for a in (0, 1):
        for b in (0, 1):
            weight = jnp.concatenate([w_down[4 * a + 2 * b], w_down[4 * a + 2 * b + 1]], axis=1)
            cells = [
                jnp.concatenate(
                    [split[pl.ds((4 * a + 2 * y + b) * 128, 128), lanes(c)] for y in (0, 1)],
                    axis=1,
                )
                for c in (0, 1)
            ]
            total = total + dot(weight, jnp.concatenate(cells, axis=0))
    down_pre[...] = total
    total = silu(total).astype(jnp.bfloat16)
    low[1, 1] = total[:, :128]
    low[1, 2] = total[:, 128:]
    pl.semaphore_wait(barrier, 8)
    copies = exchange(0, low, low, brick_places)

    label_rows = dot(labels[...].astype(jnp.float32).astype(jnp.bfloat16), apart)
    loads[1].wait()
    for tap in range(64):
        mixed = dot(w_head[...], w_up[pl.ds(tap * 128, 128), :])
        head[pl.ds(tap * 8, 8), :] = mixed[:8]
    head_t[...] = jnp.transpose(head[...])
    loads[0].wait()

    finish(copies, low)
    rows, cols = grid_of(128, 256)
    moves = table(rows == jnp.where(cols < 128, cols - 1, cols - 127))
    for x in range(3):
        for y in range(4):
            low_moved[1, x, y] = low[x, y]
            both = dot(low[x, y], moves).astype(jnp.bfloat16)
            low_moved[0, x, y] = both[:, :128]
            low_moved[2, x, y] = both[:, 128:]
    total = jnp.zeros((256, 256), jnp.float32)
    for a in range(3):
        for b in range(3):
            taps = [9 * a + 3 * b + c for c in range(3)]
            weight = jnp.concatenate([w_mid[pl.ds(t * 256, 256), :] for t in taps], axis=1)
            cells = [
                jnp.concatenate([low_moved[c, a, b], low_moved[c, a, b + 1]], axis=1)
                for c in range(3)
            ]
            total = total + dot(weight, jnp.concatenate(cells, axis=0))
    mid_pre[...] = total
    mid = silu(total).astype(jnp.bfloat16)

    head_high = head[...].astype(jnp.bfloat16)
    head_low = (head[...] - head_high.astype(jnp.float32)).astype(jnp.bfloat16)
    spread = dot(head_high, mid) + dot(head_low, mid)
    for x in range(4):
        for y in range(6):
            block = None
            for cell in (0, 1):
                tap = y - 2 * cell
                if 0 <= tap < 4:
                    piece = spread[(4 * x + tap) * 32 : (4 * x + tap + 1) * 32,
                                   cell * 128 : cell * 128 + 128]
                    block = piece if block is None else block + piece
            partial[x, y, :, lanes(0)] = block[8:16] + earlier_cell(block[24:32])
            partial[x, y, :, lanes(1)] = block[16:24] + later_cell(block[0:8])
    copies = exchange(1, partial, arrived, spill_places)
    own_logits = []
    for column in range(8):
        own_logits.append(dot(w_head[...], split[pl.ds(column * 128, 128), :])[:8])
    finish(copies, arrived)
    classes = lax.broadcasted_iota(jnp.int32, (8, 256), 0)
    for a in (0, 1):
        for y in range(4):
            x_at, y_at = 1 + a, 1 + y
            value = own_logits[4 * a + y] + partial[x_at, y_at]
            x_side = 0 if a == 0 else 3
            value = value + arrived[x_side, y_at]
            if y in (0, 3):
                y_side = 0 if y == 0 else 5
                value = value + arrived[x_at, y_side] + arrived[x_side, y_side]
            label = label_rows[4 * a + y : 4 * a + y + 1, :]
            target = (classes.astype(jnp.float32) == label).astype(jnp.float32)
            grad = jax.nn.sigmoid(value) - target
            grad = jnp.where(classes < 4, grad, 0.0)
            logit_grad[x_at, y_at] = grad.astype(jnp.bfloat16).astype(jnp.float32)
    copies = exchange(2, logit_grad, logit_grad, upper_places)
    slope = silu_slope(mid_pre[...])
    head_t_high = head_t[...].astype(jnp.bfloat16)
    head_t_low = (head_t[...] - head_t_high.astype(jnp.float32)).astype(jnp.bfloat16)
    finish(copies, logit_grad)
    for x in range(4):
        for y in range(6):
            even, odd = logit_grad[x, y, :, lanes(0)], logit_grad[x, y, :, lanes(1)]
            block = jnp.concatenate([earlier_cell(odd), even, odd, later_cell(even)], axis=0)
            block = block.astype(jnp.bfloat16)
            for cell in (0, 1):
                tap = y - 2 * cell
                if 0 <= tap < 4:
                    columns[pl.ds((4 * x + tap) * 32, 32), lanes(cell)] = block
    mid_grad = dot(head_t_high, columns[...]) + dot(head_t_low, columns[...])
    mid_pre_grad = (mid_grad * slope).astype(jnp.bfloat16)
    turned = jnp.transpose(mid_pre_grad)
    back[1, 1] = turned[:128]
    back[1, 2] = turned[128:]
    copies = exchange(3, back, back, brick_places)

    for a in range(3):
        for b in range(3):
            for c in range(3):
                cells = jnp.concatenate([low_moved[c, a, b], low_moved[c, a, b + 1]], axis=1)
                part_out[pl.ds((9 * a + 3 * b + c) * 256, 256), :] = dot(
                    mid_pre_grad, cells, NT
                ).astype(jnp.bfloat16)
    part_out[pl.ds(27 * 256, 512), :] = dot(columns[...], mid, NT).astype(jnp.bfloat16)
    part_out[pl.ds(27 * 256 + 512, 256), :] = jnp.zeros((256, 256), jnp.bfloat16)

    finish(copies, back)
    rows, cols = grid_of(256, 128)
    moves = table(cols == jnp.where(rows < 128, rows + 1, rows - 129))
    for x in range(3):
        for y in range(4):
            back_moved[x, y, :, pl.ds(256, 256)] = back[x, y]
            both = dot(moves, back[x, y]).astype(jnp.bfloat16)
            back_moved[x, y, :, pl.ds(0, 256)] = both[:128]
            back_moved[x, y, :, pl.ds(512, 256)] = both[128:]
    total = jnp.zeros((256, 256), jnp.float32)
    for a in range(3):
        for b in range(3):
            cells = jnp.concatenate(
                [back_moved[2 - a, 2 - b], back_moved[2 - a, 3 - b]], axis=0
            )
            total = total + dot(cells, w_mid[pl.ds((3 * a + b) * 768, 768), :])
    down_grad = (jnp.transpose(total) * silu_slope(down_pre[...])).astype(jnp.bfloat16)
    for a in (0, 1):
        for b in (0, 1):
            weight = jnp.concatenate([w_down[4 * a + 2 * b], w_down[4 * a + 2 * b + 1]], axis=1)
            pieces = dot(weight, down_grad, TN)
            for cell in (0, 1):
                y = 2 * cell + b
                grad = jnp.concatenate(
                    [logit_grad[1 + a, 1 + y], jnp.zeros((8, 256), jnp.float32)], axis=0
                ).astype(jnp.bfloat16)
                hidden = dot(w_head[...], grad, TN).astype(jnp.bfloat16).astype(jnp.float32)
                at = slice(cell * 128, cell * 128 + 128)
                whole = jnp.concatenate([pieces[:128, at], pieces[128:, at]], axis=1) + hidden
                grad_out[pl.ds((4 * a + y) * 128, 128), :] = dot(
                    whole.astype(jnp.bfloat16), apart, NT
                ).astype(jnp.bfloat16)
    for copy in sent:
        copy.wait_send()


def window(features, labels, w_down, w_mid, w_up, w_head):
    half = lambda *shape: pltpu.VMEM(shape, jnp.bfloat16)
    full = lambda *shape: pltpu.VMEM(shape, jnp.float32)
    vmem, hbm = pl.BlockSpec(memory_space=pltpu.VMEM), pl.BlockSpec(memory_space=pl.ANY)
    return pl.pallas_call(
        window_kernel,
        out_shape=[
            jax.ShapeDtypeStruct((1024, 256), jnp.bfloat16),
            jax.ShapeDtypeStruct((ROWS, 256), jnp.bfloat16),
        ],
        in_specs=[vmem, vmem, vmem, vmem, hbm, hbm],
        out_specs=[vmem, vmem],
        scratch_shapes=[
            half(27 * 256, 256), half(64 * 128, 256),
            half(3, 4, 256, 128), half(3, 3, 4, 256, 128),
            full(256, 256), full(256, 256),
            half(1024, 256), full(512, 256), full(256, 512),
            full(4, 6, 8, 256), full(4, 6, 8, 256), full(4, 6, 8, 256),
            half(512, 256), half(3, 4, 128, 256), half(3, 4, 128, 768),
            pltpu.SemaphoreType.DMA((2,)),
            pltpu.SemaphoreType.DMA((32,)),
            pltpu.SemaphoreType.DMA((32,)),
        ],
        compiler_params=pltpu.CompilerParams(
            collective_id=8, has_side_effects=True, vmem_limit_bytes=56 * 2**20
        ),
        cost_estimate=pl.CostEstimate(flops=4 * 10**9, bytes_accessed=2 * 10**7, transcendentals=0),
        name="window",
    )(features, labels, w_down, w_head, w_mid, w_up)


def local(features, labels, w_down, w_mid, w_up, w_head):
    chans_up = features.shape[0]
    chans_mid = w_mid.shape[3]
    flat = features.transpose(1, 2, 0, 3).reshape(8 * chans_up, 256)
    head = jnp.concatenate([w_head, jnp.zeros((12, chans_up), w_head.dtype)])
    grad, part = window(
        flat, labels.reshape(8, 256), w_down.reshape(8, chans_mid, chans_up),
        w_mid.reshape(27 * chans_mid, chans_mid), w_up.reshape(64 * chans_up, chans_mid), head,
    )
    total = reduce_all(part, 1.0 / math.sqrt(32768))
    feature_grad = grad.reshape(2, 4, chans_up, 256).transpose(2, 0, 1, 3)
    mid_out = total[: 27 * chans_mid].reshape(3, 3, 3, chans_mid, chans_mid)
    mixed = total[27 * chans_mid : 27 * chans_mid + 512].reshape(64, 8, chans_mid)[:, :4]
    up_out = jnp.einsum("kj,tkm->tjm", w_head, mixed, preferred_element_type=jnp.float32)
    up_out = up_out.astype(jnp.bfloat16).reshape(4, 4, 4, chans_up, chans_mid)
    return feature_grad, mid_out, up_out


def solution(mesh):
    return jax.shard_map(
        local,
        mesh=mesh,
        in_specs=(P(None, "gx", "gy", None), P("gx", "gy", None), P(), P(), P(), P()),
        out_specs=(P(None, "gx", "gy", None), P(), P()),
        check_vma=False,
    )
```

```python
import functools
import math

import jax
import jax.numpy as jnp
from jax import lax
from jax.experimental import pallas as pl
from jax.experimental.pallas import tpu as pltpu
from jax.sharding import PartitionSpec as P

MESH = pl.DeviceIdType.MESH
ROWS = 7680
PART = ROWS // 3
SIZES = [(640, 320), (160, 80), (48, 32)]
THIRD = 4 * 48
STEP = 80


def my_place():
    gx, gy = lax.axis_index("gx"), lax.axis_index("gy")
    return lax.div(gx, 4), lax.div(gy, 2), lax.rem(gx, 4), lax.rem(gy, 2)


def device_at(x, y, z, core):
    return (x * 4 + z, y * 2 + core)


def moved(place, axis, distance):
    spot = list(place)
    spot[axis] = lax.rem(spot[axis] + distance, 4)
    return device_at(*spot)


def rows_at(start, count):
    return pl.ds(pl.multiple_of(start, 16), count)


def for_rows(count, step, body):
    def one(i, carry):
        body(i * step)
        return carry

    lax.fori_loop(0, count // step, one, 0)


class Summing:
    axes = [(0, 1, 2), (1, 2, 0), (2, 0, 1)]

    def __init__(self, part, out, got, work, half, slabs, sums, piece, res, send_sem, recv_sem):
        self.part, self.out, self.got, self.work, self.half = part, out, got, work, half
        self.slabs, self.sums, self.piece, self.res = slabs, sums, piece, res
        self.send_sem, self.recv_sem = send_sem, recv_sem
        self.place = my_place()
        self.core = self.place[3]
        self.other = device_at(*self.place[:3], 1 - self.core)
        self.count, self.sent, self.outs = 0, [], []
        self.first, self.opened, self.spread = {}, {}, {}

    def peers(self):
        places = [moved(self.place, axis, d) for axis in range(3) for d in (1, 2, 3)]
        return [self.other] + places

    def send(self, src, dst, target):
        copy = pltpu.make_async_remote_copy(
            src_ref=src, dst_ref=dst, send_sem=self.send_sem.at[self.count],
            recv_sem=self.recv_sem.at[self.count], device_id=target, device_id_type=MESH,
        )
        self.count += 1
        copy.start()
        self.sent.append(copy)
        return copy

    def spots(self, k, level):
        p = self.place[self.axes[k][level]]
        return p, lax.rem(p + 1, 4), lax.rem(p + 2, 4), lax.rem(p + 3, 4)

    def peer(self, k, level, distance):
        return moved(self.place, self.axes[k][level], distance)

    def send_other(self, k):
        rows = pl.ds(k * PART, PART)
        src = self.part.at[1 - self.core, rows]
        self.first[k] = self.send(src, self.got.at[rows], self.other)

    def add_other(self, k):
        self.first[k].wait_recv()

        def body(start):
            rows = rows_at(k * PART + start, STEP)
            self.work[rows] = self.part[self.core, rows] + self.got[rows]

        for_rows(PART, STEP, body)

    def open_ring(self, k):
        size, cut = SIZES[0]
        _, up, far, down = self.spots(k, 0)
        after, before = self.peer(k, 0, 1), self.peer(k, 0, 3)
        base = k * PART
        src, slab = self.work, self.slabs[0]
        self.opened[k, 0] = [
            self.send(src.at[rows_at(base + far * size, cut)], self.half.at[k, 0], after),
            self.send(src.at[rows_at(base + far * size + cut, cut)], self.half.at[k, 1], before),
            self.send(src.at[rows_at(base + up * size + cut, cut)],
                      slab.at[k, 0, pl.ds(cut, cut)], after),
            self.send(src.at[rows_at(base + down * size, cut)], slab.at[k, 1, pl.ds(0, cut)],
                      before),
        ]

    def pass_ring(self, k):
        size, cut = SIZES[0]
        _, up, _, down = self.spots(k, 0)
        base = k * PART
        slab, copies = self.slabs[0], self.opened[k, 0]
        for side, start, target, at in (
            (0, base + up * size, self.peer(k, 0, 1), 0),
            (1, base + down * size + cut, self.peer(k, 0, 3), cut),
        ):
            copies[side].wait_recv()

            def body(offset):
                rows = rows_at(start + offset, STEP)
                passed = self.half[k, side, rows_at(offset, STEP)]
                self.work[rows] = self.work[rows] + passed

            for_rows(cut, STEP, body)
            copies.append(
                self.send(self.work.at[rows_at(start, cut)], slab.at[k, side, pl.ds(at, cut)],
                          target)
            )

    def open_level(self, k, level):
        size = SIZES[level][0]
        src, base = self.sums[level - 1], k * 4 * size
        spots = self.spots(k, level)
        self.opened[k, level] = [
            self.send(src.at[rows_at(base + spots[d] * size, size)],
                      self.slabs[level].at[k, d - 1], self.peer(k, level, d))
            for d in (1, 2, 3)
        ]

    def close_level(self, k, level, store):
        size = SIZES[level][0]
        step = 48 if level == 2 else STEP
        copies = self.opened[k, level]
        for copy in copies[2:] if level == 0 else copies:
            copy.wait_recv()
        src, base = (self.work, k * PART) if level == 0 else (self.sums[level - 1], k * 4 * size)
        base = base + self.spots(k, level)[0] * size
        slab = self.slabs[level]

        def body(start):
            total = src[rows_at(base + start, step)].astype(jnp.float32)
            for side in range(slab.shape[1]):
                total = total + slab[k, side, rows_at(start, step)].astype(jnp.float32)
            store(start, total)

        for_rows(size, step, body)

    def store_sum(self, k, level):
        pitch = PART // 4 if level == 0 else THIRD

        def store(start, total):
            self.sums[level][rows_at(k * pitch + start, STEP)] = total.astype(jnp.bfloat16)

        self.close_level(k, level, store)
        if level == 1:
            self.sums[1][pl.ds(k * THIRD + 160, 32)] = jnp.zeros((32, 128), jnp.bfloat16)

    def store_last(self, k, scale):
        def store(start, total):
            rows = rows_at(k * THIRD + self.spots(k, 2)[0] * 48 + start, 48)
            self.piece[rows] = (total * scale).astype(jnp.bfloat16)

        self.close_level(k, 2, store)

    def spread_rows(self, k, level):
        if level == 2:
            return self.piece, k * THIRD
        base = k * PART
        if level == 1:
            base = base + self.spots(k, 0)[0] * SIZES[0][0]
        return self.res, base

    def open_spread(self, k, level):
        size = SIZES[level][0]
        ref, base = self.spread_rows(k, level)
        rows = rows_at(base + self.spots(k, level)[0] * size, size)
        self.spread[k, level] = [
            self.send(ref.at[rows], ref.at[rows], self.peer(k, level, d))
            for d in ((1, 3) if level == 0 else (1, 2, 3))
        ]

    def close_spread(self, k, level):
        for copy in self.spread[k, level]:
            copy.wait_recv()
        if level == 2:
            base = k * PART + self.spots(k, 0)[0] * 640 + self.spots(k, 1)[0] * 160
            self.res[rows_at(base, 160)] = self.piece[pl.ds(k * THIRD, 160)]

    def hand_out(self, start, count):
        rows = rows_at(start, count)
        lanes = pl.ds(pl.multiple_of(self.core * 128, 128), 128)
        near = pltpu.make_async_copy(
            self.res.at[rows], self.out.at[rows, lanes], self.send_sem.at[self.count]
        )
        self.count += 1
        near.start()
        self.outs.append((near, self.send(self.res.at[rows], self.out.at[rows, lanes], self.other)))

    def hand_own(self, k):
        self.hand_out(k * PART + self.spots(k, 0)[0] * 640, 640)

    def pass_spread(self, k):
        size, cut = SIZES[0]
        base = k * PART
        _, up, far, down = self.spots(k, 0)
        copies = self.spread[k, 0]
        copies[0].wait_recv()
        rows = rows_at(base + down * size, cut)
        copies.append(self.send(self.res.at[rows], self.res.at[rows], self.peer(k, 0, 1)))
        copies[1].wait_recv()
        rows = rows_at(base + up * size + cut, cut)
        copies.append(self.send(self.res.at[rows], self.res.at[rows], self.peer(k, 0, 3)))

    def hand_sides(self, k):
        _, up, _, down = self.spots(k, 0)
        self.hand_out(k * PART + down * 640, 640)
        self.hand_out(k * PART + up * 640, 640)

    def hand_far(self, k):
        for copy in self.spread[k, 0][2:]:
            copy.wait_recv()
        self.hand_out(k * PART + self.spots(k, 0)[2] * 640, 640)

    def end(self):
        for copy in self.sent:
            copy.wait_send()
        for near, far in self.outs:
            near.wait()
            far.wait_recv()


NEAR = [(0, 1), (0, -1), (1, 0), (-1, 0), (1, 1), (1, -1), (-1, 1), (-1, -1)]
NN = (((1,), (0,)), ((), ()))
NT = (((1,), (1,)), ((), ()))
TN = (((0,), (0,)), ((), ()))


def dot(left, right, dims=NN):
    return lax.dot_general(left, right, dims, preferred_element_type=jnp.float32)


def silu(value):
    return value * jax.nn.sigmoid(value)


def silu_slope(value):
    gate = jax.nn.sigmoid(value)
    return gate * (1.0 + value * (1.0 - gate))


def grid_of(rows, cols):
    return (
        lax.broadcasted_iota(jnp.int32, (rows, cols), 0),
        lax.broadcasted_iota(jnp.int32, (rows, cols), 1),
    )


def table(mask):
    return mask.astype(jnp.float32).astype(jnp.bfloat16)


def later_cell(block):
    lane = lax.broadcasted_iota(jnp.int32, block.shape, 1)
    return jnp.where(lane == 127, 0.0, pltpu.roll(block, 127, 1))


def earlier_cell(block):
    lane = lax.broadcasted_iota(jnp.int32, block.shape, 1)
    return jnp.where(lane == 0, 0.0, pltpu.roll(block, 1, 1))


def window_kernel(scale, features, labels, w_down, head_rows, w_mid_hbm, w_up_hbm, grad_out, sum_out,
                  w_head, label_cells, w_mid, w_up, low, low_moved, down_pre, mid_pre, split, head, head_t,
                  partial, arrived, logit_grad, columns, back, back_moved,
                  part, got, work, half, slab0, slab1, slab2, sum0, sum1, piece, res,
                  load_sem, send_sem, recv_sem, sum_send, sum_recv):
    gx, gy = lax.axis_index("gx"), lax.axis_index("gy")

    def near(dx, dy):
        return (lax.rem(gx + (dx + 16), 16), lax.rem(gy + (dy + 8), 8))

    loads = [
        pltpu.make_async_copy(w_mid_hbm, w_mid, load_sem.at[0]),
        pltpu.make_async_copy(w_up_hbm, w_up, load_sem.at[1]),
    ]
    for load in loads:
        load.start()
    barrier = pltpu.get_barrier_semaphore()
    summing = Summing(
        part, sum_out, got, work, half, (slab0, slab1, slab2), (sum0, sum1), piece, res,
        sum_send, sum_recv,
    )
    peers = [near(dx, dy) for dx, dy in NEAR] + summing.peers()
    for peer in peers:
        pl.semaphore_signal(barrier, inc=1, device_id=peer, device_id_type=MESH)
    w_head[...] = jnp.zeros((16, 128), jnp.float32)
    w_head[pl.ds(0, 4), :] = head_rows[...].astype(jnp.float32)
    heads = w_head[...].astype(jnp.bfloat16)
    for a in (0, 1):
        label_cells[pl.ds(4 * a, 4), :] = labels[a].astype(jnp.float32)

    sent = []

    def exchange(stage, src, dst, places):
        copies = []
        for index, (dx, dy) in enumerate(NEAR):
            src_x, dst_x, src_y, dst_y = places(dx, dy)
            copy = pltpu.make_async_remote_copy(
                src_ref=src.at[src_x, src_y], dst_ref=dst.at[dst_x, dst_y],
                send_sem=send_sem.at[8 * stage + index], recv_sem=recv_sem.at[8 * stage + index],
                device_id=near(dx, dy), device_id_type=MESH,
            )
            copy.start()
            copies.append(copy)
        sent.extend(copies)
        return copies

    def finish(copies, buffer):
        for copy in copies:
            copy.wait_recv()
        wide, tall = buffer.shape[0], buffer.shape[1]

        @pl.when(gx == 0)
        def _():
            buffer[0] = jnp.zeros(buffer.shape[1:], buffer.dtype)

        @pl.when(gx == 15)
        def _():
            buffer[wide - 1] = jnp.zeros(buffer.shape[1:], buffer.dtype)

        @pl.when(gy == 0)
        def _():
            for x in range(wide):
                buffer[x, 0] = jnp.zeros(buffer.shape[2:], buffer.dtype)

        @pl.when(gy == 7)
        def _():
            for x in range(wide):
                buffer[x, tall - 1] = jnp.zeros(buffer.shape[2:], buffer.dtype)

    one = lambda i: pl.ds(i, 1)

    def brick_places(dx, dy):
        src_y = {0: pl.ds(1, 2), 1: one(2), -1: one(1)}[dy]
        dst_y = {0: pl.ds(1, 2), 1: one(0), -1: one(3)}[dy]
        return one(1), one(1 - dx), src_y, dst_y

    def upper_places(dx, dy):
        src_x = {0: pl.ds(1, 2), 1: one(2), -1: one(1)}[dx]
        dst_x = {0: pl.ds(1, 2), 1: one(0), -1: one(3)}[dx]
        src_y = {0: pl.ds(1, 4), 1: one(4), -1: one(1)}[dy]
        dst_y = {0: pl.ds(1, 4), 1: one(0), -1: one(5)}[dy]
        return src_x, dst_x, src_y, dst_y

    def spill_places(dx, dy):
        src_x = {0: pl.ds(1, 2), 1: one(3), -1: one(0)}[dx]
        src_y = {0: pl.ds(1, 4), 1: one(5), -1: one(0)}[dy]
        _, dst_x, _, dst_y = upper_places(dx, dy)
        return src_x, dst_x, src_y, dst_y

    lanes = lambda i: pl.ds(i * 128, 128)
    rows, cols = grid_of(256, 256)
    apart = table(rows == jnp.where(cols < 128, 2 * cols, 2 * cols - 255))
    split[...] = dot(features[...], apart).astype(jnp.bfloat16)
    total = jnp.zeros((256, 256), jnp.float32)
    for a in (0, 1):
        for b in (0, 1):
            weight = jnp.concatenate([w_down[4 * a + 2 * b], w_down[4 * a + 2 * b + 1]], axis=1)
            cells = [
                jnp.concatenate(
                    [split[pl.ds((4 * a + 2 * y + b) * 128, 128), lanes(c)] for y in (0, 1)],
                    axis=1,
                )
                for c in (0, 1)
            ]
            total = total + dot(weight, jnp.concatenate(cells, axis=0))
    down_pre[...] = total
    total = silu(total).astype(jnp.bfloat16)
    low[1, 1] = total[:, :128]
    low[1, 2] = total[:, 128:]
    pl.semaphore_wait(barrier, len(peers))
    copies = exchange(0, low, low, brick_places)

    label_rows = dot(label_cells[...].astype(jnp.bfloat16), apart)
    loads[1].wait()
    for tap in range(64):
        mixed = dot(heads, w_up[pl.ds(tap * 128, 128), :])
        head[pl.ds(tap * 8, 8), :] = mixed[:8]
    head_t[...] = jnp.transpose(head[...])
    loads[0].wait()

    finish(copies, low)
    rows, cols = grid_of(128, 256)
    moves = table(rows == jnp.where(cols < 128, cols - 1, cols - 127))
    for x in range(3):
        for y in range(4):
            low_moved[1, x, y] = low[x, y]
            both = dot(low[x, y], moves).astype(jnp.bfloat16)
            low_moved[0, x, y] = both[:, :128]
            low_moved[2, x, y] = both[:, 128:]
    total = jnp.zeros((256, 256), jnp.float32)
    for a in range(3):
        for b in range(3):
            taps = [9 * a + 3 * b + c for c in range(3)]
            weight = jnp.concatenate([w_mid[pl.ds(t * 256, 256), :] for t in taps], axis=1)
            cells = [
                jnp.concatenate([low_moved[c, a, b], low_moved[c, a, b + 1]], axis=1)
                for c in range(3)
            ]
            total = total + dot(weight, jnp.concatenate(cells, axis=0))
    mid_pre[...] = total
    mid = silu(total).astype(jnp.bfloat16)

    head_high = head[...].astype(jnp.bfloat16)
    head_low = (head[...] - head_high.astype(jnp.float32)).astype(jnp.bfloat16)
    spread = dot(head_high, mid) + dot(head_low, mid)
    for x in range(4):
        for y in range(6):
            block = None
            for cell in (0, 1):
                tap = y - 2 * cell
                if 0 <= tap < 4:
                    piece = spread[(4 * x + tap) * 32 : (4 * x + tap + 1) * 32,
                                   cell * 128 : cell * 128 + 128]
                    block = piece if block is None else block + piece
            partial[x, y, :, lanes(0)] = block[8:16] + earlier_cell(block[24:32])
            partial[x, y, :, lanes(1)] = block[16:24] + later_cell(block[0:8])
    copies = exchange(1, partial, arrived, spill_places)
    own_logits = []
    for column in range(8):
        own_logits.append(dot(heads, split[pl.ds(column * 128, 128), :])[:8])
    finish(copies, arrived)
    classes = lax.broadcasted_iota(jnp.int32, (8, 256), 0)
    for a in (0, 1):
        for y in range(4):
            x_at, y_at = 1 + a, 1 + y
            value = own_logits[4 * a + y] + partial[x_at, y_at]
            x_side = 0 if a == 0 else 3
            value = value + arrived[x_side, y_at]
            if y in (0, 3):
                y_side = 0 if y == 0 else 5
                value = value + arrived[x_at, y_side] + arrived[x_side, y_side]
            label = label_rows[4 * a + y : 4 * a + y + 1, :]
            target = (classes.astype(jnp.float32) == label).astype(jnp.float32)
            grad = jax.nn.sigmoid(value) - target
            grad = jnp.where(classes < 4, grad, 0.0)
            logit_grad[x_at, y_at] = grad.astype(jnp.bfloat16).astype(jnp.float32)
    copies = exchange(2, logit_grad, logit_grad, upper_places)
    slope = silu_slope(mid_pre[...])
    head_t_high = head_t[...].astype(jnp.bfloat16)
    head_t_low = (head_t[...] - head_t_high.astype(jnp.float32)).astype(jnp.bfloat16)
    finish(copies, logit_grad)
    for x in range(4):
        for y in range(6):
            even, odd = logit_grad[x, y, :, lanes(0)], logit_grad[x, y, :, lanes(1)]
            block = jnp.concatenate([earlier_cell(odd), even, odd, later_cell(even)], axis=0)
            block = block.astype(jnp.bfloat16)
            for cell in (0, 1):
                tap = y - 2 * cell
                if 0 <= tap < 4:
                    columns[pl.ds((4 * x + tap) * 32, 32), lanes(cell)] = block
    mid_grad = dot(head_t_high, columns[...]) + dot(head_t_low, columns[...])
    mid_pre_grad = (mid_grad * slope).astype(jnp.bfloat16)
    turned = jnp.transpose(mid_pre_grad)
    back[1, 1] = turned[:128]
    back[1, 2] = turned[128:]
    copies = exchange(3, back, back, brick_places)

    def keep(start, value):
        value = value.astype(jnp.bfloat16)
        rows = pl.ds(start, value.shape[0])
        part[0, rows] = value[:, :128]
        part[1, rows] = value[:, 128:]

    thirds = range(3)
    for tap in range(27):
        a, b, c = tap // 9, tap // 3 % 3, tap % 3
        cells = jnp.concatenate([low_moved[c, a, b], low_moved[c, a, b + 1]], axis=1)
        keep(tap * 256, dot(mid_pre_grad, cells, NT))
        if tap in (9, 19):
            summing.send_other(tap // 10)
    keep(27 * 256, dot(columns[...], mid, NT))
    keep(27 * 256 + 512, jnp.zeros((256, 256), jnp.float32))
    summing.send_other(2)
    for k in thirds:
        summing.add_other(k)
        summing.open_ring(k)
    for k in thirds:
        summing.pass_ring(k)

    finish(copies, back)
    rows, cols = grid_of(256, 128)
    moves = table(cols == jnp.where(rows < 128, rows + 1, rows - 129))
    for x in range(3):
        for y in range(4):
            back_moved[x, y, :, pl.ds(256, 256)] = back[x, y]
            both = dot(moves, back[x, y]).astype(jnp.bfloat16)
            back_moved[x, y, :, pl.ds(0, 256)] = both[:128]
            back_moved[x, y, :, pl.ds(512, 256)] = both[128:]
    for k in thirds:
        summing.store_sum(k, 0)
        summing.open_level(k, 1)

    total = jnp.zeros((256, 256), jnp.float32)
    for a in range(3):
        for b in range(3):
            cells = jnp.concatenate(
                [back_moved[2 - a, 2 - b], back_moved[2 - a, 3 - b]], axis=0
            )
            total = total + dot(cells, w_mid[pl.ds((3 * a + b) * 768, 768), :])
    down_grad = (jnp.transpose(total) * silu_slope(down_pre[...])).astype(jnp.bfloat16)
    for k in thirds:
        summing.store_sum(k, 1)
        summing.open_level(k, 2)

    def finish_features(a):
        for b in (0, 1):
            weight = jnp.concatenate([w_down[4 * a + 2 * b], w_down[4 * a + 2 * b + 1]], axis=1)
            pieces = dot(weight, down_grad, TN)
            for cell in (0, 1):
                y = 2 * cell + b
                grad = jnp.concatenate(
                    [logit_grad[1 + a, 1 + y], jnp.zeros((8, 256), jnp.float32)], axis=0
                ).astype(jnp.bfloat16)
                hidden = dot(heads, grad, TN).astype(jnp.bfloat16).astype(jnp.float32)
                at = slice(cell * 128, cell * 128 + 128)
                whole = jnp.concatenate([pieces[:128, at], pieces[128:, at]], axis=1) + hidden
                grad_out[pl.ds((4 * a + y) * 128, 128), :] = dot(
                    whole.astype(jnp.bfloat16), apart, NT
                ).astype(jnp.bfloat16)

    finish_features(0)
    for k in thirds:
        summing.store_last(k, scale)
        summing.open_spread(k, 2)
    finish_features(1)
    for k in thirds:
        summing.close_spread(k, 2)
        summing.open_spread(k, 1)
    for k in thirds:
        summing.close_spread(k, 1)
        summing.open_spread(k, 0)
    for k in thirds:
        summing.hand_own(k)
    for k in thirds:
        summing.pass_spread(k)
    for k in thirds:
        summing.hand_sides(k)
    for k in thirds:
        summing.hand_far(k)
    for copy in sent:
        copy.wait_send()
    summing.end()


def expand_kernel(sums, head_rows, mid_out, up_out, w_head, mixed, up, load_sem, mid_sem, up_sem):
    mid_copy = pltpu.make_async_copy(sums.at[pl.ds(0, 6912)], mid_out, mid_sem)
    load = pltpu.make_async_copy(sums.at[pl.ds(6912, 512)], mixed, load_sem)
    load.start()
    mid_copy.start()
    w_head[...] = jnp.zeros((16, 256), jnp.float32)
    w_head[pl.ds(0, 4), pl.ds(0, 128)] = head_rows[...].astype(jnp.float32)
    w_head[pl.ds(8, 4), pl.ds(128, 128)] = head_rows[...].astype(jnp.float32)
    heads = jnp.transpose(w_head[...]).astype(jnp.bfloat16)
    load.wait()
    stores = []
    for pair in range(32):
        pairs = dot(heads, mixed[pl.ds(pair * 16, 16), :])
        up[pl.ds(pair * 256, 256), :] = pairs.astype(jnp.bfloat16)
        if pair % 8 == 7:
            rows = pl.ds((pair - 7) * 256, 2048)
            store = pltpu.make_async_copy(up.at[rows], up_out.at[rows], up_sem.at[pair // 8])
            store.start()
            stores.append(store)
    for store in stores:
        store.wait()
    mid_copy.wait()


def expand(sums, w_head):
    vmem, hbm = pl.BlockSpec(memory_space=pltpu.VMEM), pl.BlockSpec(memory_space=pl.ANY)
    return pl.pallas_call(
        expand_kernel,
        out_shape=[
            jax.ShapeDtypeStruct((6912, 256), jnp.bfloat16),
            jax.ShapeDtypeStruct((8192, 256), jnp.bfloat16),
        ],
        in_specs=[hbm, vmem],
        out_specs=[hbm, hbm],
        scratch_shapes=[
            pltpu.VMEM((16, 256), jnp.float32),
            pltpu.VMEM((512, 256), jnp.bfloat16),
            pltpu.VMEM((8192, 256), jnp.bfloat16),
            pltpu.SemaphoreType.DMA(()),
            pltpu.SemaphoreType.DMA(()),
            pltpu.SemaphoreType.DMA((4,)),
        ],
        compiler_params=pltpu.CompilerParams(vmem_limit_bytes=32 * 2**20),
        cost_estimate=pl.CostEstimate(flops=10**8, bytes_accessed=12 * 10**6, transcendentals=0),
        name="expand",
    )(sums, w_head)


def window(features, labels, w_down, w_mid, w_up, w_head):
    half = lambda *shape: pltpu.VMEM(shape, jnp.bfloat16)
    full = lambda *shape: pltpu.VMEM(shape, jnp.float32)
    vmem, hbm = pl.BlockSpec(memory_space=pltpu.VMEM), pl.BlockSpec(memory_space=pl.ANY)
    return pl.pallas_call(
        functools.partial(window_kernel, 1.0 / math.sqrt(32768)),
        out_shape=[
            jax.ShapeDtypeStruct((1024, 256), jnp.bfloat16),
            jax.ShapeDtypeStruct((ROWS, 256), jnp.bfloat16),
        ],
        in_specs=[vmem, vmem, vmem, vmem, hbm, hbm],
        out_specs=[vmem, hbm],
        scratch_shapes=[
            full(16, 128), full(8, 256),
            half(27 * 256, 256), half(64 * 128, 256),
            half(3, 4, 256, 128), half(3, 3, 4, 256, 128),
            full(256, 256), full(256, 256),
            half(1024, 256), full(512, 256), full(256, 512),
            full(4, 6, 8, 256), full(4, 6, 8, 256), full(4, 6, 8, 256),
            half(512, 256), half(3, 4, 128, 256), half(3, 4, 128, 768),
            half(2, ROWS, 128), half(ROWS, 128), half(ROWS, 128),
            half(3, 2, 320, 128),
            half(3, 2, 640, 128), half(3, 3, 160, 128), half(3, 3, 48, 128),
            half(3 * 640, 128), half(3 * THIRD, 128), half(3 * THIRD, 128),
            half(ROWS, 128),
            pltpu.SemaphoreType.DMA((2,)),
            pltpu.SemaphoreType.DMA((32,)),
            pltpu.SemaphoreType.DMA((32,)),
            pltpu.SemaphoreType.DMA((100,)),
            pltpu.SemaphoreType.DMA((100,)),
        ],
        compiler_params=pltpu.CompilerParams(
            collective_id=8, has_side_effects=True, vmem_limit_bytes=56 * 2**20
        ),
        cost_estimate=pl.CostEstimate(flops=4 * 10**9, bytes_accessed=2 * 10**7, transcendentals=0),
        name="window",
    )(features, labels, w_down, w_head, w_mid, w_up)


def local(features, labels, w_down, w_mid, w_up, w_head):
    chans_up = features.shape[0]
    chans_mid = w_mid.shape[3]
    flat = features.transpose(1, 2, 0, 3).reshape(8 * chans_up, 256)
    grad, sums = window(
        flat, labels, w_down.reshape(8, chans_mid, chans_up),
        w_mid.reshape(27 * chans_mid, chans_mid), w_up.reshape(64 * chans_up, chans_mid), w_head,
    )
    feature_grad = grad.reshape(2, 4, chans_up, 256).transpose(2, 0, 1, 3)
    mid_out, up_out = expand(sums, w_head)
    return (
        feature_grad,
        mid_out.reshape(3, 3, 3, chans_mid, chans_mid),
        up_out.reshape(4, 4, 4, chans_up, chans_mid),
    )


def solution(mesh):
    return jax.shard_map(
        local,
        mesh=mesh,
        in_specs=(P(None, "gx", "gy", None), P("gx", "gy", None), P(), P(), P(), P()),
        out_specs=(P(None, "gx", "gy", None), P(), P()),
        check_vma=False,
    )
```

```python
import functools
import math

import jax
import jax.numpy as jnp
from jax import lax
from jax.experimental import pallas as pl
from jax.experimental.pallas import tpu as pltpu
from jax.sharding import PartitionSpec as P

MESH = pl.DeviceIdType.MESH
ROWS = 7680
PART = ROWS // 3
SIZES = [(640, 320), (160, 80), (48, 32)]
THIRD = 4 * 48
STEP = 320


def my_place():
    gx, gy = lax.axis_index("gx"), lax.axis_index("gy")
    return lax.div(gx, 4), lax.div(gy, 2), lax.rem(gx, 4), lax.rem(gy, 2)


def device_at(x, y, z, core):
    return (x * 4 + z, y * 2 + core)


def moved(place, axis, distance):
    spot = list(place)
    spot[axis] = lax.rem(spot[axis] + distance, 4)
    return device_at(*spot)


def rows_at(start, count):
    return pl.ds(pl.multiple_of(start, 16), count)


def for_rows(count, step, body):
    def one(i, carry):
        body(i * step)
        return carry

    lax.fori_loop(0, count // step, one, 0)


class Summing:
    axes = [(0, 1, 2), (1, 2, 0), (2, 0, 1)]

    def __init__(self, part, out, got, work, half, slabs, sums, piece, res, send_sem, recv_sem):
        self.part, self.out, self.got, self.work, self.half = part, out, got, work, half
        self.slabs, self.sums, self.piece, self.res = slabs, sums, piece, res
        self.send_sem, self.recv_sem = send_sem, recv_sem
        self.place = my_place()
        self.core = self.place[3]
        self.other = device_at(*self.place[:3], 1 - self.core)
        self.count, self.sent, self.outs = 0, [], []
        self.first, self.opened, self.spread = {}, {}, {}

    def peers(self):
        places = [moved(self.place, axis, d) for axis in range(3) for d in (1, 2, 3)]
        return [self.other] + places

    def send(self, src, dst, target):
        copy = pltpu.make_async_remote_copy(
            src_ref=src, dst_ref=dst, send_sem=self.send_sem.at[self.count],
            recv_sem=self.recv_sem.at[self.count], device_id=target, device_id_type=MESH,
        )
        self.count += 1
        copy.start()
        self.sent.append(copy)
        return copy

    def spots(self, k, level):
        p = self.place[self.axes[k][level]]
        return p, lax.rem(p + 1, 4), lax.rem(p + 2, 4), lax.rem(p + 3, 4)

    def peer(self, k, level, distance):
        return moved(self.place, self.axes[k][level], distance)

    def send_other(self, k):
        rows = pl.ds(k * PART, PART)
        src = self.part.at[1 - self.core, rows]
        self.first[k] = self.send(src, self.got.at[rows], self.other)

    def add_other(self, k):
        self.first[k].wait_recv()

        def body(start):
            rows = rows_at(k * PART + start, STEP)
            self.work[rows] = self.part[self.core, rows] + self.got[rows]

        for_rows(PART, STEP, body)

    def open_ring(self, k):
        size, cut = SIZES[0]
        _, up, far, down = self.spots(k, 0)
        after, before = self.peer(k, 0, 1), self.peer(k, 0, 3)
        base = k * PART
        src, slab = self.work, self.slabs[0]
        self.opened[k, 0] = [
            self.send(src.at[rows_at(base + far * size, cut)], self.half.at[k, 0], after),
            self.send(src.at[rows_at(base + far * size + cut, cut)], self.half.at[k, 1], before),
            self.send(src.at[rows_at(base + up * size + cut, cut)],
                      slab.at[k, 0, pl.ds(cut, cut)], after),
            self.send(src.at[rows_at(base + down * size, cut)], slab.at[k, 1, pl.ds(0, cut)],
                      before),
        ]

    def pass_ring(self, k):
        size, cut = SIZES[0]
        _, up, _, down = self.spots(k, 0)
        base = k * PART
        slab, copies = self.slabs[0], self.opened[k, 0]
        for side, start, target, at in (
            (0, base + up * size, self.peer(k, 0, 1), 0),
            (1, base + down * size + cut, self.peer(k, 0, 3), cut),
        ):
            copies[side].wait_recv()

            def body(offset):
                rows = rows_at(start + offset, STEP)
                passed = self.half[k, side, rows_at(offset, STEP)]
                self.work[rows] = self.work[rows] + passed

            for_rows(cut, STEP, body)
            copies.append(
                self.send(self.work.at[rows_at(start, cut)], slab.at[k, side, pl.ds(at, cut)],
                          target)
            )

    def open_level(self, k, level):
        size = SIZES[level][0]
        src, base = self.sums[level - 1], k * 4 * size
        spots = self.spots(k, level)
        self.opened[k, level] = [
            self.send(src.at[rows_at(base + spots[d] * size, size)],
                      self.slabs[level].at[k, d - 1], self.peer(k, level, d))
            for d in (1, 2, 3)
        ]

    def close_level(self, k, level, store):
        size = SIZES[level][0]
        step = (STEP, 160, 48)[level]
        copies = self.opened[k, level]
        for copy in copies[2:] if level == 0 else copies:
            copy.wait_recv()
        src, base = (self.work, k * PART) if level == 0 else (self.sums[level - 1], k * 4 * size)
        base = base + self.spots(k, level)[0] * size
        slab = self.slabs[level]

        def body(start):
            total = src[rows_at(base + start, step)].astype(jnp.float32)
            for side in range(slab.shape[1]):
                total = total + slab[k, side, rows_at(start, step)].astype(jnp.float32)
            store(start, total)

        for_rows(size, step, body)

    def store_sum(self, k, level):
        pitch = PART // 4 if level == 0 else THIRD

        def store(start, total):
            self.sums[level][rows_at(k * pitch + start, total.shape[0])] = total.astype(jnp.bfloat16)

        self.close_level(k, level, store)
        if level == 1:
            self.sums[1][pl.ds(k * THIRD + 160, 32)] = jnp.zeros((32, 128), jnp.bfloat16)

    def store_last(self, k, scale):
        def store(start, total):
            rows = rows_at(k * THIRD + self.spots(k, 2)[0] * 48 + start, 48)
            self.piece[rows] = (total * scale).astype(jnp.bfloat16)

        self.close_level(k, 2, store)

    def spread_rows(self, k, level):
        if level == 2:
            return self.piece, k * THIRD
        base = k * PART
        if level == 1:
            base = base + self.spots(k, 0)[0] * SIZES[0][0]
        return self.res, base

    def open_spread(self, k, level):
        size = SIZES[level][0]
        ref, base = self.spread_rows(k, level)
        rows = rows_at(base + self.spots(k, level)[0] * size, size)
        self.spread[k, level] = [
            self.send(ref.at[rows], ref.at[rows], self.peer(k, level, d)) for d in (1, 2, 3)
        ]

    def piece_at(self, k, slab, distance):
        index = self.spots(k, 1)[(4 - distance) % 4]
        return index, rows_at(k * PART + slab * 640 + index * 160, 160)

    def send_piece(self, k, distance):
        if distance:
            self.spread[k, 1][distance - 1].wait_recv()
        _, rows = self.piece_at(k, self.spots(k, 0)[0], distance)
        src = self.res.at[rows]
        self.spread[k, 0, distance] = [
            self.send(src, src, self.peer(k, 0, d)) for d in (1, 3)
        ]

    def pass_piece(self, k, distance):
        copies = self.spread[k, 0, distance]
        for copy in copies:
            copy.wait_recv()
        _, up, _, down = self.spots(k, 0)
        index, _ = self.piece_at(k, 0, distance)
        first = index < 2
        _, rows = self.piece_at(k, jnp.where(first, down, up), distance)
        src = self.res.at[rows]
        copies.append(self.send(src, src, self.peer(k, 0, jnp.where(first, 1, 3))))
        for slab in (down, up):
            self.hand_out(k * PART + slab * 640 + index * 160, 160)

    def close_spread(self, k, level):
        for copy in self.spread[k, level]:
            copy.wait_recv()
        _, rows = self.piece_at(k, self.spots(k, 0)[0], 0)
        self.res[rows] = self.piece[pl.ds(k * THIRD, 160)]

    def hand_out(self, start, count):
        rows = rows_at(start, count)
        lanes = pl.ds(pl.multiple_of(self.core * 128, 128), 128)
        near = pltpu.make_async_copy(
            self.res.at[rows], self.out.at[rows, lanes], self.send_sem.at[self.count]
        )
        self.count += 1
        near.start()
        self.outs.append((near, self.send(self.res.at[rows], self.out.at[rows, lanes], self.other)))

    def hand_own(self, k):
        self.hand_out(k * PART + self.spots(k, 0)[0] * 640, 640)

    def hand_far(self, k):
        for distance in range(4):
            self.spread[k, 0, distance][2].wait_recv()
        self.hand_out(k * PART + self.spots(k, 0)[2] * 640, 640)

    def end(self):
        for copy in self.sent:
            copy.wait_send()
        for near, far in self.outs:
            near.wait()
            far.wait_recv()


NEAR = [(0, 1), (0, -1), (1, 0), (-1, 0), (1, 1), (1, -1), (-1, 1), (-1, -1)]
NN = (((1,), (0,)), ((), ()))
NT = (((1,), (1,)), ((), ()))
TN = (((0,), (0,)), ((), ()))


def dot(left, right, dims=NN):
    return lax.dot_general(left, right, dims, preferred_element_type=jnp.float32)


def silu(value):
    return value * jax.nn.sigmoid(value)


def silu_slope(value):
    gate = jax.nn.sigmoid(value)
    return gate * (1.0 + value * (1.0 - gate))


def grid_of(rows, cols):
    return (
        lax.broadcasted_iota(jnp.int32, (rows, cols), 0),
        lax.broadcasted_iota(jnp.int32, (rows, cols), 1),
    )


def table(mask):
    return mask.astype(jnp.float32).astype(jnp.bfloat16)


def later_cell(block):
    lane = lax.broadcasted_iota(jnp.int32, block.shape, 1)
    return jnp.where(lane == 127, 0.0, pltpu.roll(block, 127, 1))


def earlier_cell(block):
    lane = lax.broadcasted_iota(jnp.int32, block.shape, 1)
    return jnp.where(lane == 0, 0.0, pltpu.roll(block, 1, 1))


def window_kernel(scale, features_hbm, labels, w_down_hbm, head_rows, w_mid_hbm, w_up_hbm,
                  grad_hbm, sum_out, features, w_down, grad_out, w_head, label_cells, w_mid, w_up, low, low_moved, down_pre, mid_pre, split, head, head_t,
                  partial, arrived, known, logit_grad, columns, back, back_moved,
                  part, got, work, half, slab0, slab1, slab2, sum0, sum1, piece, res,
                  load_sem, send_sem, recv_sem, sum_send, sum_recv):
    gx, gy = lax.axis_index("gx"), lax.axis_index("gy")

    def near(dx, dy):
        return (lax.rem(gx + (dx + 16), 16), lax.rem(gy + (dy + 8), 8))

    loads = [
        pltpu.make_async_copy(src, dst, load_sem.at[index])
        for index, (src, dst) in enumerate(
            [(w_mid_hbm, w_mid), (w_up_hbm, w_up), (features_hbm, features), (w_down_hbm, w_down)]
        )
    ]
    barrier = pltpu.get_barrier_semaphore()
    summing = Summing(
        part, sum_out, got, work, half, (slab0, slab1, slab2), (sum0, sum1), piece, res,
        sum_send, sum_recv,
    )
    peers = [near(dx, dy) for dx, dy in NEAR] + summing.peers()
    for peer in peers:
        pl.semaphore_signal(barrier, inc=1, device_id=peer, device_id_type=MESH)
    for index in (2, 3, 1, 0):
        loads[index].start()
    w_head[...] = jnp.zeros((16, 128), jnp.float32)
    w_head[pl.ds(0, 4), :] = head_rows[...].astype(jnp.float32)
    heads = w_head[...].astype(jnp.bfloat16)
    for a in (0, 1):
        label_cells[pl.ds(4 * a, 4), :] = labels[a].astype(jnp.float32)

    sent = []

    def exchange(stage, src, dst, places, apart=False):
        copies = []
        for index, (dx, dy) in enumerate(NEAR):
            src_x, dst_x, src_y, dst_y = places(dx, dy)
            copy = pltpu.make_async_remote_copy(
                src_ref=src.at[src_x, src_y],
                dst_ref=dst.at[index, dst_x, dst_y] if apart else dst.at[dst_x, dst_y],
                send_sem=send_sem.at[8 * stage + index], recv_sem=recv_sem.at[8 * stage + index],
                device_id=near(dx, dy), device_id_type=MESH,
            )
            copy.start()
            copies.append(copy)
        sent.extend(copies)
        return copies

    def finish(copies, buffer):
        for copy in copies:
            copy.wait_recv()
        wide, tall = buffer.shape[0], buffer.shape[1]

        @pl.when(gx == 0)
        def _():
            buffer[0] = jnp.zeros(buffer.shape[1:], buffer.dtype)

        @pl.when(gx == 15)
        def _():
            buffer[wide - 1] = jnp.zeros(buffer.shape[1:], buffer.dtype)

        @pl.when(gy == 0)
        def _():
            for x in range(wide):
                buffer[x, 0] = jnp.zeros(buffer.shape[2:], buffer.dtype)

        @pl.when(gy == 7)
        def _():
            for x in range(wide):
                buffer[x, tall - 1] = jnp.zeros(buffer.shape[2:], buffer.dtype)

    one = lambda i: pl.ds(i, 1)

    def brick_places(dx, dy):
        src_y = {0: pl.ds(1, 2), 1: one(2), -1: one(1)}[dy]
        dst_y = {0: pl.ds(1, 2), 1: one(0), -1: one(3)}[dy]
        return one(1), one(1 - dx), src_y, dst_y

    def upper_places(dx, dy):
        src_x = {0: pl.ds(1, 2), 1: one(2), -1: one(1)}[dx]
        dst_x = {0: pl.ds(1, 2), 1: one(0), -1: one(3)}[dx]
        src_y = {0: pl.ds(1, 4), 1: one(4), -1: one(1)}[dy]
        dst_y = {0: pl.ds(1, 4), 1: one(0), -1: one(5)}[dy]
        return src_x, dst_x, src_y, dst_y

    def spill_places(dx, dy):
        low_two, all_x, all_y = pl.ds(0, 2), pl.ds(0, 4), pl.ds(0, 6)
        src_x = {0: all_x, 1: pl.ds(2, 2), -1: low_two}[dx]
        dst_x = {0: all_x, 1: low_two, -1: pl.ds(2, 2)}[dx]
        src_y = {0: all_y, 1: pl.ds(4, 2), -1: low_two}[dy]
        dst_y = {0: all_y, 1: low_two, -1: pl.ds(4, 2)}[dy]
        return src_x, dst_x, src_y, dst_y

    inside_x = {0: (gx > 0).astype(jnp.float32), 1: (gx < 15).astype(jnp.float32)}
    inside_y = {0: (gy > 0).astype(jnp.float32), 1: (gy < 7).astype(jnp.float32)}

    def inside(value, x, y):
        value = value if x is None else value * inside_x[x]
        return value if y is None else value * inside_y[y]

    lanes = lambda i: pl.ds(i * 128, 128)
    rows, cols = grid_of(256, 256)
    apart = table(rows == jnp.where(cols < 128, 2 * cols, 2 * cols - 255))
    loads[2].wait()
    split[...] = dot(features[...], apart).astype(jnp.bfloat16)
    loads[3].wait()
    total = jnp.zeros((256, 256), jnp.float32)
    for a in (0, 1):
        for b in (0, 1):
            weight = jnp.concatenate([w_down[4 * a + 2 * b], w_down[4 * a + 2 * b + 1]], axis=1)
            cells = [
                jnp.concatenate(
                    [split[pl.ds((4 * a + 2 * y + b) * 128, 128), lanes(c)] for y in (0, 1)],
                    axis=1,
                )
                for c in (0, 1)
            ]
            total = total + dot(weight, jnp.concatenate(cells, axis=0))
    down_pre[...] = total
    total = silu(total).astype(jnp.bfloat16)
    low[1, 1] = total[:, :128]
    low[1, 2] = total[:, 128:]
    pl.semaphore_wait(barrier, len(peers))
    copies = exchange(0, low, low, brick_places)

    own_logits = [
        dot(heads, split[pl.ds(column * 128, 128), :])[:8] for column in range(8)
    ]
    label_rows = dot(label_cells[...].astype(jnp.bfloat16), apart)
    for a in (0, 1):
        for y in range(4):
            known[1 + a, 1 + y] = own_logits[4 * a + y]
            known[1 + a, 1 + y, pl.ds(4, 1), :] = label_rows[4 * a + y : 4 * a + y + 1, :]
    known_copies = exchange(2, known, known, upper_places)
    loads[1].wait()
    for tap in range(64):
        mixed = dot(heads, w_up[pl.ds(tap * 128, 128), :])
        head[pl.ds(tap * 8, 8), :] = mixed[:8]
    head_t[...] = jnp.transpose(head[...])
    loads[0].wait()

    finish(copies, low)
    rows, cols = grid_of(128, 256)
    moves = table(rows == jnp.where(cols < 128, cols - 1, cols - 127))
    for x in range(3):
        for y in range(4):
            low_moved[1, x, y] = low[x, y]
            both = dot(low[x, y], moves).astype(jnp.bfloat16)
            low_moved[0, x, y] = both[:, :128]
            low_moved[2, x, y] = both[:, 128:]
    total = jnp.zeros((256, 256), jnp.float32)
    for a in range(3):
        for b in range(3):
            taps = [9 * a + 3 * b + c for c in range(3)]
            weight = jnp.concatenate([w_mid[pl.ds(t * 256, 256), :] for t in taps], axis=1)
            cells = [
                jnp.concatenate([low_moved[c, a, b], low_moved[c, a, b + 1]], axis=1)
                for c in range(3)
            ]
            total = total + dot(weight, jnp.concatenate(cells, axis=0))
    mid_pre[...] = total
    mid = silu(total).astype(jnp.bfloat16)

    head_high = head[...].astype(jnp.bfloat16)
    head_low = (head[...] - head_high.astype(jnp.float32)).astype(jnp.bfloat16)
    spread = dot(head_high, mid) + dot(head_low, mid)
    for x in range(4):
        for y in range(6):
            block = None
            for cell in (0, 1):
                tap = y - 2 * cell
                if 0 <= tap < 4:
                    piece = spread[(4 * x + tap) * 32 : (4 * x + tap + 1) * 32,
                                   cell * 128 : cell * 128 + 128]
                    block = piece if block is None else block + piece
            partial[x, y, :, lanes(0)] = block[8:16] + earlier_cell(block[24:32])
            partial[x, y, :, lanes(1)] = block[16:24] + later_cell(block[0:8])
    copies = exchange(1, partial, arrived, spill_places, True)
    slope = silu_slope(mid_pre[...])
    head_t_high = head_t[...].astype(jnp.bfloat16)
    head_t_low = (head_t[...] - head_t_high.astype(jnp.float32)).astype(jnp.bfloat16)
    classes = lax.broadcasted_iota(jnp.int32, (8, 256), 0)
    for copy in known_copies + copies:
        copy.wait_recv()
    for x in range(4):
        for y in range(6):
            value = known[x, y] + partial[x, y]
            side_x = 0 if x < 2 else 1
            side_y = {0: 0, 1: 0, 4: 1, 5: 1}.get(y)
            from_x, from_y = 1 - 2 * side_x, None if side_y is None else 1 - 2 * side_y
            value = value + inside(arrived[NEAR.index((from_x, 0)), x, y], side_x, None)
            if side_y is not None:
                value = value + inside(arrived[NEAR.index((0, from_y)), x, y], None, side_y)
                value = value + inside(
                    arrived[NEAR.index((from_x, from_y)), x, y], side_x, side_y
                )
            target = (classes.astype(jnp.float32) == known[x, y, pl.ds(4, 1), :])
            grad = jax.nn.sigmoid(value) - target.astype(jnp.float32)
            grad = jnp.where(classes < 4, grad, 0.0).astype(jnp.bfloat16).astype(jnp.float32)
            grad = inside(grad, {0: 0, 3: 1}.get(x), {0: 0, 5: 1}.get(y))
            logit_grad[x, y] = grad
            even, odd = grad[:, :128], grad[:, 128:]
            block = jnp.concatenate([earlier_cell(odd), even, odd, later_cell(even)], axis=0)
            block = block.astype(jnp.bfloat16)
            for cell in (0, 1):
                tap = y - 2 * cell
                if 0 <= tap < 4:
                    columns[pl.ds((4 * x + tap) * 32, 32), lanes(cell)] = block
    mid_grad = dot(head_t_high, columns[...]) + dot(head_t_low, columns[...])
    mid_pre_grad = (mid_grad * slope).astype(jnp.bfloat16)
    turned = jnp.transpose(mid_pre_grad)
    back[1, 1] = turned[:128]
    back[1, 2] = turned[128:]

    def keep(start, value):
        value = value.astype(jnp.bfloat16)
        rows = pl.ds(start, value.shape[0])
        part[0, rows] = value[:, :128]
        part[1, rows] = value[:, 128:]

    thirds = range(3)
    for tap in range(27):
        a, b, c = tap // 9, tap // 3 % 3, tap % 3
        cells = jnp.concatenate([low_moved[c, a, b], low_moved[c, a, b + 1]], axis=1)
        keep(tap * 256, dot(mid_pre_grad, cells, NT))
        if tap in (9, 19):
            summing.send_other(tap // 10)
    keep(27 * 256, dot(columns[...], mid, NT))
    keep(27 * 256 + 512, jnp.zeros((256, 256), jnp.float32))
    summing.send_other(2)
    for k in thirds:
        summing.add_other(k)
        summing.open_ring(k)
    for k in thirds:
        summing.pass_ring(k)

    for k in thirds:
        summing.store_sum(k, 0)
        summing.open_level(k, 1)

    for k in thirds:
        summing.store_sum(k, 1)
        summing.open_level(k, 2)
    copies = exchange(3, back, back, brick_places)

    for k in thirds:
        summing.store_last(k, scale)
        summing.open_spread(k, 2)
    for k in thirds:
        summing.close_spread(k, 2)
        summing.open_spread(k, 1)
        summing.send_piece(k, 0)

    finish(copies, back)
    rows, cols = grid_of(256, 128)
    moves = table(cols == jnp.where(rows < 128, rows + 1, rows - 129))
    for x in range(3):
        for y in range(4):
            back_moved[x, y, :, pl.ds(256, 256)] = back[x, y]
            both = dot(moves, back[x, y]).astype(jnp.bfloat16)
            back_moved[x, y, :, pl.ds(0, 256)] = both[:128]
            back_moved[x, y, :, pl.ds(512, 256)] = both[128:]
    total = jnp.zeros((256, 256), jnp.float32)
    for a in range(3):
        for b in range(3):
            cells = jnp.concatenate(
                [back_moved[2 - a, 2 - b], back_moved[2 - a, 3 - b]], axis=0
            )
            total = total + dot(cells, w_mid[pl.ds((3 * a + b) * 768, 768), :])
    for distance in (1, 3, 2):
        for k in thirds:
            summing.send_piece(k, distance)
    for k in thirds:
        summing.hand_own(k)
    down_grad = (jnp.transpose(total) * silu_slope(down_pre[...])).astype(jnp.bfloat16)

    def finish_features(a):
        for b in (0, 1):
            weight = jnp.concatenate([w_down[4 * a + 2 * b], w_down[4 * a + 2 * b + 1]], axis=1)
            pieces = dot(weight, down_grad, TN)
            for cell in (0, 1):
                y = 2 * cell + b
                grad = jnp.concatenate(
                    [logit_grad[1 + a, 1 + y], jnp.zeros((8, 256), jnp.float32)], axis=0
                ).astype(jnp.bfloat16)
                hidden = dot(heads, grad, TN).astype(jnp.bfloat16).astype(jnp.float32)
                at = slice(cell * 128, cell * 128 + 128)
                whole = jnp.concatenate([pieces[:128, at], pieces[128:, at]], axis=1) + hidden
                grad_out[pl.ds((4 * a + y) * 128, 128), :] = dot(
                    whole.astype(jnp.bfloat16), apart, NT
                ).astype(jnp.bfloat16)

    finish_features(0)
    for distance in (0, 1, 3, 2):
        for k in thirds:
            summing.pass_piece(k, distance)
    finish_features(1)
    store_grad = pltpu.make_async_copy(grad_out, grad_hbm, load_sem.at[4])
    store_grad.start()
    for k in thirds:
        summing.hand_far(k)
    for copy in sent:
        copy.wait_send()
    summing.end()
    store_grad.wait()


def expand_kernel(sums, head_rows, mid_out, up_out, w_head, mixed, up, load_sem, mid_sem, up_sem):
    mid_copy = pltpu.make_async_copy(sums.at[pl.ds(0, 6912)], mid_out, mid_sem)
    load = pltpu.make_async_copy(sums.at[pl.ds(6912, 512)], mixed, load_sem)
    load.start()
    mid_copy.start()
    w_head[...] = jnp.zeros((16, 256), jnp.float32)
    w_head[pl.ds(0, 4), pl.ds(0, 128)] = head_rows[...].astype(jnp.float32)
    w_head[pl.ds(8, 4), pl.ds(128, 128)] = head_rows[...].astype(jnp.float32)
    heads = jnp.transpose(w_head[...]).astype(jnp.bfloat16)
    load.wait()
    stores = []
    for pair in range(32):
        pairs = dot(heads, mixed[pl.ds(pair * 16, 16), :])
        up[pl.ds(pair * 256, 256), :] = pairs.astype(jnp.bfloat16)
        if pair % 8 == 7:
            rows = pl.ds((pair - 7) * 256, 2048)
            store = pltpu.make_async_copy(up.at[rows], up_out.at[rows], up_sem.at[pair // 8])
            store.start()
            stores.append(store)
    for store in stores:
        store.wait()
    mid_copy.wait()


def expand(sums, w_head):
    vmem, hbm = pl.BlockSpec(memory_space=pltpu.VMEM), pl.BlockSpec(memory_space=pl.ANY)
    return pl.pallas_call(
        expand_kernel,
        out_shape=[
            jax.ShapeDtypeStruct((6912, 256), jnp.bfloat16),
            jax.ShapeDtypeStruct((8192, 256), jnp.bfloat16),
        ],
        in_specs=[hbm, vmem],
        out_specs=[hbm, hbm],
        scratch_shapes=[
            pltpu.VMEM((16, 256), jnp.float32),
            pltpu.VMEM((512, 256), jnp.bfloat16),
            pltpu.VMEM((8192, 256), jnp.bfloat16),
            pltpu.SemaphoreType.DMA(()),
            pltpu.SemaphoreType.DMA(()),
            pltpu.SemaphoreType.DMA((4,)),
        ],
        compiler_params=pltpu.CompilerParams(vmem_limit_bytes=32 * 2**20),
        cost_estimate=pl.CostEstimate(flops=10**8, bytes_accessed=12 * 10**6, transcendentals=0),
        name="expand",
    )(sums, w_head)


def window(features, labels, w_down, w_mid, w_up, w_head):
    half = lambda *shape: pltpu.VMEM(shape, jnp.bfloat16)
    full = lambda *shape: pltpu.VMEM(shape, jnp.float32)
    vmem, hbm = pl.BlockSpec(memory_space=pltpu.VMEM), pl.BlockSpec(memory_space=pl.ANY)
    return pl.pallas_call(
        functools.partial(window_kernel, 1.0 / math.sqrt(32768)),
        out_shape=[
            jax.ShapeDtypeStruct((1024, 256), jnp.bfloat16),
            jax.ShapeDtypeStruct((ROWS, 256), jnp.bfloat16),
        ],
        in_specs=[hbm, vmem, hbm, vmem, hbm, hbm],
        out_specs=[hbm, hbm],
        scratch_shapes=[
            half(1024, 256), half(8, 256, 128), half(1024, 256),
            full(16, 128), full(8, 256),
            half(27 * 256, 256), half(64 * 128, 256),
            half(3, 4, 256, 128), half(3, 3, 4, 256, 128),
            full(256, 256), full(256, 256),
            half(1024, 256), full(512, 256), full(256, 512),
            full(4, 6, 8, 256), full(8, 4, 6, 8, 256), full(4, 6, 8, 256), full(4, 6, 8, 256),
            half(512, 256), half(3, 4, 128, 256), half(3, 4, 128, 768),
            half(2, ROWS, 128), half(ROWS, 128), half(ROWS, 128),
            half(3, 2, 320, 128),
            half(3, 2, 640, 128), half(3, 3, 160, 128), half(3, 3, 48, 128),
            half(3 * 640, 128), half(3 * THIRD, 128), half(3 * THIRD, 128),
            half(ROWS, 128),
            pltpu.SemaphoreType.DMA((5,)),
            pltpu.SemaphoreType.DMA((32,)),
            pltpu.SemaphoreType.DMA((32,)),
            pltpu.SemaphoreType.DMA((200,)),
            pltpu.SemaphoreType.DMA((200,)),
        ],
        compiler_params=pltpu.CompilerParams(
            collective_id=8, has_side_effects=True, vmem_limit_bytes=60 * 2**20
        ),
        cost_estimate=pl.CostEstimate(flops=4 * 10**9, bytes_accessed=2 * 10**7, transcendentals=0),
        name="window",
    )(features, labels, w_down, w_head, w_mid, w_up)


def local(features, labels, w_down, w_mid, w_up, w_head):
    chans_up = features.shape[0]
    chans_mid = w_mid.shape[3]
    flat = features.transpose(1, 2, 0, 3).reshape(8 * chans_up, 256)
    grad, sums = window(
        flat, labels, w_down.reshape(8, chans_mid, chans_up),
        w_mid.reshape(27 * chans_mid, chans_mid), w_up.reshape(64 * chans_up, chans_mid), w_head,
    )
    feature_grad = grad.reshape(2, 4, chans_up, 256).transpose(2, 0, 1, 3)
    mid_out, up_out = expand(sums, w_head)
    return (
        feature_grad,
        mid_out.reshape(3, 3, 3, chans_mid, chans_mid),
        up_out.reshape(4, 4, 4, chans_up, chans_mid),
    )


def solution(mesh):
    return jax.shard_map(
        local,
        mesh=mesh,
        in_specs=(P(None, "gx", "gy", None), P("gx", "gy", None), P(), P(), P(), P()),
        out_specs=(P(None, "gx", "gy", None), P(), P()),
        check_vma=False,
    )
```

```python
import functools
import math

import jax
import jax.numpy as jnp
from jax import lax
from jax.experimental import pallas as pl
from jax.experimental.pallas import tpu as pltpu
from jax.sharding import PartitionSpec as P

MESH = pl.DeviceIdType.MESH
ROWS = 7680
PART = ROWS // 3
SIZES = [(640, 320), (160, 80), (48, 32)]
THIRD = 4 * 48
STEP = 320


def my_place():
    gx, gy = lax.axis_index("gx"), lax.axis_index("gy")
    return lax.div(gx, 4), lax.div(gy, 2), lax.rem(gx, 4), lax.rem(gy, 2)


def device_at(x, y, z, core):
    return (x * 4 + z, y * 2 + core)


def moved(place, axis, distance):
    spot = list(place)
    spot[axis] = lax.rem(spot[axis] + distance, 4)
    return device_at(*spot)


def rows_at(start, count):
    return pl.ds(pl.multiple_of(start, 16), count)


def for_rows(count, step, body):
    def one(i, carry):
        body(i * step)
        return carry

    lax.fori_loop(0, count // step, one, 0)


class Summing:
    axes = [(0, 1, 2), (1, 2, 0), (2, 0, 1)]

    def __init__(self, part, out, got, work, half, slabs, sums, piece, res, send_sem, recv_sem):
        self.part, self.out, self.got, self.work, self.half = part, out, got, work, half
        self.slabs, self.sums, self.piece, self.res = slabs, sums, piece, res
        self.send_sem, self.recv_sem = send_sem, recv_sem
        self.place = my_place()
        self.core = self.place[3]
        self.other = device_at(*self.place[:3], 1 - self.core)
        self.count, self.sent, self.outs = 0, [], []
        self.first, self.opened, self.spread = {}, {}, {}

    def peers(self):
        places = [moved(self.place, axis, d) for axis in range(3) for d in (1, 2, 3)]
        return [self.other] + places

    def send(self, src, dst, target):
        copy = pltpu.make_async_remote_copy(
            src_ref=src, dst_ref=dst, send_sem=self.send_sem.at[self.count],
            recv_sem=self.recv_sem.at[self.count], device_id=target, device_id_type=MESH,
        )
        self.count += 1
        copy.start()
        self.sent.append(copy)
        return copy

    def spots(self, k, level):
        p = self.place[self.axes[k][level]]
        return p, lax.rem(p + 1, 4), lax.rem(p + 2, 4), lax.rem(p + 3, 4)

    def peer(self, k, level, distance):
        return moved(self.place, self.axes[k][level], distance)

    def send_other(self, k):
        rows = pl.ds(k * PART, PART)
        src = self.part.at[1 - self.core, rows]
        self.first[k] = self.send(src, self.got.at[rows], self.other)

    def add_other(self, k):
        self.first[k].wait_recv()

        def body(start):
            rows = rows_at(k * PART + start, STEP)
            self.work[rows] = self.part[self.core, rows] + self.got[rows]

        for_rows(PART, STEP, body)

    def open_ring(self, k):
        size, cut = SIZES[0]
        _, up, far, down = self.spots(k, 0)
        after, before = self.peer(k, 0, 1), self.peer(k, 0, 3)
        base = k * PART
        src, slab = self.work, self.slabs[0]
        self.opened[k, 0] = [
            self.send(src.at[rows_at(base + far * size, cut)], self.half.at[k, 0], after),
            self.send(src.at[rows_at(base + far * size + cut, cut)], self.half.at[k, 1], before),
            self.send(src.at[rows_at(base + up * size + cut, cut)],
                      slab.at[k, 0, pl.ds(cut, cut)], after),
            self.send(src.at[rows_at(base + down * size, cut)], slab.at[k, 1, pl.ds(0, cut)],
                      before),
        ]

    def pass_ring(self, k):
        size, cut = SIZES[0]
        _, up, _, down = self.spots(k, 0)
        base = k * PART
        slab, copies = self.slabs[0], self.opened[k, 0]
        for side, start, target, at in (
            (0, base + up * size, self.peer(k, 0, 1), 0),
            (1, base + down * size + cut, self.peer(k, 0, 3), cut),
        ):
            copies[side].wait_recv()

            def body(offset):
                rows = rows_at(start + offset, STEP)
                passed = self.half[k, side, rows_at(offset, STEP)]
                self.work[rows] = self.work[rows] + passed

            for_rows(cut, STEP, body)
            copies.append(
                self.send(self.work.at[rows_at(start, cut)], slab.at[k, side, pl.ds(at, cut)],
                          target)
            )

    def open_level(self, k, level):
        size = SIZES[level][0]
        src, base = self.sums[level - 1], k * 4 * size
        spots = self.spots(k, level)
        self.opened[k, level] = [
            self.send(src.at[rows_at(base + spots[d] * size, size)],
                      self.slabs[level].at[k, d - 1], self.peer(k, level, d))
            for d in (1, 2, 3)
        ]

    def close_level(self, k, level, store):
        size = SIZES[level][0]
        step = (STEP, 160, 48)[level]
        copies = self.opened[k, level]
        for copy in copies[2:] if level == 0 else copies:
            copy.wait_recv()
        src, base = (self.work, k * PART) if level == 0 else (self.sums[level - 1], k * 4 * size)
        base = base + self.spots(k, level)[0] * size
        slab = self.slabs[level]

        def body(start):
            total = src[rows_at(base + start, step)].astype(jnp.float32)
            for side in range(slab.shape[1]):
                total = total + slab[k, side, rows_at(start, step)].astype(jnp.float32)
            store(start, total)

        for_rows(size, step, body)

    def store_sum(self, k, level):
        pitch = PART // 4 if level == 0 else THIRD

        def store(start, total):
            self.sums[level][rows_at(k * pitch + start, total.shape[0])] = total.astype(jnp.bfloat16)

        self.close_level(k, level, store)
        if level == 1:
            self.sums[1][pl.ds(k * THIRD + 160, 32)] = jnp.zeros((32, 128), jnp.bfloat16)

    def store_last(self, k, scale):
        def store(start, total):
            rows = rows_at(k * THIRD + self.spots(k, 2)[0] * 48 + start, 48)
            self.piece[rows] = (total * scale).astype(jnp.bfloat16)

        self.close_level(k, 2, store)

    def spread_rows(self, k, level):
        if level == 2:
            return self.piece, k * THIRD
        base = k * PART
        if level == 1:
            base = base + self.spots(k, 0)[0] * SIZES[0][0]
        return self.res, base

    def open_spread(self, k, level):
        size = SIZES[level][0]
        ref, base = self.spread_rows(k, level)
        rows = rows_at(base + self.spots(k, level)[0] * size, size)
        self.spread[k, level] = [
            self.send(ref.at[rows], ref.at[rows], self.peer(k, level, d)) for d in (1, 2, 3)
        ]

    def piece_at(self, k, slab, distance):
        index = self.spots(k, 1)[(4 - distance) % 4]
        return index, rows_at(k * PART + slab * 640 + index * 160, 160)

    def send_piece(self, k, distance):
        if distance:
            self.spread[k, 1][distance - 1].wait_recv()
        _, rows = self.piece_at(k, self.spots(k, 0)[0], distance)
        src = self.res.at[rows]
        self.spread[k, 0, distance] = [
            self.send(src, src, self.peer(k, 0, d)) for d in (1, 3)
        ]

    def pass_piece(self, k, distance):
        copies = self.spread[k, 0, distance]
        for copy in copies:
            copy.wait_recv()
        _, up, _, down = self.spots(k, 0)
        index, _ = self.piece_at(k, 0, distance)
        first = index < 2
        _, rows = self.piece_at(k, jnp.where(first, down, up), distance)
        src = self.res.at[rows]
        copies.append(self.send(src, src, self.peer(k, 0, jnp.where(first, 1, 3))))
        for slab in (down, up):
            self.hand_out(k * PART + slab * 640 + index * 160, 160)

    def close_spread(self, k, level):
        for copy in self.spread[k, level]:
            copy.wait_recv()
        _, rows = self.piece_at(k, self.spots(k, 0)[0], 0)
        self.res[rows] = self.piece[pl.ds(k * THIRD, 160)]

    def hand_out(self, start, count):
        rows = rows_at(start, count)
        lanes = pl.ds(pl.multiple_of(self.core * 128, 128), 128)
        near = pltpu.make_async_copy(
            self.res.at[rows], self.out.at[rows, lanes], self.send_sem.at[self.count]
        )
        self.count += 1
        near.start()
        self.outs.append((near, self.send(self.res.at[rows], self.out.at[rows, lanes], self.other)))

    def hand_own(self, k):
        self.hand_out(k * PART + self.spots(k, 0)[0] * 640, 640)

    def hand_far(self, k):
        for distance in range(4):
            self.spread[k, 0, distance][2].wait_recv()
        self.hand_out(k * PART + self.spots(k, 0)[2] * 640, 640)

    def end(self):
        for copy in self.sent:
            copy.wait_send()
        for near, far in self.outs:
            near.wait()
            far.wait_recv()


NEAR = [(1, 0), (-1, 0), (1, 1), (-1, -1), (1, -1), (-1, 1), (0, 1), (0, -1)]
NN = (((1,), (0,)), ((), ()))
NT = (((1,), (1,)), ((), ()))
TN = (((0,), (0,)), ((), ()))


def dot(left, right, dims=NN):
    return lax.dot_general(left, right, dims, preferred_element_type=jnp.float32)


def silu(value):
    return value * jax.nn.sigmoid(value)


def silu_slope(value):
    gate = jax.nn.sigmoid(value)
    return gate * (1.0 + value * (1.0 - gate))


def grid_of(rows, cols):
    return (
        lax.broadcasted_iota(jnp.int32, (rows, cols), 0),
        lax.broadcasted_iota(jnp.int32, (rows, cols), 1),
    )


def table(mask):
    return mask.astype(jnp.float32).astype(jnp.bfloat16)


def later_cell(block):
    lane = lax.broadcasted_iota(jnp.int32, block.shape, 1)
    return jnp.where(lane == 127, 0.0, pltpu.roll(block, 127, 1))


def earlier_cell(block):
    lane = lax.broadcasted_iota(jnp.int32, block.shape, 1)
    return jnp.where(lane == 0, 0.0, pltpu.roll(block, 1, 1))


def window_kernel(scale, features_hbm, labels, w_down_hbm, head_rows, w_mid_hbm, w_up_hbm,
                  grad_hbm, sum_out, features, w_down, grad_out, w_head, label_cells, w_mid, w_up, low, low_moved, down_pre, mid_pre, split, head, head_t,
                  partial, arrived, known, logit_grad, columns, back, back_moved,
                  part, got, work, half, slab0, slab1, slab2, sum0, sum1, piece, res,
                  load_sem, send_sem, recv_sem, sum_send, sum_recv):
    gx, gy = lax.axis_index("gx"), lax.axis_index("gy")

    def near(dx, dy):
        return (lax.rem(gx + (dx + 16), 16), lax.rem(gy + (dy + 8), 8))

    loads = [
        pltpu.make_async_copy(src, dst, load_sem.at[index])
        for index, (src, dst) in enumerate(
            [(w_mid_hbm, w_mid), (w_up_hbm, w_up), (features_hbm, features), (w_down_hbm, w_down)]
        )
    ]
    barrier = pltpu.get_barrier_semaphore()
    summing = Summing(
        part, sum_out, got, work, half, (slab0, slab1, slab2), (sum0, sum1), piece, res,
        sum_send, sum_recv,
    )
    peers = [near(dx, dy) for dx, dy in NEAR] + summing.peers()
    for peer in peers:
        pl.semaphore_signal(barrier, inc=1, device_id=peer, device_id_type=MESH)
    for index in (2, 3, 1, 0):
        loads[index].start()
    w_head[...] = jnp.zeros((16, 128), jnp.float32)
    w_head[pl.ds(0, 4), :] = head_rows[...].astype(jnp.float32)
    heads = w_head[...].astype(jnp.bfloat16)
    for a in (0, 1):
        label_cells[pl.ds(4 * a, 4), :] = labels[a].astype(jnp.float32)

    sent = []

    def exchange(stage, src, dst, places, apart=False):
        copies = []
        for index, (dx, dy) in enumerate(NEAR):
            src_x, dst_x, src_y, dst_y = places(dx, dy)
            copy = pltpu.make_async_remote_copy(
                src_ref=src.at[src_x, src_y],
                dst_ref=dst.at[index, dst_x, dst_y] if apart else dst.at[dst_x, dst_y],
                send_sem=send_sem.at[8 * stage + index], recv_sem=recv_sem.at[8 * stage + index],
                device_id=near(dx, dy), device_id_type=MESH,
            )
            copy.start()
            copies.append(copy)
        sent.extend(copies)
        return copies

    def finish(copies, buffer):
        for copy in copies:
            copy.wait_recv()
        wide, tall = buffer.shape[0], buffer.shape[1]

        @pl.when(gx == 0)
        def _():
            buffer[0] = jnp.zeros(buffer.shape[1:], buffer.dtype)

        @pl.when(gx == 15)
        def _():
            buffer[wide - 1] = jnp.zeros(buffer.shape[1:], buffer.dtype)

        @pl.when(gy == 0)
        def _():
            for x in range(wide):
                buffer[x, 0] = jnp.zeros(buffer.shape[2:], buffer.dtype)

        @pl.when(gy == 7)
        def _():
            for x in range(wide):
                buffer[x, tall - 1] = jnp.zeros(buffer.shape[2:], buffer.dtype)

    one = lambda i: pl.ds(i, 1)

    def brick_places(dx, dy):
        src_y = {0: pl.ds(1, 2), 1: one(2), -1: one(1)}[dy]
        dst_y = {0: pl.ds(1, 2), 1: one(0), -1: one(3)}[dy]
        return one(1), one(1 - dx), src_y, dst_y

    def upper_places(dx, dy):
        src_x = {0: pl.ds(1, 2), 1: one(2), -1: one(1)}[dx]
        dst_x = {0: pl.ds(1, 2), 1: one(0), -1: one(3)}[dx]
        src_y = {0: pl.ds(1, 4), 1: one(4), -1: one(1)}[dy]
        dst_y = {0: pl.ds(1, 4), 1: one(0), -1: one(5)}[dy]
        return src_x, dst_x, src_y, dst_y

    def spill_places(dx, dy):
        low_two, all_x, all_y = pl.ds(0, 2), pl.ds(0, 4), pl.ds(0, 6)
        src_x = {0: all_x, 1: pl.ds(2, 2), -1: low_two}[dx]
        dst_x = {0: all_x, 1: low_two, -1: pl.ds(2, 2)}[dx]
        src_y = {0: all_y, 1: pl.ds(4, 2), -1: low_two}[dy]
        dst_y = {0: all_y, 1: low_two, -1: pl.ds(4, 2)}[dy]
        return src_x, dst_x, src_y, dst_y

    inside_x = {0: (gx > 0).astype(jnp.float32), 1: (gx < 15).astype(jnp.float32)}
    inside_y = {0: (gy > 0).astype(jnp.float32), 1: (gy < 7).astype(jnp.float32)}

    def inside(value, x, y):
        value = value if x is None else value * inside_x[x]
        return value if y is None else value * inside_y[y]

    lanes = lambda i: pl.ds(i * 128, 128)
    rows, cols = grid_of(256, 256)
    apart = table(rows == jnp.where(cols < 128, 2 * cols, 2 * cols - 255))
    loads[2].wait()
    split[...] = dot(features[...], apart).astype(jnp.bfloat16)
    loads[3].wait()
    total = jnp.zeros((256, 256), jnp.float32)
    for a in (0, 1):
        for b in (0, 1):
            weight = jnp.concatenate([w_down[4 * a + 2 * b], w_down[4 * a + 2 * b + 1]], axis=1)
            cells = [
                jnp.concatenate(
                    [split[pl.ds((4 * a + 2 * y + b) * 128, 128), lanes(c)] for y in (0, 1)],
                    axis=1,
                )
                for c in (0, 1)
            ]
            total = total + dot(weight, jnp.concatenate(cells, axis=0))
    down_pre[...] = total
    total = silu(total).astype(jnp.bfloat16)
    low[1, 1] = total[:, :128]
    low[1, 2] = total[:, 128:]
    pl.semaphore_wait(barrier, len(peers))
    copies = exchange(0, low, low, brick_places)

    own_logits = [
        dot(heads, split[pl.ds(column * 128, 128), :])[:8] for column in range(8)
    ]
    label_rows = dot(label_cells[...].astype(jnp.bfloat16), apart)
    for a in (0, 1):
        for y in range(4):
            known[1 + a, 1 + y] = own_logits[4 * a + y]
            known[1 + a, 1 + y, pl.ds(4, 1), :] = label_rows[4 * a + y : 4 * a + y + 1, :]
    known_copies = exchange(2, known, known, upper_places)
    loads[1].wait()
    for tap in range(64):
        mixed = dot(heads, w_up[pl.ds(tap * 128, 128), :])
        head[pl.ds(tap * 8, 8), :] = mixed[:8]
    head_t[...] = jnp.transpose(head[...])
    loads[0].wait()

    finish(copies, low)
    rows, cols = grid_of(128, 256)
    moves = table(rows == jnp.where(cols < 128, cols - 1, cols - 127))
    for x in range(3):
        for y in range(4):
            low_moved[1, x, y] = low[x, y]
            both = dot(low[x, y], moves).astype(jnp.bfloat16)
            low_moved[0, x, y] = both[:, :128]
            low_moved[2, x, y] = both[:, 128:]
    total = jnp.zeros((256, 256), jnp.float32)
    for a in range(3):
        for b in range(3):
            taps = [9 * a + 3 * b + c for c in range(3)]
            weight = jnp.concatenate([w_mid[pl.ds(t * 256, 256), :] for t in taps], axis=1)
            cells = [
                jnp.concatenate([low_moved[c, a, b], low_moved[c, a, b + 1]], axis=1)
                for c in range(3)
            ]
            total = total + dot(weight, jnp.concatenate(cells, axis=0))
    mid_pre[...] = total
    mid = silu(total).astype(jnp.bfloat16)

    head_high = head[...].astype(jnp.bfloat16)
    head_low = (head[...] - head_high.astype(jnp.float32)).astype(jnp.bfloat16)
    spread = dot(head_high, mid) + dot(head_low, mid)
    for x in range(4):
        for y in range(6):
            block = None
            for cell in (0, 1):
                tap = y - 2 * cell
                if 0 <= tap < 4:
                    piece = spread[(4 * x + tap) * 32 : (4 * x + tap + 1) * 32,
                                   cell * 128 : cell * 128 + 128]
                    block = piece if block is None else block + piece
            partial[x, y, :, lanes(0)] = block[8:16] + earlier_cell(block[24:32])
            partial[x, y, :, lanes(1)] = block[16:24] + later_cell(block[0:8])
    copies = exchange(1, partial, arrived, spill_places, True)
    slope = silu_slope(mid_pre[...])
    head_t_high = head_t[...].astype(jnp.bfloat16)
    head_t_low = (head_t[...] - head_t_high.astype(jnp.float32)).astype(jnp.bfloat16)
    classes = lax.broadcasted_iota(jnp.int32, (8, 256), 0)
    for copy in known_copies + copies:
        copy.wait_recv()
    for x in range(4):
        for y in range(6):
            value = known[x, y] + partial[x, y]
            side_x = 0 if x < 2 else 1
            side_y = {0: 0, 1: 0, 4: 1, 5: 1}.get(y)
            from_x, from_y = 1 - 2 * side_x, None if side_y is None else 1 - 2 * side_y
            value = value + inside(arrived[NEAR.index((from_x, 0)), x, y], side_x, None)
            if side_y is not None:
                value = value + inside(arrived[NEAR.index((0, from_y)), x, y], None, side_y)
                value = value + inside(
                    arrived[NEAR.index((from_x, from_y)), x, y], side_x, side_y
                )
            target = (classes.astype(jnp.float32) == known[x, y, pl.ds(4, 1), :])
            grad = jax.nn.sigmoid(value) - target.astype(jnp.float32)
            grad = jnp.where(classes < 4, grad, 0.0).astype(jnp.bfloat16).astype(jnp.float32)
            grad = inside(grad, {0: 0, 3: 1}.get(x), {0: 0, 5: 1}.get(y))
            logit_grad[x, y] = grad
            even, odd = grad[:, :128], grad[:, 128:]
            block = jnp.concatenate([earlier_cell(odd), even, odd, later_cell(even)], axis=0)
            block = block.astype(jnp.bfloat16)
            for cell in (0, 1):
                tap = y - 2 * cell
                if 0 <= tap < 4:
                    columns[pl.ds((4 * x + tap) * 32, 32), lanes(cell)] = block
    mid_grad = dot(head_t_high, columns[...]) + dot(head_t_low, columns[...])
    mid_pre_grad = (mid_grad * slope).astype(jnp.bfloat16)
    turned = jnp.transpose(mid_pre_grad)
    back[1, 1] = turned[:128]
    back[1, 2] = turned[128:]

    def keep(start, value):
        value = value.astype(jnp.bfloat16)
        rows = pl.ds(start, value.shape[0])
        part[0, rows] = value[:, :128]
        part[1, rows] = value[:, 128:]

    thirds = range(3)
    for tap in range(27):
        a, b, c = tap // 9, tap // 3 % 3, tap % 3
        cells = jnp.concatenate([low_moved[c, a, b], low_moved[c, a, b + 1]], axis=1)
        keep(tap * 256, dot(mid_pre_grad, cells, NT))
        if tap in (9, 19):
            summing.send_other(tap // 10)
    keep(27 * 256, dot(columns[...], mid, NT))
    keep(27 * 256 + 512, jnp.zeros((256, 256), jnp.float32))
    summing.send_other(2)
    for k in thirds:
        summing.add_other(k)
        summing.open_ring(k)
    for k in thirds:
        summing.pass_ring(k)

    for k in thirds:
        summing.store_sum(k, 0)
        summing.open_level(k, 1)

    for k in thirds:
        summing.store_sum(k, 1)
        summing.open_level(k, 2)
    copies = exchange(3, back, back, brick_places)

    for k in thirds:
        summing.store_last(k, scale)
        summing.open_spread(k, 2)
    for k in thirds:
        summing.close_spread(k, 2)
        summing.open_spread(k, 1)
        summing.send_piece(k, 0)

    finish(copies, back)
    rows, cols = grid_of(256, 128)
    moves = table(cols == jnp.where(rows < 128, rows + 1, rows - 129))
    for x in range(3):
        for y in range(4):
            back_moved[x, y, :, pl.ds(256, 256)] = back[x, y]
            both = dot(moves, back[x, y]).astype(jnp.bfloat16)
            back_moved[x, y, :, pl.ds(0, 256)] = both[:128]
            back_moved[x, y, :, pl.ds(512, 256)] = both[128:]
    total = jnp.zeros((256, 256), jnp.float32)
    for a in range(3):
        for b in range(3):
            cells = jnp.concatenate(
                [back_moved[2 - a, 2 - b], back_moved[2 - a, 3 - b]], axis=0
            )
            total = total + dot(cells, w_mid[pl.ds((3 * a + b) * 768, 768), :])
    for distance in (1, 3, 2):
        for k in thirds:
            summing.send_piece(k, distance)
    for k in thirds:
        summing.hand_own(k)
    down_grad = (jnp.transpose(total) * silu_slope(down_pre[...])).astype(jnp.bfloat16)

    def finish_features(a):
        for b in (0, 1):
            weight = jnp.concatenate([w_down[4 * a + 2 * b], w_down[4 * a + 2 * b + 1]], axis=1)
            pieces = dot(weight, down_grad, TN)
            for cell in (0, 1):
                y = 2 * cell + b
                grad = jnp.concatenate(
                    [logit_grad[1 + a, 1 + y], jnp.zeros((8, 256), jnp.float32)], axis=0
                ).astype(jnp.bfloat16)
                hidden = dot(heads, grad, TN).astype(jnp.bfloat16).astype(jnp.float32)
                at = slice(cell * 128, cell * 128 + 128)
                whole = jnp.concatenate([pieces[:128, at], pieces[128:, at]], axis=1) + hidden
                grad_out[pl.ds((4 * a + y) * 128, 128), :] = dot(
                    whole.astype(jnp.bfloat16), apart, NT
                ).astype(jnp.bfloat16)

    finish_features(0)
    for distance in (0, 1, 3, 2):
        for k in thirds:
            summing.pass_piece(k, distance)
    finish_features(1)
    store_grad = pltpu.make_async_copy(grad_out, grad_hbm, load_sem.at[4])
    store_grad.start()
    for k in thirds:
        summing.hand_far(k)
    for copy in sent:
        copy.wait_send()
    summing.end()
    store_grad.wait()


def expand_kernel(sums, head_rows, mid_out, up_out, w_head, mixed, up, load_sem, mid_sem, up_sem):
    mid_copy = pltpu.make_async_copy(sums.at[pl.ds(0, 6912)], mid_out, mid_sem)
    load = pltpu.make_async_copy(sums.at[pl.ds(6912, 512)], mixed, load_sem)
    load.start()
    mid_copy.start()
    w_head[...] = jnp.zeros((16, 256), jnp.float32)
    w_head[pl.ds(0, 4), pl.ds(0, 128)] = head_rows[...].astype(jnp.float32)
    w_head[pl.ds(8, 4), pl.ds(128, 128)] = head_rows[...].astype(jnp.float32)
    heads = jnp.transpose(w_head[...]).astype(jnp.bfloat16)
    load.wait()
    stores = []
    for pair in range(32):
        pairs = dot(heads, mixed[pl.ds(pair * 16, 16), :])
        up[pl.ds(pair * 256, 256), :] = pairs.astype(jnp.bfloat16)
        if pair % 8 == 7:
            rows = pl.ds((pair - 7) * 256, 2048)
            store = pltpu.make_async_copy(up.at[rows], up_out.at[rows], up_sem.at[pair // 8])
            store.start()
            stores.append(store)
    for store in stores:
        store.wait()
    mid_copy.wait()


def expand(sums, w_head):
    vmem, hbm = pl.BlockSpec(memory_space=pltpu.VMEM), pl.BlockSpec(memory_space=pl.ANY)
    return pl.pallas_call(
        expand_kernel,
        out_shape=[
            jax.ShapeDtypeStruct((6912, 256), jnp.bfloat16),
            jax.ShapeDtypeStruct((8192, 256), jnp.bfloat16),
        ],
        in_specs=[hbm, vmem],
        out_specs=[hbm, hbm],
        scratch_shapes=[
            pltpu.VMEM((16, 256), jnp.float32),
            pltpu.VMEM((512, 256), jnp.bfloat16),
            pltpu.VMEM((8192, 256), jnp.bfloat16),
            pltpu.SemaphoreType.DMA(()),
            pltpu.SemaphoreType.DMA(()),
            pltpu.SemaphoreType.DMA((4,)),
        ],
        compiler_params=pltpu.CompilerParams(vmem_limit_bytes=32 * 2**20),
        cost_estimate=pl.CostEstimate(flops=10**8, bytes_accessed=12 * 10**6, transcendentals=0),
        name="expand",
    )(sums, w_head)


def window(features, labels, w_down, w_mid, w_up, w_head):
    half = lambda *shape: pltpu.VMEM(shape, jnp.bfloat16)
    full = lambda *shape: pltpu.VMEM(shape, jnp.float32)
    vmem, hbm = pl.BlockSpec(memory_space=pltpu.VMEM), pl.BlockSpec(memory_space=pl.ANY)
    return pl.pallas_call(
        functools.partial(window_kernel, 1.0 / math.sqrt(32768)),
        out_shape=[
            jax.ShapeDtypeStruct((1024, 256), jnp.bfloat16),
            jax.ShapeDtypeStruct((ROWS, 256), jnp.bfloat16),
        ],
        in_specs=[hbm, vmem, hbm, vmem, hbm, hbm],
        out_specs=[hbm, hbm],
        scratch_shapes=[
            half(1024, 256), half(8, 256, 128), half(1024, 256),
            full(16, 128), full(8, 256),
            half(27 * 256, 256), half(64 * 128, 256),
            half(3, 4, 256, 128), half(3, 3, 4, 256, 128),
            full(256, 256), full(256, 256),
            half(1024, 256), full(512, 256), full(256, 512),
            full(4, 6, 8, 256), full(8, 4, 6, 8, 256), full(4, 6, 8, 256), full(4, 6, 8, 256),
            half(512, 256), half(3, 4, 128, 256), half(3, 4, 128, 768),
            half(2, ROWS, 128), half(ROWS, 128), half(ROWS, 128),
            half(3, 2, 320, 128),
            half(3, 2, 640, 128), half(3, 3, 160, 128), half(3, 3, 48, 128),
            half(3 * 640, 128), half(3 * THIRD, 128), half(3 * THIRD, 128),
            half(ROWS, 128),
            pltpu.SemaphoreType.DMA((5,)),
            pltpu.SemaphoreType.DMA((32,)),
            pltpu.SemaphoreType.DMA((32,)),
            pltpu.SemaphoreType.DMA((200,)),
            pltpu.SemaphoreType.DMA((200,)),
        ],
        compiler_params=pltpu.CompilerParams(
            collective_id=8, has_side_effects=True, vmem_limit_bytes=60 * 2**20
        ),
        cost_estimate=pl.CostEstimate(flops=4 * 10**9, bytes_accessed=2 * 10**7, transcendentals=0),
        name="window",
    )(features, labels, w_down, w_head, w_mid, w_up)


def local(features, labels, w_down, w_mid, w_up, w_head):
    chans_up = features.shape[0]
    chans_mid = w_mid.shape[3]
    flat = features.transpose(1, 2, 0, 3).reshape(8 * chans_up, 256)
    grad, sums = window(
        flat, labels, w_down.reshape(8, chans_mid, chans_up),
        w_mid.reshape(27 * chans_mid, chans_mid), w_up.reshape(64 * chans_up, chans_mid), w_head,
    )
    feature_grad = grad.reshape(2, 4, chans_up, 256).transpose(2, 0, 1, 3)
    mid_out, up_out = expand(sums, w_head)
    return (
        feature_grad,
        mid_out.reshape(3, 3, 3, chans_mid, chans_mid),
        up_out.reshape(4, 4, 4, chans_up, chans_mid),
    )


def solution(mesh):
    return jax.shard_map(
        local,
        mesh=mesh,
        in_specs=(P(None, "gx", "gy", None), P("gx", "gy", None), P(), P(), P(), P()),
        out_specs=(P(None, "gx", "gy", None), P(), P()),
        check_vma=False,
    )
```

```python
import functools
import math

import jax
import jax.numpy as jnp
from jax import lax
from jax.experimental import pallas as pl
from jax.experimental.pallas import tpu as pltpu
from jax.sharding import PartitionSpec as P

MESH = pl.DeviceIdType.MESH
ROWS = 7680
PART = ROWS // 3
SIZES = [(640, 320), (160, 80), (48, 32)]
THIRD = 4 * 48
STEP = 320


def my_place():
    gx, gy = lax.axis_index("gx"), lax.axis_index("gy")
    return lax.div(gx, 4), lax.div(gy, 2), lax.rem(gx, 4), lax.rem(gy, 2)


def device_at(x, y, z, core):
    return (x * 4 + z, y * 2 + core)


def moved(place, axis, distance):
    spot = list(place)
    spot[axis] = lax.rem(spot[axis] + distance, 4)
    return device_at(*spot)


def rows_at(start, count):
    return pl.ds(pl.multiple_of(start, 16), count)


def for_rows(count, step, body):
    def one(i, carry):
        body(i * step)
        return carry

    lax.fori_loop(0, count // step, one, 0)


class Summing:
    axes = [(0, 1, 2), (1, 2, 0), (2, 0, 1)]

    def __init__(self, part, out, got, work, half, slabs, sums, piece, res, send_sem, recv_sem):
        self.part, self.out, self.got, self.work, self.half = part, out, got, work, half
        self.slabs, self.sums, self.piece, self.res = slabs, sums, piece, res
        self.send_sem, self.recv_sem = send_sem, recv_sem
        self.place = my_place()
        self.core = self.place[3]
        self.other = device_at(*self.place[:3], 1 - self.core)
        self.count, self.sent, self.outs = 0, [], []
        self.first, self.opened, self.spread = {}, {}, {}

    def peers(self):
        places = [moved(self.place, axis, d) for axis in range(3) for d in (1, 2, 3)]
        return [self.other] + places

    def send(self, src, dst, target):
        copy = pltpu.make_async_remote_copy(
            src_ref=src, dst_ref=dst, send_sem=self.send_sem.at[self.count],
            recv_sem=self.recv_sem.at[self.count], device_id=target, device_id_type=MESH,
        )
        self.count += 1
        copy.start()
        self.sent.append(copy)
        return copy

    def spots(self, k, level):
        p = self.place[self.axes[k][level]]
        return p, lax.rem(p + 1, 4), lax.rem(p + 2, 4), lax.rem(p + 3, 4)

    def peer(self, k, level, distance):
        return moved(self.place, self.axes[k][level], distance)

    def send_other(self, k):
        rows = pl.ds(k * PART, PART)
        src = self.part.at[1 - self.core, rows]
        self.first[k] = self.send(src, self.got.at[rows], self.other)

    def add_other(self, k):
        self.first[k].wait_recv()

        def body(start):
            rows = rows_at(k * PART + start, STEP)
            self.work[rows] = self.part[self.core, rows] + self.got[rows]

        for_rows(PART, STEP, body)

    def open_ring(self, k):
        size, cut = SIZES[0]
        _, up, far, down = self.spots(k, 0)
        after, before = self.peer(k, 0, 1), self.peer(k, 0, 3)
        base = k * PART
        src, slab = self.work, self.slabs[0]
        copies = []
        for start in (0, 160):
            for side, target in ((0, after), (1, before)):
                rows = rows_at(base + far * size + side * cut + start, 160)
                copies.append(
                    self.send(src.at[rows], self.half.at[k, side, pl.ds(start, 160)], target)
                )
        copies += [
            self.send(src.at[rows_at(base + up * size + cut, cut)],
                      slab.at[k, 0, pl.ds(cut, cut)], after),
            self.send(src.at[rows_at(base + down * size, cut)], slab.at[k, 1, pl.ds(0, cut)],
                      before),
        ]
        self.opened[k, 0] = copies

    def pass_ring(self, k):
        size, cut = SIZES[0]
        _, up, _, down = self.spots(k, 0)
        base = k * PART
        slab, copies = self.slabs[0], self.opened[k, 0]
        for step in (0, 160):
            for side, start, target, at in (
                (0, base + up * size, self.peer(k, 0, 1), 0),
                (1, base + down * size + cut, self.peer(k, 0, 3), cut),
            ):
                copies[step // 80 + side].wait_recv()
                rows = rows_at(start + step, 160)
                self.work[rows] = self.work[rows] + self.half[k, side, pl.ds(step, 160)]
                copies.append(
                    self.send(self.work.at[rows], slab.at[k, side, pl.ds(at + step, 160)], target)
                )

    def open_level(self, k, level):
        size = SIZES[level][0]
        src, base = self.sums[level - 1], k * 4 * size
        spots = self.spots(k, level)
        self.opened[k, level] = [
            self.send(src.at[rows_at(base + spots[d] * size, size)],
                      self.slabs[level].at[k, d - 1], self.peer(k, level, d))
            for d in (1, 2, 3)
        ]

    def close_level(self, k, level, store):
        size = SIZES[level][0]
        step = (STEP, 160, 48)[level]
        copies = self.opened[k, level]
        for copy in copies[4:] if level == 0 else copies:
            copy.wait_recv()
        src, base = (self.work, k * PART) if level == 0 else (self.sums[level - 1], k * 4 * size)
        base = base + self.spots(k, level)[0] * size
        slab = self.slabs[level]

        def body(start):
            total = src[rows_at(base + start, step)].astype(jnp.float32)
            for side in range(slab.shape[1]):
                total = total + slab[k, side, rows_at(start, step)].astype(jnp.float32)
            store(start, total)

        for_rows(size, step, body)

    def store_sum(self, k, level):
        pitch = PART // 4 if level == 0 else THIRD

        def store(start, total):
            self.sums[level][rows_at(k * pitch + start, total.shape[0])] = total.astype(jnp.bfloat16)

        self.close_level(k, level, store)
        if level == 1:
            self.sums[1][pl.ds(k * THIRD + 160, 32)] = jnp.zeros((32, 128), jnp.bfloat16)

    def store_last(self, k, scale):
        def store(start, total):
            rows = rows_at(k * THIRD + self.spots(k, 2)[0] * 48 + start, 48)
            self.piece[rows] = (total * scale).astype(jnp.bfloat16)

        self.close_level(k, 2, store)

    def spread_rows(self, k, level):
        if level == 2:
            return self.piece, k * THIRD
        base = k * PART
        if level == 1:
            base = base + self.spots(k, 0)[0] * SIZES[0][0]
        return self.res, base

    def open_spread(self, k, level):
        size = SIZES[level][0]
        ref, base = self.spread_rows(k, level)
        rows = rows_at(base + self.spots(k, level)[0] * size, size)
        self.spread[k, level] = [
            self.send(ref.at[rows], ref.at[rows], self.peer(k, level, d)) for d in (1, 2, 3)
        ]

    def piece_at(self, k, slab, distance):
        index = self.spots(k, 1)[(4 - distance) % 4]
        return index, rows_at(k * PART + slab * 640 + index * 160, 160)

    def send_piece(self, k, distance):
        if distance:
            self.spread[k, 1][distance - 1].wait_recv()
        _, rows = self.piece_at(k, self.spots(k, 0)[0], distance)
        src = self.res.at[rows]
        self.spread[k, 0, distance] = [
            self.send(src, src, self.peer(k, 0, d)) for d in (1, 3)
        ]

    def pass_piece(self, k, distance):
        copies = self.spread[k, 0, distance]
        for copy in copies:
            copy.wait_recv()
        _, up, _, down = self.spots(k, 0)
        index, _ = self.piece_at(k, 0, distance)
        first = index < 2
        _, rows = self.piece_at(k, jnp.where(first, down, up), distance)
        src = self.res.at[rows]
        copies.append(self.send(src, src, self.peer(k, 0, jnp.where(first, 1, 3))))
        for slab in (down, up):
            self.hand_out(k * PART + slab * 640 + index * 160, 160)

    def close_spread(self, k, level):
        for copy in self.spread[k, level]:
            copy.wait_recv()
        _, rows = self.piece_at(k, self.spots(k, 0)[0], 0)
        self.res[rows] = self.piece[pl.ds(k * THIRD, 160)]

    def hand_out(self, start, count):
        rows = rows_at(start, count)
        lanes = pl.ds(pl.multiple_of(self.core * 128, 128), 128)
        near = pltpu.make_async_copy(
            self.res.at[rows], self.out.at[rows, lanes], self.send_sem.at[self.count]
        )
        self.count += 1
        near.start()
        self.outs.append((near, self.send(self.res.at[rows], self.out.at[rows, lanes], self.other)))

    def hand_own(self, k):
        self.hand_out(k * PART + self.spots(k, 0)[0] * 640, 640)

    def hand_far(self, k):
        for distance in range(4):
            self.spread[k, 0, distance][2].wait_recv()
        self.hand_out(k * PART + self.spots(k, 0)[2] * 640, 640)

    def end(self):
        for copy in self.sent:
            copy.wait_send()
        for near, far in self.outs:
            near.wait()
            far.wait_recv()


NEAR = [(1, 0), (-1, 0), (1, 1), (-1, -1), (1, -1), (-1, 1), (0, 1), (0, -1)]
NN = (((1,), (0,)), ((), ()))
NT = (((1,), (1,)), ((), ()))
TN = (((0,), (0,)), ((), ()))


def dot(left, right, dims=NN):
    return lax.dot_general(left, right, dims, preferred_element_type=jnp.float32)


def silu(value):
    return value * jax.nn.sigmoid(value)


def silu_slope(value):
    gate = jax.nn.sigmoid(value)
    return gate * (1.0 + value * (1.0 - gate))


def grid_of(rows, cols):
    return (
        lax.broadcasted_iota(jnp.int32, (rows, cols), 0),
        lax.broadcasted_iota(jnp.int32, (rows, cols), 1),
    )


def table(mask):
    return mask.astype(jnp.float32).astype(jnp.bfloat16)


def later_cell(block):
    lane = lax.broadcasted_iota(jnp.int32, block.shape, 1)
    return jnp.where(lane == 127, 0.0, pltpu.roll(block, 127, 1))


def earlier_cell(block):
    lane = lax.broadcasted_iota(jnp.int32, block.shape, 1)
    return jnp.where(lane == 0, 0.0, pltpu.roll(block, 1, 1))


def window_kernel(scale, features_hbm, labels, w_down_hbm, head_rows, w_mid_hbm, w_up_hbm,
                  grad_hbm, sum_out, features, w_down, grad_out, w_head, label_cells, w_mid, w_up, low, low_moved, down_pre, mid_pre, split, head, head_t,
                  partial, arrived, known, logit_grad, columns, back, back_moved,
                  part, got, work, half, slab0, slab1, slab2, sum0, sum1, piece, res,
                  load_sem, send_sem, recv_sem, sum_send, sum_recv):
    gx, gy = lax.axis_index("gx"), lax.axis_index("gy")

    def near(dx, dy):
        return (lax.rem(gx + (dx + 16), 16), lax.rem(gy + (dy + 8), 8))

    loads = [
        pltpu.make_async_copy(src, dst, load_sem.at[index])
        for index, (src, dst) in enumerate(
            [(w_mid_hbm, w_mid), (w_up_hbm, w_up), (features_hbm, features), (w_down_hbm, w_down)]
        )
    ]
    barrier = pltpu.get_barrier_semaphore()
    summing = Summing(
        part, sum_out, got, work, half, (slab0, slab1, slab2), (sum0, sum1), piece, res,
        sum_send, sum_recv,
    )
    peers = [near(dx, dy) for dx, dy in NEAR] + summing.peers()
    for peer in peers:
        pl.semaphore_signal(barrier, inc=1, device_id=peer, device_id_type=MESH)
    for index in (2, 3, 1, 0):
        loads[index].start()
    w_head[...] = jnp.zeros((16, 128), jnp.float32)
    w_head[pl.ds(0, 4), :] = head_rows[...].astype(jnp.float32)
    heads = w_head[...].astype(jnp.bfloat16)
    for a in (0, 1):
        label_cells[pl.ds(4 * a, 4), :] = labels[a].astype(jnp.float32)

    sent = []

    def exchange(stage, src, dst, places, apart=False):
        copies = []
        for index, (dx, dy) in enumerate(NEAR):
            src_x, dst_x, src_y, dst_y = places(dx, dy)
            copy = pltpu.make_async_remote_copy(
                src_ref=src.at[src_x, src_y],
                dst_ref=dst.at[index, dst_x, dst_y] if apart else dst.at[dst_x, dst_y],
                send_sem=send_sem.at[8 * stage + index], recv_sem=recv_sem.at[8 * stage + index],
                device_id=near(dx, dy), device_id_type=MESH,
            )
            copy.start()
            copies.append(copy)
        sent.extend(copies)
        return copies

    def finish(copies, buffer):
        for copy in copies:
            copy.wait_recv()
        wide, tall = buffer.shape[0], buffer.shape[1]

        @pl.when(gx == 0)
        def _():
            buffer[0] = jnp.zeros(buffer.shape[1:], buffer.dtype)

        @pl.when(gx == 15)
        def _():
            buffer[wide - 1] = jnp.zeros(buffer.shape[1:], buffer.dtype)

        @pl.when(gy == 0)
        def _():
            for x in range(wide):
                buffer[x, 0] = jnp.zeros(buffer.shape[2:], buffer.dtype)

        @pl.when(gy == 7)
        def _():
            for x in range(wide):
                buffer[x, tall - 1] = jnp.zeros(buffer.shape[2:], buffer.dtype)

    one = lambda i: pl.ds(i, 1)

    def brick_places(dx, dy):
        src_y = {0: pl.ds(1, 2), 1: one(2), -1: one(1)}[dy]
        dst_y = {0: pl.ds(1, 2), 1: one(0), -1: one(3)}[dy]
        return one(1), one(1 - dx), src_y, dst_y

    def upper_places(dx, dy):
        src_x = {0: pl.ds(1, 2), 1: one(2), -1: one(1)}[dx]
        dst_x = {0: pl.ds(1, 2), 1: one(0), -1: one(3)}[dx]
        src_y = {0: pl.ds(1, 4), 1: one(4), -1: one(1)}[dy]
        dst_y = {0: pl.ds(1, 4), 1: one(0), -1: one(5)}[dy]
        return src_x, dst_x, src_y, dst_y

    def spill_places(dx, dy):
        low_two, all_x, all_y = pl.ds(0, 2), pl.ds(0, 4), pl.ds(0, 6)
        src_x = {0: all_x, 1: pl.ds(2, 2), -1: low_two}[dx]
        dst_x = {0: all_x, 1: low_two, -1: pl.ds(2, 2)}[dx]
        src_y = {0: all_y, 1: pl.ds(4, 2), -1: low_two}[dy]
        dst_y = {0: all_y, 1: low_two, -1: pl.ds(4, 2)}[dy]
        return src_x, dst_x, src_y, dst_y

    inside_x = {0: (gx > 0).astype(jnp.float32), 1: (gx < 15).astype(jnp.float32)}
    inside_y = {0: (gy > 0).astype(jnp.float32), 1: (gy < 7).astype(jnp.float32)}

    def inside(value, x, y):
        value = value if x is None else value * inside_x[x]
        return value if y is None else value * inside_y[y]

    lanes = lambda i: pl.ds(i * 128, 128)
    rows, cols = grid_of(256, 256)
    apart = table(rows == jnp.where(cols < 128, 2 * cols, 2 * cols - 255))
    loads[2].wait()
    split[...] = dot(features[...], apart).astype(jnp.bfloat16)
    loads[3].wait()
    total = jnp.zeros((256, 256), jnp.float32)
    for a in (0, 1):
        for b in (0, 1):
            weight = jnp.concatenate([w_down[4 * a + 2 * b], w_down[4 * a + 2 * b + 1]], axis=1)
            cells = [
                jnp.concatenate(
                    [split[pl.ds((4 * a + 2 * y + b) * 128, 128), lanes(c)] for y in (0, 1)],
                    axis=1,
                )
                for c in (0, 1)
            ]
            total = total + dot(weight, jnp.concatenate(cells, axis=0))
    down_pre[...] = total
    total = silu(total).astype(jnp.bfloat16)
    low[1, 1] = total[:, :128]
    low[1, 2] = total[:, 128:]
    pl.semaphore_wait(barrier, len(peers))
    copies = exchange(0, low, low, brick_places)

    own_logits = [
        dot(heads, split[pl.ds(column * 128, 128), :])[:8] for column in range(8)
    ]
    label_rows = dot(label_cells[...].astype(jnp.bfloat16), apart)
    for a in (0, 1):
        for y in range(4):
            known[1 + a, 1 + y] = own_logits[4 * a + y]
            known[1 + a, 1 + y, pl.ds(4, 1), :] = label_rows[4 * a + y : 4 * a + y + 1, :]
    known_copies = exchange(2, known, known, upper_places)
    loads[1].wait()
    for tap in range(64):
        mixed = dot(heads, w_up[pl.ds(tap * 128, 128), :])
        head[pl.ds(tap * 8, 8), :] = mixed[:8]
    head_t[...] = jnp.transpose(head[...])
    loads[0].wait()

    finish(copies, low)
    rows, cols = grid_of(128, 256)
    moves = table(rows == jnp.where(cols < 128, cols - 1, cols - 127))
    for x in range(3):
        for y in range(4):
            low_moved[1, x, y] = low[x, y]
            both = dot(low[x, y], moves).astype(jnp.bfloat16)
            low_moved[0, x, y] = both[:, :128]
            low_moved[2, x, y] = both[:, 128:]
    total = jnp.zeros((256, 256), jnp.float32)
    for a in range(3):
        for b in range(3):
            taps = [9 * a + 3 * b + c for c in range(3)]
            weight = jnp.concatenate([w_mid[pl.ds(t * 256, 256), :] for t in taps], axis=1)
            cells = [
                jnp.concatenate([low_moved[c, a, b], low_moved[c, a, b + 1]], axis=1)
                for c in range(3)
            ]
            total = total + dot(weight, jnp.concatenate(cells, axis=0))
    mid_pre[...] = total
    mid = silu(total).astype(jnp.bfloat16)

    head_high = head[...].astype(jnp.bfloat16)
    head_low = (head[...] - head_high.astype(jnp.float32)).astype(jnp.bfloat16)
    spread = dot(head_high, mid) + dot(head_low, mid)
    for x in range(4):
        for y in range(6):
            block = None
            for cell in (0, 1):
                tap = y - 2 * cell
                if 0 <= tap < 4:
                    piece = spread[(4 * x + tap) * 32 : (4 * x + tap + 1) * 32,
                                   cell * 128 : cell * 128 + 128]
                    block = piece if block is None else block + piece
            partial[x, y, :, lanes(0)] = block[8:16] + earlier_cell(block[24:32])
            partial[x, y, :, lanes(1)] = block[16:24] + later_cell(block[0:8])
    copies = exchange(1, partial, arrived, spill_places, True)
    slope = silu_slope(mid_pre[...])
    head_t_high = head_t[...].astype(jnp.bfloat16)
    head_t_low = (head_t[...] - head_t_high.astype(jnp.float32)).astype(jnp.bfloat16)
    classes = lax.broadcasted_iota(jnp.int32, (8, 256), 0)
    for copy in known_copies + copies:
        copy.wait_recv()
    for x in range(4):
        for y in range(6):
            value = known[x, y] + partial[x, y]
            side_x = 0 if x < 2 else 1
            side_y = {0: 0, 1: 0, 4: 1, 5: 1}.get(y)
            from_x, from_y = 1 - 2 * side_x, None if side_y is None else 1 - 2 * side_y
            value = value + inside(arrived[NEAR.index((from_x, 0)), x, y], side_x, None)
            if side_y is not None:
                value = value + inside(arrived[NEAR.index((0, from_y)), x, y], None, side_y)
                value = value + inside(
                    arrived[NEAR.index((from_x, from_y)), x, y], side_x, side_y
                )
            target = (classes.astype(jnp.float32) == known[x, y, pl.ds(4, 1), :])
            grad = jax.nn.sigmoid(value) - target.astype(jnp.float32)
            grad = jnp.where(classes < 4, grad, 0.0).astype(jnp.bfloat16).astype(jnp.float32)
            grad = inside(grad, {0: 0, 3: 1}.get(x), {0: 0, 5: 1}.get(y))
            logit_grad[x, y] = grad
            even, odd = grad[:, :128], grad[:, 128:]
            block = jnp.concatenate([earlier_cell(odd), even, odd, later_cell(even)], axis=0)
            block = block.astype(jnp.bfloat16)
            for cell in (0, 1):
                tap = y - 2 * cell
                if 0 <= tap < 4:
                    columns[pl.ds((4 * x + tap) * 32, 32), lanes(cell)] = block
    mid_grad = dot(head_t_high, columns[...]) + dot(head_t_low, columns[...])
    mid_pre_grad = (mid_grad * slope).astype(jnp.bfloat16)
    turned = jnp.transpose(mid_pre_grad)
    back[1, 1] = turned[:128]
    back[1, 2] = turned[128:]

    def keep(start, value):
        value = value.astype(jnp.bfloat16)
        rows = pl.ds(start, value.shape[0])
        part[0, rows] = value[:, :128]
        part[1, rows] = value[:, 128:]

    thirds = range(3)
    for tap in range(27):
        a, b, c = tap // 9, tap // 3 % 3, tap % 3
        cells = jnp.concatenate([low_moved[c, a, b], low_moved[c, a, b + 1]], axis=1)
        keep(tap * 256, dot(mid_pre_grad, cells, NT))
        if tap in (9, 19):
            summing.send_other(tap // 10)
    keep(27 * 256, dot(columns[...], mid, NT))
    keep(27 * 256 + 512, jnp.zeros((256, 256), jnp.float32))
    summing.send_other(2)
    for k in thirds:
        summing.add_other(k)
        summing.open_ring(k)
    for k in thirds:
        summing.pass_ring(k)

    for k in thirds:
        summing.store_sum(k, 0)
        summing.open_level(k, 1)

    for k in thirds:
        summing.store_sum(k, 1)
        summing.open_level(k, 2)
    copies = exchange(3, back, back, brick_places)

    for k in thirds:
        summing.store_last(k, scale)
        summing.open_spread(k, 2)
    for k in thirds:
        summing.close_spread(k, 2)
        summing.open_spread(k, 1)
        summing.send_piece(k, 0)

    finish(copies, back)
    rows, cols = grid_of(256, 128)
    moves = table(cols == jnp.where(rows < 128, rows + 1, rows - 129))
    for x in range(3):
        for y in range(4):
            back_moved[x, y, :, pl.ds(256, 256)] = back[x, y]
            both = dot(moves, back[x, y]).astype(jnp.bfloat16)
            back_moved[x, y, :, pl.ds(0, 256)] = both[:128]
            back_moved[x, y, :, pl.ds(512, 256)] = both[128:]
    total = jnp.zeros((256, 256), jnp.float32)
    for a in range(3):
        for b in range(3):
            cells = jnp.concatenate(
                [back_moved[2 - a, 2 - b], back_moved[2 - a, 3 - b]], axis=0
            )
            total = total + dot(cells, w_mid[pl.ds((3 * a + b) * 768, 768), :])
    for distance in (1, 3, 2):
        for k in thirds:
            summing.send_piece(k, distance)
    for k in thirds:
        summing.hand_own(k)
    down_grad = (jnp.transpose(total) * silu_slope(down_pre[...])).astype(jnp.bfloat16)

    def finish_features(a):
        for b in (0, 1):
            weight = jnp.concatenate([w_down[4 * a + 2 * b], w_down[4 * a + 2 * b + 1]], axis=1)
            pieces = dot(weight, down_grad, TN)
            for cell in (0, 1):
                y = 2 * cell + b
                grad = jnp.concatenate(
                    [logit_grad[1 + a, 1 + y], jnp.zeros((8, 256), jnp.float32)], axis=0
                ).astype(jnp.bfloat16)
                hidden = dot(heads, grad, TN).astype(jnp.bfloat16).astype(jnp.float32)
                at = slice(cell * 128, cell * 128 + 128)
                whole = jnp.concatenate([pieces[:128, at], pieces[128:, at]], axis=1) + hidden
                grad_out[pl.ds((4 * a + y) * 128, 128), :] = dot(
                    whole.astype(jnp.bfloat16), apart, NT
                ).astype(jnp.bfloat16)

    finish_features(0)
    for distance in (0, 1, 3, 2):
        for k in thirds:
            summing.pass_piece(k, distance)
    finish_features(1)
    store_grad = pltpu.make_async_copy(grad_out, grad_hbm, load_sem.at[4])
    store_grad.start()
    for k in thirds:
        summing.hand_far(k)
    for copy in sent:
        copy.wait_send()
    summing.end()
    store_grad.wait()


def expand_kernel(sums, head_rows, mid_out, up_out, w_head, mixed, up, load_sem, mid_sem, up_sem):
    mid_copy = pltpu.make_async_copy(sums.at[pl.ds(0, 6912)], mid_out, mid_sem)
    load = pltpu.make_async_copy(sums.at[pl.ds(6912, 512)], mixed, load_sem)
    load.start()
    mid_copy.start()
    w_head[...] = jnp.zeros((16, 256), jnp.float32)
    w_head[pl.ds(0, 4), pl.ds(0, 128)] = head_rows[...].astype(jnp.float32)
    w_head[pl.ds(8, 4), pl.ds(128, 128)] = head_rows[...].astype(jnp.float32)
    heads = jnp.transpose(w_head[...]).astype(jnp.bfloat16)
    load.wait()
    stores = []
    for pair in range(32):
        pairs = dot(heads, mixed[pl.ds(pair * 16, 16), :])
        up[pl.ds(pair * 256, 256), :] = pairs.astype(jnp.bfloat16)
        if pair % 8 == 7:
            rows = pl.ds((pair - 7) * 256, 2048)
            store = pltpu.make_async_copy(up.at[rows], up_out.at[rows], up_sem.at[pair // 8])
            store.start()
            stores.append(store)
    for store in stores:
        store.wait()
    mid_copy.wait()


def expand(sums, w_head):
    vmem, hbm = pl.BlockSpec(memory_space=pltpu.VMEM), pl.BlockSpec(memory_space=pl.ANY)
    return pl.pallas_call(
        expand_kernel,
        out_shape=[
            jax.ShapeDtypeStruct((6912, 256), jnp.bfloat16),
            jax.ShapeDtypeStruct((8192, 256), jnp.bfloat16),
        ],
        in_specs=[hbm, vmem],
        out_specs=[hbm, hbm],
        scratch_shapes=[
            pltpu.VMEM((16, 256), jnp.float32),
            pltpu.VMEM((512, 256), jnp.bfloat16),
            pltpu.VMEM((8192, 256), jnp.bfloat16),
            pltpu.SemaphoreType.DMA(()),
            pltpu.SemaphoreType.DMA(()),
            pltpu.SemaphoreType.DMA((4,)),
        ],
        compiler_params=pltpu.CompilerParams(vmem_limit_bytes=32 * 2**20),
        cost_estimate=pl.CostEstimate(flops=10**8, bytes_accessed=12 * 10**6, transcendentals=0),
        name="expand",
    )(sums, w_head)


def window(features, labels, w_down, w_mid, w_up, w_head):
    half = lambda *shape: pltpu.VMEM(shape, jnp.bfloat16)
    full = lambda *shape: pltpu.VMEM(shape, jnp.float32)
    vmem, hbm = pl.BlockSpec(memory_space=pltpu.VMEM), pl.BlockSpec(memory_space=pl.ANY)
    return pl.pallas_call(
        functools.partial(window_kernel, 1.0 / math.sqrt(32768)),
        out_shape=[
            jax.ShapeDtypeStruct((1024, 256), jnp.bfloat16),
            jax.ShapeDtypeStruct((ROWS, 256), jnp.bfloat16),
        ],
        in_specs=[hbm, vmem, hbm, vmem, hbm, hbm],
        out_specs=[hbm, hbm],
        scratch_shapes=[
            half(1024, 256), half(8, 256, 128), half(1024, 256),
            full(16, 128), full(8, 256),
            half(27 * 256, 256), half(64 * 128, 256),
            half(3, 4, 256, 128), half(3, 3, 4, 256, 128),
            full(256, 256), full(256, 256),
            half(1024, 256), full(512, 256), full(256, 512),
            full(4, 6, 8, 256), full(8, 4, 6, 8, 256), full(4, 6, 8, 256), full(4, 6, 8, 256),
            half(512, 256), half(3, 4, 128, 256), half(3, 4, 128, 768),
            half(2, ROWS, 128), half(ROWS, 128), half(ROWS, 128),
            half(3, 2, 320, 128),
            half(3, 2, 640, 128), half(3, 3, 160, 128), half(3, 3, 48, 128),
            half(3 * 640, 128), half(3 * THIRD, 128), half(3 * THIRD, 128),
            half(ROWS, 128),
            pltpu.SemaphoreType.DMA((5,)),
            pltpu.SemaphoreType.DMA((32,)),
            pltpu.SemaphoreType.DMA((32,)),
            pltpu.SemaphoreType.DMA((200,)),
            pltpu.SemaphoreType.DMA((200,)),
        ],
        compiler_params=pltpu.CompilerParams(
            collective_id=8, has_side_effects=True, vmem_limit_bytes=60 * 2**20
        ),
        cost_estimate=pl.CostEstimate(flops=4 * 10**9, bytes_accessed=2 * 10**7, transcendentals=0),
        name="window",
    )(features, labels, w_down, w_head, w_mid, w_up)


def local(features, labels, w_down, w_mid, w_up, w_head):
    chans_up = features.shape[0]
    chans_mid = w_mid.shape[3]
    flat = features.transpose(1, 2, 0, 3).reshape(8 * chans_up, 256)
    grad, sums = window(
        flat, labels, w_down.reshape(8, chans_mid, chans_up),
        w_mid.reshape(27 * chans_mid, chans_mid), w_up.reshape(64 * chans_up, chans_mid), w_head,
    )
    feature_grad = grad.reshape(2, 4, chans_up, 256).transpose(2, 0, 1, 3)
    mid_out, up_out = expand(sums, w_head)
    return (
        feature_grad,
        mid_out.reshape(3, 3, 3, chans_mid, chans_mid),
        up_out.reshape(4, 4, 4, chans_up, chans_mid),
    )


def solution(mesh):
    return jax.shard_map(
        local,
        mesh=mesh,
        in_specs=(P(None, "gx", "gy", None), P("gx", "gy", None), P(), P(), P(), P()),
        out_specs=(P(None, "gx", "gy", None), P(), P()),
        check_vma=False,
    )
```

```python
import functools
import math

import jax
import jax.numpy as jnp
from jax import lax
from jax.experimental import pallas as pl
from jax.experimental.pallas import tpu as pltpu
from jax.sharding import PartitionSpec as P

MESH = pl.DeviceIdType.MESH
ROWS = 7680
PART = ROWS // 3
SIZES = [(640, 320), (160, 80), (48, 32)]
THIRD = 4 * 48
STEP = 320


def my_place():
    gx, gy = lax.axis_index("gx"), lax.axis_index("gy")
    return lax.div(gx, 4), lax.div(gy, 2), lax.rem(gx, 4), lax.rem(gy, 2)


def device_at(x, y, z, core):
    return (x * 4 + z, y * 2 + core)


def moved(place, axis, distance):
    spot = list(place)
    spot[axis] = lax.rem(spot[axis] + distance, 4)
    return device_at(*spot)


def rows_at(start, count):
    return pl.ds(pl.multiple_of(start, 16), count)


def for_rows(count, step, body):
    def one(i, carry):
        body(i * step)
        return carry

    lax.fori_loop(0, count // step, one, 0)


class Summing:
    axes = [(0, 1, 2), (1, 2, 0), (2, 0, 1)]

    def __init__(self, part, out, got, work, half, slabs, sums, piece, res, send_sem, recv_sem):
        self.part, self.out, self.got, self.work, self.half = part, out, got, work, half
        self.slabs, self.sums, self.piece, self.res = slabs, sums, piece, res
        self.send_sem, self.recv_sem = send_sem, recv_sem
        self.place = my_place()
        self.core = self.place[3]
        self.other = device_at(*self.place[:3], 1 - self.core)
        self.count, self.sent, self.outs = 0, [], []
        self.first, self.opened, self.spread = {}, {}, {}

    def peers(self):
        places = [moved(self.place, axis, d) for axis in range(3) for d in (1, 2, 3)]
        return [self.other] + places

    def send(self, src, dst, target):
        copy = pltpu.make_async_remote_copy(
            src_ref=src, dst_ref=dst, send_sem=self.send_sem.at[self.count],
            recv_sem=self.recv_sem.at[self.count], device_id=target, device_id_type=MESH,
        )
        self.count += 1
        copy.start()
        self.sent.append(copy)
        return copy

    def spots(self, k, level):
        p = self.place[self.axes[k][level]]
        return p, lax.rem(p + 1, 4), lax.rem(p + 2, 4), lax.rem(p + 3, 4)

    def peer(self, k, level, distance):
        return moved(self.place, self.axes[k][level], distance)

    def send_other(self, k):
        rows = pl.ds(k * PART, PART)
        src = self.part.at[1 - self.core, rows]
        self.first[k] = self.send(src, self.got.at[rows], self.other)

    def add_other(self, k):
        self.first[k].wait_recv()

        def body(start):
            rows = rows_at(k * PART + start, STEP)
            self.work[rows] = self.part[self.core, rows] + self.got[rows]

        for_rows(PART, STEP, body)

    def open_ring(self, k):
        size, cut = SIZES[0]
        _, up, far, down = self.spots(k, 0)
        after, before = self.peer(k, 0, 1), self.peer(k, 0, 3)
        base = k * PART
        src, slab = self.work, self.slabs[0]
        copies = []
        for start in (0, 160):
            for side, target in ((0, after), (1, before)):
                rows = rows_at(base + far * size + side * cut + start, 160)
                copies.append(
                    self.send(src.at[rows], self.half.at[k, side, pl.ds(start, 160)], target)
                )
        copies += [
            self.send(src.at[rows_at(base + up * size + cut, cut)],
                      slab.at[k, 0, pl.ds(cut, cut)], after),
            self.send(src.at[rows_at(base + down * size, cut)], slab.at[k, 1, pl.ds(0, cut)],
                      before),
        ]
        self.opened[k, 0] = copies

    def pass_ring(self, k):
        size, cut = SIZES[0]
        _, up, _, down = self.spots(k, 0)
        base = k * PART
        slab, copies = self.slabs[0], self.opened[k, 0]
        for step in (0, 160):
            for side, start, target, at in (
                (0, base + up * size, self.peer(k, 0, 1), 0),
                (1, base + down * size + cut, self.peer(k, 0, 3), cut),
            ):
                copies[step // 80 + side].wait_recv()
                rows = rows_at(start + step, 160)
                self.work[rows] = self.work[rows] + self.half[k, side, pl.ds(step, 160)]
                copies.append(
                    self.send(self.work.at[rows], slab.at[k, side, pl.ds(at + step, 160)], target)
                )

    def open_level(self, k, level):
        size = SIZES[level][0]
        src, base = self.sums[level - 1], k * 4 * size
        spots = self.spots(k, level)
        self.opened[k, level] = [
            self.send(src.at[rows_at(base + spots[d] * size, size)],
                      self.slabs[level].at[k, d - 1], self.peer(k, level, d))
            for d in (1, 2, 3)
        ]

    def close_level(self, k, level, store):
        size = SIZES[level][0]
        step = (STEP, 160, 48)[level]
        copies = self.opened[k, level]
        for copy in copies[4:] if level == 0 else copies:
            copy.wait_recv()
        src, base = (self.work, k * PART) if level == 0 else (self.sums[level - 1], k * 4 * size)
        base = base + self.spots(k, level)[0] * size
        slab = self.slabs[level]

        def body(start):
            total = src[rows_at(base + start, step)].astype(jnp.float32)
            for side in range(slab.shape[1]):
                total = total + slab[k, side, rows_at(start, step)].astype(jnp.float32)
            store(start, total)

        for_rows(size, step, body)

    def store_sum(self, k, level):
        pitch = PART // 4 if level == 0 else THIRD

        def store(start, total):
            self.sums[level][rows_at(k * pitch + start, total.shape[0])] = total.astype(jnp.bfloat16)

        self.close_level(k, level, store)
        if level == 1:
            self.sums[1][pl.ds(k * THIRD + 160, 32)] = jnp.zeros((32, 128), jnp.bfloat16)

    def store_last(self, k, scale):
        def store(start, total):
            rows = rows_at(k * THIRD + self.spots(k, 2)[0] * 48 + start, 48)
            self.piece[rows] = (total * scale).astype(jnp.bfloat16)

        self.close_level(k, 2, store)

    def spread_rows(self, k, level):
        if level == 2:
            return self.piece, k * THIRD
        base = k * PART
        if level == 1:
            base = base + self.spots(k, 0)[0] * SIZES[0][0]
        return self.res, base

    def open_spread(self, k, level):
        size = SIZES[level][0]
        ref, base = self.spread_rows(k, level)
        rows = rows_at(base + self.spots(k, level)[0] * size, size)
        self.spread[k, level] = [
            self.send(ref.at[rows], ref.at[rows], self.peer(k, level, d)) for d in (1, 2, 3)
        ]

    def piece_at(self, k, slab, distance):
        index = self.spots(k, 1)[(4 - distance) % 4]
        return index, rows_at(k * PART + slab * 640 + index * 160, 160)

    def send_piece(self, k, distance):
        if distance:
            self.spread[k, 1][distance - 1].wait_recv()
        _, rows = self.piece_at(k, self.spots(k, 0)[0], distance)
        src = self.res.at[rows]
        self.spread[k, 0, distance] = [
            self.send(src, src, self.peer(k, 0, d)) for d in (1, 3)
        ]

    def pass_piece(self, k, distance):
        copies = self.spread[k, 0, distance]
        for copy in copies:
            copy.wait_recv()
        _, up, _, down = self.spots(k, 0)
        index, _ = self.piece_at(k, 0, distance)
        first = index < 2
        _, rows = self.piece_at(k, jnp.where(first, down, up), distance)
        src = self.res.at[rows]
        copies.append(self.send(src, src, self.peer(k, 0, jnp.where(first, 1, 3))))
        for slab in (down, up):
            self.hand_out(k * PART + slab * 640 + index * 160, 160)

    def close_spread(self, k, level):
        for copy in self.spread[k, level]:
            copy.wait_recv()
        _, rows = self.piece_at(k, self.spots(k, 0)[0], 0)
        self.res[rows] = self.piece[pl.ds(k * THIRD, 160)]

    def hand_out(self, start, count):
        rows = rows_at(start, count)
        lanes = pl.ds(pl.multiple_of(self.core * 128, 128), 128)
        near = pltpu.make_async_copy(
            self.res.at[rows], self.out.at[rows, lanes], self.send_sem.at[self.count]
        )
        self.count += 1
        near.start()
        self.outs.append((near, self.send(self.res.at[rows], self.out.at[rows, lanes], self.other)))

    def hand_own(self, k):
        self.hand_out(k * PART + self.spots(k, 0)[0] * 640, 640)

    def hand_far(self, k):
        for distance in range(4):
            self.spread[k, 0, distance][2].wait_recv()
        self.hand_out(k * PART + self.spots(k, 0)[2] * 640, 640)

    def end(self):
        for copy in self.sent:
            copy.wait_send()
        for near, far in self.outs:
            near.wait()
            far.wait_recv()


NEAR = [(1, 0), (-1, 0), (1, 1), (-1, -1), (1, -1), (-1, 1), (0, 1), (0, -1)]
NN = (((1,), (0,)), ((), ()))
NT = (((1,), (1,)), ((), ()))
TN = (((0,), (0,)), ((), ()))


def dot(left, right, dims=NN):
    return lax.dot_general(left, right, dims, preferred_element_type=jnp.float32)


def silu(value):
    return value * jax.nn.sigmoid(value)


def silu_slope(value):
    gate = jax.nn.sigmoid(value)
    return gate * (1.0 + value * (1.0 - gate))


def grid_of(rows, cols):
    return (
        lax.broadcasted_iota(jnp.int32, (rows, cols), 0),
        lax.broadcasted_iota(jnp.int32, (rows, cols), 1),
    )


def table(mask):
    return mask.astype(jnp.float32).astype(jnp.bfloat16)


def later_cell(block):
    lane = lax.broadcasted_iota(jnp.int32, block.shape, 1)
    return jnp.where(lane == 127, 0.0, pltpu.roll(block, 127, 1))


def earlier_cell(block):
    lane = lax.broadcasted_iota(jnp.int32, block.shape, 1)
    return jnp.where(lane == 0, 0.0, pltpu.roll(block, 1, 1))


def window_kernel(scale, features_hbm, labels, w_down_hbm, head_rows, w_mid_hbm, w_up_hbm,
                  grad_hbm, sum_out, features, w_down, grad_out, w_head, label_cells, w_mid, w_up, low, low_moved, down_pre, mid_pre, split, head, head_t,
                  partial, arrived, known, logit_grad, columns, back, back_moved,
                  part, got, work, half, slab0, slab1, slab2, sum0, sum1, piece, res,
                  load_sem, send_sem, recv_sem, sum_send, sum_recv):
    gx, gy = lax.axis_index("gx"), lax.axis_index("gy")

    def near(dx, dy):
        return (lax.rem(gx + (dx + 16), 16), lax.rem(gy + (dy + 8), 8))

    loads = [
        pltpu.make_async_copy(src, dst, load_sem.at[index])
        for index, (src, dst) in enumerate(
            [(w_mid_hbm, w_mid), (w_up_hbm, w_up), (features_hbm, features), (w_down_hbm, w_down)]
        )
    ]
    barrier = pltpu.get_barrier_semaphore()
    summing = Summing(
        part, sum_out, got, work, half, (slab0, slab1, slab2), (sum0, sum1), piece, res,
        sum_send, sum_recv,
    )
    peers = [near(dx, dy) for dx, dy in NEAR] + summing.peers()
    for peer in peers:
        pl.semaphore_signal(barrier, inc=1, device_id=peer, device_id_type=MESH)
    for index in (2, 3, 1, 0):
        loads[index].start()
    w_head[...] = jnp.zeros((16, 128), jnp.float32)
    w_head[pl.ds(0, 4), :] = head_rows[...].astype(jnp.float32)
    heads = w_head[...].astype(jnp.bfloat16)
    for a in (0, 1):
        label_cells[pl.ds(4 * a, 4), :] = labels[a].astype(jnp.float32)

    sent = []

    def exchange(stage, src, dst, places, apart=False):
        copies = []
        for index, (dx, dy) in enumerate(NEAR):
            src_x, dst_x, src_y, dst_y = places(dx, dy)
            copy = pltpu.make_async_remote_copy(
                src_ref=src.at[src_x, src_y],
                dst_ref=dst.at[index, dst_x, dst_y] if apart else dst.at[dst_x, dst_y],
                send_sem=send_sem.at[8 * stage + index], recv_sem=recv_sem.at[8 * stage + index],
                device_id=near(dx, dy), device_id_type=MESH,
            )
            copy.start()
            copies.append(copy)
        sent.extend(copies)
        return copies

    def finish(copies, buffer):
        for copy in copies:
            copy.wait_recv()
        wide, tall = buffer.shape[0], buffer.shape[1]

        @pl.when(gx == 0)
        def _():
            buffer[0] = jnp.zeros(buffer.shape[1:], buffer.dtype)

        @pl.when(gx == 15)
        def _():
            buffer[wide - 1] = jnp.zeros(buffer.shape[1:], buffer.dtype)

        @pl.when(gy == 0)
        def _():
            for x in range(wide):
                buffer[x, 0] = jnp.zeros(buffer.shape[2:], buffer.dtype)

        @pl.when(gy == 7)
        def _():
            for x in range(wide):
                buffer[x, tall - 1] = jnp.zeros(buffer.shape[2:], buffer.dtype)

    one = lambda i: pl.ds(i, 1)

    def brick_places(dx, dy):
        src_y = {0: pl.ds(1, 2), 1: one(2), -1: one(1)}[dy]
        dst_y = {0: pl.ds(1, 2), 1: one(0), -1: one(3)}[dy]
        return one(1), one(1 - dx), src_y, dst_y

    def upper_places(dx, dy):
        src_x = {0: pl.ds(1, 2), 1: one(2), -1: one(1)}[dx]
        dst_x = {0: pl.ds(1, 2), 1: one(0), -1: one(3)}[dx]
        src_y = {0: pl.ds(1, 4), 1: one(4), -1: one(1)}[dy]
        dst_y = {0: pl.ds(1, 4), 1: one(0), -1: one(5)}[dy]
        return src_x, dst_x, src_y, dst_y

    def spill_places(dx, dy):
        low_two, all_x, all_y = pl.ds(0, 2), pl.ds(0, 4), pl.ds(0, 6)
        src_x = {0: all_x, 1: pl.ds(2, 2), -1: low_two}[dx]
        dst_x = {0: all_x, 1: low_two, -1: pl.ds(2, 2)}[dx]
        src_y = {0: all_y, 1: pl.ds(4, 2), -1: low_two}[dy]
        dst_y = {0: all_y, 1: low_two, -1: pl.ds(4, 2)}[dy]
        return src_x, dst_x, src_y, dst_y

    inside_x = {0: (gx > 0).astype(jnp.float32), 1: (gx < 15).astype(jnp.float32)}
    inside_y = {0: (gy > 0).astype(jnp.float32), 1: (gy < 7).astype(jnp.float32)}

    def inside(value, x, y):
        value = value if x is None else value * inside_x[x]
        return value if y is None else value * inside_y[y]

    lanes = lambda i: pl.ds(i * 128, 128)
    rows, cols = grid_of(256, 256)
    apart = table(rows == jnp.where(cols < 128, 2 * cols, 2 * cols - 255))
    loads[2].wait()
    split[...] = dot(features[...], apart).astype(jnp.bfloat16)
    loads[3].wait()
    total = jnp.zeros((256, 256), jnp.float32)
    for a in (0, 1):
        for b in (0, 1):
            weight = jnp.concatenate([w_down[4 * a + 2 * b], w_down[4 * a + 2 * b + 1]], axis=1)
            cells = [
                jnp.concatenate(
                    [split[pl.ds((4 * a + 2 * y + b) * 128, 128), lanes(c)] for y in (0, 1)],
                    axis=1,
                )
                for c in (0, 1)
            ]
            total = total + dot(weight, jnp.concatenate(cells, axis=0))
    down_pre[...] = total
    total = silu(total).astype(jnp.bfloat16)
    low[1, 1] = total[:, :128]
    low[1, 2] = total[:, 128:]
    pl.semaphore_wait(barrier, len(peers))
    copies = exchange(0, low, low, brick_places)

    own_logits = [
        dot(heads, split[pl.ds(column * 128, 128), :])[:8] for column in range(8)
    ]
    label_rows = dot(label_cells[...].astype(jnp.bfloat16), apart)
    for a in (0, 1):
        for y in range(4):
            known[1 + a, 1 + y] = own_logits[4 * a + y]
            known[1 + a, 1 + y, pl.ds(4, 1), :] = label_rows[4 * a + y : 4 * a + y + 1, :]
    known_copies = exchange(2, known, known, upper_places)
    loads[1].wait()
    for tap in range(64):
        mixed = dot(heads, w_up[pl.ds(tap * 128, 128), :])
        head[pl.ds(tap * 8, 8), :] = mixed[:8]
    head_t[...] = jnp.transpose(head[...])
    loads[0].wait()

    finish(copies, low)
    rows, cols = grid_of(128, 256)
    moves = table(rows == jnp.where(cols < 128, cols - 1, cols - 127))
    for x in range(3):
        for y in range(4):
            low_moved[1, x, y] = low[x, y]
            both = dot(low[x, y], moves).astype(jnp.bfloat16)
            low_moved[0, x, y] = both[:, :128]
            low_moved[2, x, y] = both[:, 128:]
    total = jnp.zeros((256, 256), jnp.float32)
    for a in range(3):
        for b in range(3):
            taps = [9 * a + 3 * b + c for c in range(3)]
            weight = jnp.concatenate([w_mid[pl.ds(t * 256, 256), :] for t in taps], axis=1)
            cells = [
                jnp.concatenate([low_moved[c, a, b], low_moved[c, a, b + 1]], axis=1)
                for c in range(3)
            ]
            total = total + dot(weight, jnp.concatenate(cells, axis=0))
    mid_pre[...] = total
    mid = silu(total).astype(jnp.bfloat16)

    head_high = head[...].astype(jnp.bfloat16)
    head_low = (head[...] - head_high.astype(jnp.float32)).astype(jnp.bfloat16)
    spread = dot(head_high, mid) + dot(head_low, mid)
    for x in range(4):
        for y in range(6):
            block = None
            for cell in (0, 1):
                tap = y - 2 * cell
                if 0 <= tap < 4:
                    piece = spread[(4 * x + tap) * 32 : (4 * x + tap + 1) * 32,
                                   cell * 128 : cell * 128 + 128]
                    block = piece if block is None else block + piece
            partial[x, y, :, lanes(0)] = block[8:16] + earlier_cell(block[24:32])
            partial[x, y, :, lanes(1)] = block[16:24] + later_cell(block[0:8])
    copies = exchange(1, partial, arrived, spill_places, True)
    slope = silu_slope(mid_pre[...])
    head_t_high = head_t[...].astype(jnp.bfloat16)
    head_t_low = (head_t[...] - head_t_high.astype(jnp.float32)).astype(jnp.bfloat16)
    classes = lax.broadcasted_iota(jnp.int32, (8, 256), 0)
    for copy in known_copies + copies:
        copy.wait_recv()
    for x in range(4):
        for y in range(6):
            value = known[x, y] + partial[x, y]
            side_x = 0 if x < 2 else 1
            side_y = {0: 0, 1: 0, 4: 1, 5: 1}.get(y)
            from_x, from_y = 1 - 2 * side_x, None if side_y is None else 1 - 2 * side_y
            value = value + inside(arrived[NEAR.index((from_x, 0)), x, y], side_x, None)
            if side_y is not None:
                value = value + inside(arrived[NEAR.index((0, from_y)), x, y], None, side_y)
                value = value + inside(
                    arrived[NEAR.index((from_x, from_y)), x, y], side_x, side_y
                )
            target = (classes.astype(jnp.float32) == known[x, y, pl.ds(4, 1), :])
            grad = jax.nn.sigmoid(value) - target.astype(jnp.float32)
            grad = jnp.where(classes < 4, grad, 0.0).astype(jnp.bfloat16).astype(jnp.float32)
            grad = inside(grad, {0: 0, 3: 1}.get(x), {0: 0, 5: 1}.get(y))
            logit_grad[x, y] = grad
            even, odd = grad[:, :128], grad[:, 128:]
            block = jnp.concatenate([earlier_cell(odd), even, odd, later_cell(even)], axis=0)
            block = block.astype(jnp.bfloat16)
            for cell in (0, 1):
                tap = y - 2 * cell
                if 0 <= tap < 4:
                    columns[pl.ds((4 * x + tap) * 32, 32), lanes(cell)] = block
    mid_grad = dot(head_t_high, columns[...]) + dot(head_t_low, columns[...])
    mid_pre_grad = (mid_grad * slope).astype(jnp.bfloat16)
    turned = jnp.transpose(mid_pre_grad)
    back[1, 1] = turned[:128]
    back[1, 2] = turned[128:]

    def keep(start, value):
        value = value.astype(jnp.bfloat16)
        rows = pl.ds(start, value.shape[0])
        part[0, rows] = value[:, :128]
        part[1, rows] = value[:, 128:]

    thirds = range(3)
    for tap in range(27):
        a, b, c = tap // 9, tap // 3 % 3, tap % 3
        cells = jnp.concatenate([low_moved[c, a, b], low_moved[c, a, b + 1]], axis=1)
        keep(tap * 256, dot(mid_pre_grad, cells, NT))
        if tap in (9, 19):
            summing.send_other(tap // 10)
    keep(27 * 256, dot(columns[...], mid, NT))
    keep(27 * 256 + 512, jnp.zeros((256, 256), jnp.float32))
    summing.send_other(2)
    for k in thirds:
        summing.add_other(k)
        summing.open_ring(k)
    for k in thirds:
        summing.pass_ring(k)

    for k in thirds:
        summing.store_sum(k, 0)
        summing.open_level(k, 1)

    for k in thirds:
        summing.store_sum(k, 1)
        summing.open_level(k, 2)
    copies = exchange(3, back, back, brick_places)

    for k in thirds:
        summing.store_last(k, scale)
        summing.open_spread(k, 2)
    for k in thirds:
        summing.close_spread(k, 2)
        summing.open_spread(k, 1)
        summing.send_piece(k, 0)

    finish(copies, back)
    rows, cols = grid_of(256, 128)
    moves = table(cols == jnp.where(rows < 128, rows + 1, rows - 129))
    for x in range(3):
        for y in range(4):
            back_moved[x, y, :, pl.ds(256, 256)] = back[x, y]
            both = dot(moves, back[x, y]).astype(jnp.bfloat16)
            back_moved[x, y, :, pl.ds(0, 256)] = both[:128]
            back_moved[x, y, :, pl.ds(512, 256)] = both[128:]
    total = jnp.zeros((256, 256), jnp.float32)
    for a in range(3):
        for b in range(3):
            cells = jnp.concatenate(
                [back_moved[2 - a, 2 - b], back_moved[2 - a, 3 - b]], axis=0
            )
            total = total + dot(cells, w_mid[pl.ds((3 * a + b) * 768, 768), :])
    for distance in (1, 3, 2):
        for k in thirds:
            summing.send_piece(k, distance)
    for k in thirds:
        summing.pass_piece(k, 0)
    for k in thirds:
        summing.hand_own(k)
    down_grad = (jnp.transpose(total) * silu_slope(down_pre[...])).astype(jnp.bfloat16)

    def finish_features(a):
        for b in (0, 1):
            weight = jnp.concatenate([w_down[4 * a + 2 * b], w_down[4 * a + 2 * b + 1]], axis=1)
            pieces = dot(weight, down_grad, TN)
            for cell in (0, 1):
                y = 2 * cell + b
                grad = jnp.concatenate(
                    [logit_grad[1 + a, 1 + y], jnp.zeros((8, 256), jnp.float32)], axis=0
                ).astype(jnp.bfloat16)
                hidden = dot(heads, grad, TN).astype(jnp.bfloat16).astype(jnp.float32)
                at = slice(cell * 128, cell * 128 + 128)
                whole = jnp.concatenate([pieces[:128, at], pieces[128:, at]], axis=1) + hidden
                grad_out[pl.ds((4 * a + y) * 128, 128), :] = dot(
                    whole.astype(jnp.bfloat16), apart, NT
                ).astype(jnp.bfloat16)

    for k in thirds:
        summing.pass_piece(k, 1)
    finish_features(0)
    for distance in (3, 2):
        for k in thirds:
            summing.pass_piece(k, distance)
    finish_features(1)
    store_grad = pltpu.make_async_copy(grad_out, grad_hbm, load_sem.at[4])
    store_grad.start()
    for k in thirds:
        summing.hand_far(k)
    for copy in sent:
        copy.wait_send()
    summing.end()
    store_grad.wait()


def expand_kernel(sums, head_rows, mid_out, up_out, w_head, mixed, up, load_sem, mid_sem, up_sem):
    mid_copy = pltpu.make_async_copy(sums.at[pl.ds(0, 6912)], mid_out, mid_sem)
    load = pltpu.make_async_copy(sums.at[pl.ds(6912, 512)], mixed, load_sem)
    load.start()
    mid_copy.start()
    w_head[...] = jnp.zeros((16, 256), jnp.float32)
    w_head[pl.ds(0, 4), pl.ds(0, 128)] = head_rows[...].astype(jnp.float32)
    w_head[pl.ds(8, 4), pl.ds(128, 128)] = head_rows[...].astype(jnp.float32)
    heads = jnp.transpose(w_head[...]).astype(jnp.bfloat16)
    load.wait()
    stores = []
    for pair in range(32):
        pairs = dot(heads, mixed[pl.ds(pair * 16, 16), :])
        up[pl.ds(pair * 256, 256), :] = pairs.astype(jnp.bfloat16)
        if pair % 8 == 7:
            rows = pl.ds((pair - 7) * 256, 2048)
            store = pltpu.make_async_copy(up.at[rows], up_out.at[rows], up_sem.at[pair // 8])
            store.start()
            stores.append(store)
    for store in stores:
        store.wait()
    mid_copy.wait()


def expand(sums, w_head):
    vmem, hbm = pl.BlockSpec(memory_space=pltpu.VMEM), pl.BlockSpec(memory_space=pl.ANY)
    return pl.pallas_call(
        expand_kernel,
        out_shape=[
            jax.ShapeDtypeStruct((6912, 256), jnp.bfloat16),
            jax.ShapeDtypeStruct((8192, 256), jnp.bfloat16),
        ],
        in_specs=[hbm, vmem],
        out_specs=[hbm, hbm],
        scratch_shapes=[
            pltpu.VMEM((16, 256), jnp.float32),
            pltpu.VMEM((512, 256), jnp.bfloat16),
            pltpu.VMEM((8192, 256), jnp.bfloat16),
            pltpu.SemaphoreType.DMA(()),
            pltpu.SemaphoreType.DMA(()),
            pltpu.SemaphoreType.DMA((4,)),
        ],
        compiler_params=pltpu.CompilerParams(vmem_limit_bytes=32 * 2**20),
        cost_estimate=pl.CostEstimate(flops=10**8, bytes_accessed=12 * 10**6, transcendentals=0),
        name="expand",
    )(sums, w_head)


def window(features, labels, w_down, w_mid, w_up, w_head):
    half = lambda *shape: pltpu.VMEM(shape, jnp.bfloat16)
    full = lambda *shape: pltpu.VMEM(shape, jnp.float32)
    vmem, hbm = pl.BlockSpec(memory_space=pltpu.VMEM), pl.BlockSpec(memory_space=pl.ANY)
    return pl.pallas_call(
        functools.partial(window_kernel, 1.0 / math.sqrt(32768)),
        out_shape=[
            jax.ShapeDtypeStruct((1024, 256), jnp.bfloat16),
            jax.ShapeDtypeStruct((ROWS, 256), jnp.bfloat16),
        ],
        in_specs=[hbm, vmem, hbm, vmem, hbm, hbm],
        out_specs=[hbm, hbm],
        scratch_shapes=[
            half(1024, 256), half(8, 256, 128), half(1024, 256),
            full(16, 128), full(8, 256),
            half(27 * 256, 256), half(64 * 128, 256),
            half(3, 4, 256, 128), half(3, 3, 4, 256, 128),
            full(256, 256), full(256, 256),
            half(1024, 256), full(512, 256), full(256, 512),
            full(4, 6, 8, 256), full(8, 4, 6, 8, 256), full(4, 6, 8, 256), full(4, 6, 8, 256),
            half(512, 256), half(3, 4, 128, 256), half(3, 4, 128, 768),
            half(2, ROWS, 128), half(ROWS, 128), half(ROWS, 128),
            half(3, 2, 320, 128),
            half(3, 2, 640, 128), half(3, 3, 160, 128), half(3, 3, 48, 128),
            half(3 * 640, 128), half(3 * THIRD, 128), half(3 * THIRD, 128),
            half(ROWS, 128),
            pltpu.SemaphoreType.DMA((5,)),
            pltpu.SemaphoreType.DMA((32,)),
            pltpu.SemaphoreType.DMA((32,)),
            pltpu.SemaphoreType.DMA((200,)),
            pltpu.SemaphoreType.DMA((200,)),
        ],
        compiler_params=pltpu.CompilerParams(
            collective_id=8, has_side_effects=True, vmem_limit_bytes=60 * 2**20
        ),
        cost_estimate=pl.CostEstimate(flops=4 * 10**9, bytes_accessed=2 * 10**7, transcendentals=0),
        name="window",
    )(features, labels, w_down, w_head, w_mid, w_up)


def local(features, labels, w_down, w_mid, w_up, w_head):
    chans_up = features.shape[0]
    chans_mid = w_mid.shape[3]
    flat = features.transpose(1, 2, 0, 3).reshape(8 * chans_up, 256)
    grad, sums = window(
        flat, labels, w_down.reshape(8, chans_mid, chans_up),
        w_mid.reshape(27 * chans_mid, chans_mid), w_up.reshape(64 * chans_up, chans_mid), w_head,
    )
    feature_grad = grad.reshape(2, 4, chans_up, 256).transpose(2, 0, 1, 3)
    mid_out, up_out = expand(sums, w_head)
    return (
        feature_grad,
        mid_out.reshape(3, 3, 3, chans_mid, chans_mid),
        up_out.reshape(4, 4, 4, chans_up, chans_mid),
    )


def solution(mesh):
    return jax.shard_map(
        local,
        mesh=mesh,
        in_specs=(P(None, "gx", "gy", None), P("gx", "gy", None), P(), P(), P(), P()),
        out_specs=(P(None, "gx", "gy", None), P(), P()),
        check_vma=False,
    )
```

```python
import functools
import math

import jax
import jax.numpy as jnp
from jax import lax
from jax.experimental import pallas as pl
from jax.experimental.pallas import tpu as pltpu
from jax.sharding import PartitionSpec as P

MESH = pl.DeviceIdType.MESH
ROWS = 7680
PART = ROWS // 3
SIZES = [(640, 320), (160, 80), (48, 32)]
THIRD = 4 * 48
STEP = 320


def my_place():
    gx, gy = lax.axis_index("gx"), lax.axis_index("gy")
    return lax.div(gx, 4), lax.div(gy, 2), lax.rem(gx, 4), lax.rem(gy, 2)


def device_at(x, y, z, core):
    return (x * 4 + z, y * 2 + core)


def moved(place, axis, distance):
    spot = list(place)
    spot[axis] = lax.rem(spot[axis] + distance, 4)
    return device_at(*spot)


def rows_at(start, count):
    return pl.ds(pl.multiple_of(start, 16), count)


def for_rows(count, step, body):
    def one(i, carry):
        body(i * step)
        return carry

    lax.fori_loop(0, count // step, one, 0)


class Summing:
    axes = [(0, 1, 2), (1, 2, 0), (2, 0, 1)]

    def __init__(self, part, out, got, work, half, slabs, sums, piece, res, send_sem, recv_sem):
        self.part, self.out, self.got, self.work, self.half = part, out, got, work, half
        self.slabs, self.sums, self.piece, self.res = slabs, sums, piece, res
        self.send_sem, self.recv_sem = send_sem, recv_sem
        self.place = my_place()
        self.core = self.place[3]
        self.other = device_at(*self.place[:3], 1 - self.core)
        self.count, self.sent, self.outs = 0, [], []
        self.first, self.opened, self.spread = {}, {}, {}

    def peers(self):
        places = [moved(self.place, axis, d) for axis in range(3) for d in (1, 2, 3)]
        return [self.other] + places

    def send(self, src, dst, target):
        copy = pltpu.make_async_remote_copy(
            src_ref=src, dst_ref=dst, send_sem=self.send_sem.at[self.count],
            recv_sem=self.recv_sem.at[self.count], device_id=target, device_id_type=MESH,
        )
        self.count += 1
        copy.start()
        self.sent.append(copy)
        return copy

    def spots(self, k, level):
        p = self.place[self.axes[k][level]]
        return p, lax.rem(p + 1, 4), lax.rem(p + 2, 4), lax.rem(p + 3, 4)

    def peer(self, k, level, distance):
        return moved(self.place, self.axes[k][level], distance)

    def send_other(self, k):
        rows = pl.ds(k * (PART // 2), PART // 2)
        src = self.part.at[1 - self.core, rows]
        self.first[k] = self.send(src, self.got.at[rows], self.other)

    def add_other(self, k):
        self.first[2 * k].wait_recv()
        self.first[2 * k + 1].wait_recv()

        def body(start):
            rows = rows_at(k * PART + start, STEP)
            self.work[rows] = self.part[self.core, rows] + self.got[rows]

        for_rows(PART, STEP, body)

    def open_ring(self, k):
        size, cut = SIZES[0]
        _, up, far, down = self.spots(k, 0)
        after, before = self.peer(k, 0, 1), self.peer(k, 0, 3)
        base = k * PART
        src, slab = self.work, self.slabs[0]
        copies = []
        for start in (0, 160):
            for side, target in ((0, after), (1, before)):
                rows = rows_at(base + far * size + side * cut + start, 160)
                copies.append(
                    self.send(src.at[rows], self.half.at[k, side, pl.ds(start, 160)], target)
                )
        copies += [
            self.send(src.at[rows_at(base + up * size + cut, cut)],
                      slab.at[k, 0, pl.ds(cut, cut)], after),
            self.send(src.at[rows_at(base + down * size, cut)], slab.at[k, 1, pl.ds(0, cut)],
                      before),
        ]
        self.opened[k, 0] = copies

    def pass_ring(self, k):
        size, cut = SIZES[0]
        _, up, _, down = self.spots(k, 0)
        base = k * PART
        slab, copies = self.slabs[0], self.opened[k, 0]
        for step in (0, 160):
            for side, start, target, at in (
                (0, base + up * size, self.peer(k, 0, 1), 0),
                (1, base + down * size + cut, self.peer(k, 0, 3), cut),
            ):
                copies[step // 80 + side].wait_recv()
                rows = rows_at(start + step, 160)
                self.work[rows] = self.work[rows] + self.half[k, side, pl.ds(step, 160)]
                copies.append(
                    self.send(self.work.at[rows], slab.at[k, side, pl.ds(at + step, 160)], target)
                )

    def open_level(self, k, level):
        size = SIZES[level][0]
        src, base = self.sums[level - 1], k * 4 * size
        spots = self.spots(k, level)
        self.opened[k, level] = [
            self.send(src.at[rows_at(base + spots[d] * size, size)],
                      self.slabs[level].at[k, d - 1], self.peer(k, level, d))
            for d in (1, 2, 3)
        ]

    def close_level(self, k, level, store):
        size = SIZES[level][0]
        step = (STEP, 160, 48)[level]
        copies = self.opened[k, level]
        for copy in copies[4:] if level == 0 else copies:
            copy.wait_recv()
        src, base = (self.work, k * PART) if level == 0 else (self.sums[level - 1], k * 4 * size)
        base = base + self.spots(k, level)[0] * size
        slab = self.slabs[level]

        def body(start):
            total = src[rows_at(base + start, step)].astype(jnp.float32)
            for side in range(slab.shape[1]):
                total = total + slab[k, side, rows_at(start, step)].astype(jnp.float32)
            store(start, total)

        for_rows(size, step, body)

    def store_sum(self, k, level):
        pitch = PART // 4 if level == 0 else THIRD

        def store(start, total):
            self.sums[level][rows_at(k * pitch + start, total.shape[0])] = total.astype(jnp.bfloat16)

        self.close_level(k, level, store)
        if level == 1:
            self.sums[1][pl.ds(k * THIRD + 160, 32)] = jnp.zeros((32, 128), jnp.bfloat16)

    def store_last(self, k, scale):
        def store(start, total):
            rows = rows_at(k * THIRD + self.spots(k, 2)[0] * 48 + start, 48)
            self.piece[rows] = (total * scale).astype(jnp.bfloat16)

        self.close_level(k, 2, store)

    def spread_rows(self, k, level):
        if level == 2:
            return self.piece, k * THIRD
        base = k * PART
        if level == 1:
            base = base + self.spots(k, 0)[0] * SIZES[0][0]
        return self.res, base

    def open_spread(self, k, level):
        size = SIZES[level][0]
        ref, base = self.spread_rows(k, level)
        rows = rows_at(base + self.spots(k, level)[0] * size, size)
        self.spread[k, level] = [
            self.send(ref.at[rows], ref.at[rows], self.peer(k, level, d)) for d in (1, 2, 3)
        ]

    def piece_at(self, k, slab, distance):
        index = self.spots(k, 1)[(4 - distance) % 4]
        return index, rows_at(k * PART + slab * 640 + index * 160, 160)

    def send_piece(self, k, distance):
        if distance:
            self.spread[k, 1][distance - 1].wait_recv()
        _, rows = self.piece_at(k, self.spots(k, 0)[0], distance)
        src = self.res.at[rows]
        self.spread[k, 0, distance] = [
            self.send(src, src, self.peer(k, 0, d)) for d in (1, 3)
        ]

    def pass_piece(self, k, distance):
        copies = self.spread[k, 0, distance]
        for copy in copies:
            copy.wait_recv()
        _, up, _, down = self.spots(k, 0)
        index, _ = self.piece_at(k, 0, distance)
        first = index < 2
        _, rows = self.piece_at(k, jnp.where(first, down, up), distance)
        src = self.res.at[rows]
        copies.append(self.send(src, src, self.peer(k, 0, jnp.where(first, 1, 3))))
        for slab in (down, up):
            self.hand_out(k * PART + slab * 640 + index * 160, 160)

    def close_spread(self, k, level):
        for copy in self.spread[k, level]:
            copy.wait_recv()
        _, rows = self.piece_at(k, self.spots(k, 0)[0], 0)
        self.res[rows] = self.piece[pl.ds(k * THIRD, 160)]

    def hand_out(self, start, count):
        rows = rows_at(start, count)
        lanes = pl.ds(pl.multiple_of(self.core * 128, 128), 128)
        near = pltpu.make_async_copy(
            self.res.at[rows], self.out.at[rows, lanes], self.send_sem.at[self.count]
        )
        self.count += 1
        near.start()
        self.outs.append((near, self.send(self.res.at[rows], self.out.at[rows, lanes], self.other)))

    def hand_own(self, k):
        self.hand_out(k * PART + self.spots(k, 0)[0] * 640, 640)

    def hand_far(self, k):
        for distance in range(4):
            self.spread[k, 0, distance][2].wait_recv()
        self.hand_out(k * PART + self.spots(k, 0)[2] * 640, 640)

    def end(self):
        for copy in self.sent:
            copy.wait_send()
        for near, far in self.outs:
            near.wait()
            far.wait_recv()


NEAR = [(1, 0), (-1, 0), (1, 1), (-1, -1), (1, -1), (-1, 1), (0, 1), (0, -1)]
NN = (((1,), (0,)), ((), ()))
NT = (((1,), (1,)), ((), ()))
TN = (((0,), (0,)), ((), ()))


def dot(left, right, dims=NN):
    return lax.dot_general(left, right, dims, preferred_element_type=jnp.float32)


def silu(value):
    return value * jax.nn.sigmoid(value)


def silu_slope(value):
    gate = jax.nn.sigmoid(value)
    return gate * (1.0 + value * (1.0 - gate))


def grid_of(rows, cols):
    return (
        lax.broadcasted_iota(jnp.int32, (rows, cols), 0),
        lax.broadcasted_iota(jnp.int32, (rows, cols), 1),
    )


def table(mask):
    return mask.astype(jnp.float32).astype(jnp.bfloat16)


def later_cell(block):
    lane = lax.broadcasted_iota(jnp.int32, block.shape, 1)
    return jnp.where(lane == 127, 0.0, pltpu.roll(block, 127, 1))


def earlier_cell(block):
    lane = lax.broadcasted_iota(jnp.int32, block.shape, 1)
    return jnp.where(lane == 0, 0.0, pltpu.roll(block, 1, 1))


def window_kernel(scale, features_hbm, labels, w_down_hbm, head_rows, w_mid_hbm, w_up_hbm,
                  grad_hbm, sum_out, features, w_down, grad_out, w_head, label_cells, w_mid, w_up, low, low_moved, down_pre, mid_pre, split, head, head_t,
                  partial, arrived, known, logit_grad, columns, back, back_moved,
                  part, got, work, half, slab0, slab1, slab2, sum0, sum1, piece, res,
                  load_sem, send_sem, recv_sem, sum_send, sum_recv):
    gx, gy = lax.axis_index("gx"), lax.axis_index("gy")

    def near(dx, dy):
        return (lax.rem(gx + (dx + 16), 16), lax.rem(gy + (dy + 8), 8))

    loads = [
        pltpu.make_async_copy(src, dst, load_sem.at[index])
        for index, (src, dst) in enumerate(
            [(w_mid_hbm, w_mid), (w_up_hbm, w_up), (features_hbm, features), (w_down_hbm, w_down)]
        )
    ]
    barrier = pltpu.get_barrier_semaphore()
    summing = Summing(
        part, sum_out, got, work, half, (slab0, slab1, slab2), (sum0, sum1), piece, res,
        sum_send, sum_recv,
    )
    peers = [near(dx, dy) for dx, dy in NEAR] + summing.peers()
    for peer in peers:
        pl.semaphore_signal(barrier, inc=1, device_id=peer, device_id_type=MESH)
    for index in (2, 3, 1, 0):
        loads[index].start()
    w_head[...] = jnp.zeros((16, 128), jnp.float32)
    w_head[pl.ds(0, 4), :] = head_rows[...].astype(jnp.float32)
    heads = w_head[...].astype(jnp.bfloat16)
    for a in (0, 1):
        label_cells[pl.ds(4 * a, 4), :] = labels[a].astype(jnp.float32)

    sent = []

    def exchange(stage, src, dst, places, apart=False):
        copies = []
        for index, (dx, dy) in enumerate(NEAR):
            src_x, dst_x, src_y, dst_y = places(dx, dy)
            copy = pltpu.make_async_remote_copy(
                src_ref=src.at[src_x, src_y],
                dst_ref=dst.at[index, dst_x, dst_y] if apart else dst.at[dst_x, dst_y],
                send_sem=send_sem.at[8 * stage + index], recv_sem=recv_sem.at[8 * stage + index],
                device_id=near(dx, dy), device_id_type=MESH,
            )
            copy.start()
            copies.append(copy)
        sent.extend(copies)
        return copies

    def finish(copies, buffer):
        for copy in copies:
            copy.wait_recv()
        wide, tall = buffer.shape[0], buffer.shape[1]

        @pl.when(gx == 0)
        def _():
            buffer[0] = jnp.zeros(buffer.shape[1:], buffer.dtype)

        @pl.when(gx == 15)
        def _():
            buffer[wide - 1] = jnp.zeros(buffer.shape[1:], buffer.dtype)

        @pl.when(gy == 0)
        def _():
            for x in range(wide):
                buffer[x, 0] = jnp.zeros(buffer.shape[2:], buffer.dtype)

        @pl.when(gy == 7)
        def _():
            for x in range(wide):
                buffer[x, tall - 1] = jnp.zeros(buffer.shape[2:], buffer.dtype)

    one = lambda i: pl.ds(i, 1)

    def brick_places(dx, dy):
        src_y = {0: pl.ds(1, 2), 1: one(2), -1: one(1)}[dy]
        dst_y = {0: pl.ds(1, 2), 1: one(0), -1: one(3)}[dy]
        return one(1), one(1 - dx), src_y, dst_y

    def upper_places(dx, dy):
        src_x = {0: pl.ds(1, 2), 1: one(2), -1: one(1)}[dx]
        dst_x = {0: pl.ds(1, 2), 1: one(0), -1: one(3)}[dx]
        src_y = {0: pl.ds(1, 4), 1: one(4), -1: one(1)}[dy]
        dst_y = {0: pl.ds(1, 4), 1: one(0), -1: one(5)}[dy]
        return src_x, dst_x, src_y, dst_y

    def spill_places(dx, dy):
        low_two, all_x, all_y = pl.ds(0, 2), pl.ds(0, 4), pl.ds(0, 6)
        src_x = {0: all_x, 1: pl.ds(2, 2), -1: low_two}[dx]
        dst_x = {0: all_x, 1: low_two, -1: pl.ds(2, 2)}[dx]
        src_y = {0: all_y, 1: pl.ds(4, 2), -1: low_two}[dy]
        dst_y = {0: all_y, 1: low_two, -1: pl.ds(4, 2)}[dy]
        return src_x, dst_x, src_y, dst_y

    inside_x = {0: (gx > 0).astype(jnp.float32), 1: (gx < 15).astype(jnp.float32)}
    inside_y = {0: (gy > 0).astype(jnp.float32), 1: (gy < 7).astype(jnp.float32)}

    def inside(value, x, y):
        value = value if x is None else value * inside_x[x]
        return value if y is None else value * inside_y[y]

    lanes = lambda i: pl.ds(i * 128, 128)
    rows, cols = grid_of(256, 256)
    apart = table(rows == jnp.where(cols < 128, 2 * cols, 2 * cols - 255))
    loads[2].wait()
    split[...] = dot(features[...], apart).astype(jnp.bfloat16)
    loads[3].wait()
    total = jnp.zeros((256, 256), jnp.float32)
    for a in (0, 1):
        for b in (0, 1):
            weight = jnp.concatenate([w_down[4 * a + 2 * b], w_down[4 * a + 2 * b + 1]], axis=1)
            cells = [
                jnp.concatenate(
                    [split[pl.ds((4 * a + 2 * y + b) * 128, 128), lanes(c)] for y in (0, 1)],
                    axis=1,
                )
                for c in (0, 1)
            ]
            total = total + dot(weight, jnp.concatenate(cells, axis=0))
    down_pre[...] = total
    total = silu(total).astype(jnp.bfloat16)
    low[1, 1] = total[:, :128]
    low[1, 2] = total[:, 128:]
    pl.semaphore_wait(barrier, len(peers))
    copies = exchange(0, low, low, brick_places)

    own_logits = [
        dot(heads, split[pl.ds(column * 128, 128), :])[:8] for column in range(8)
    ]
    label_rows = dot(label_cells[...].astype(jnp.bfloat16), apart)
    for a in (0, 1):
        for y in range(4):
            known[1 + a, 1 + y] = own_logits[4 * a + y]
            known[1 + a, 1 + y, pl.ds(4, 1), :] = label_rows[4 * a + y : 4 * a + y + 1, :]
    known_copies = exchange(2, known, known, upper_places)
    loads[1].wait()
    for tap in range(64):
        mixed = dot(heads, w_up[pl.ds(tap * 128, 128), :])
        head[pl.ds(tap * 8, 8), :] = mixed[:8]
    head_t[...] = jnp.transpose(head[...])
    loads[0].wait()

    finish(copies, low)
    rows, cols = grid_of(128, 256)
    moves = table(rows == jnp.where(cols < 128, cols - 1, cols - 127))
    for x in range(3):
        for y in range(4):
            low_moved[1, x, y] = low[x, y]
            both = dot(low[x, y], moves).astype(jnp.bfloat16)
            low_moved[0, x, y] = both[:, :128]
            low_moved[2, x, y] = both[:, 128:]
    total = jnp.zeros((256, 256), jnp.float32)
    for a in range(3):
        for b in range(3):
            taps = [9 * a + 3 * b + c for c in range(3)]
            weight = jnp.concatenate([w_mid[pl.ds(t * 256, 256), :] for t in taps], axis=1)
            cells = [
                jnp.concatenate([low_moved[c, a, b], low_moved[c, a, b + 1]], axis=1)
                for c in range(3)
            ]
            total = total + dot(weight, jnp.concatenate(cells, axis=0))
    mid_pre[...] = total
    mid = silu(total).astype(jnp.bfloat16)

    head_high = head[...].astype(jnp.bfloat16)
    head_low = (head[...] - head_high.astype(jnp.float32)).astype(jnp.bfloat16)
    spread = dot(head_high, mid) + dot(head_low, mid)
    for x in range(4):
        for y in range(6):
            block = None
            for cell in (0, 1):
                tap = y - 2 * cell
                if 0 <= tap < 4:
                    piece = spread[(4 * x + tap) * 32 : (4 * x + tap + 1) * 32,
                                   cell * 128 : cell * 128 + 128]
                    block = piece if block is None else block + piece
            partial[x, y, :, lanes(0)] = block[8:16] + earlier_cell(block[24:32])
            partial[x, y, :, lanes(1)] = block[16:24] + later_cell(block[0:8])
    copies = exchange(1, partial, arrived, spill_places, True)
    slope = silu_slope(mid_pre[...])
    head_t_high = head_t[...].astype(jnp.bfloat16)
    head_t_low = (head_t[...] - head_t_high.astype(jnp.float32)).astype(jnp.bfloat16)
    classes = lax.broadcasted_iota(jnp.int32, (8, 256), 0)
    for copy in known_copies + copies:
        copy.wait_recv()
    for x in range(4):
        for y in range(6):
            value = known[x, y] + partial[x, y]
            side_x = 0 if x < 2 else 1
            side_y = {0: 0, 1: 0, 4: 1, 5: 1}.get(y)
            from_x, from_y = 1 - 2 * side_x, None if side_y is None else 1 - 2 * side_y
            value = value + inside(arrived[NEAR.index((from_x, 0)), x, y], side_x, None)
            if side_y is not None:
                value = value + inside(arrived[NEAR.index((0, from_y)), x, y], None, side_y)
                value = value + inside(
                    arrived[NEAR.index((from_x, from_y)), x, y], side_x, side_y
                )
            target = (classes.astype(jnp.float32) == known[x, y, pl.ds(4, 1), :])
            grad = jax.nn.sigmoid(value) - target.astype(jnp.float32)
            grad = jnp.where(classes < 4, grad, 0.0).astype(jnp.bfloat16).astype(jnp.float32)
            grad = inside(grad, {0: 0, 3: 1}.get(x), {0: 0, 5: 1}.get(y))
            logit_grad[x, y] = grad
            even, odd = grad[:, :128], grad[:, 128:]
            block = jnp.concatenate([earlier_cell(odd), even, odd, later_cell(even)], axis=0)
            block = block.astype(jnp.bfloat16)
            for cell in (0, 1):
                tap = y - 2 * cell
                if 0 <= tap < 4:
                    columns[pl.ds((4 * x + tap) * 32, 32), lanes(cell)] = block
    mid_grad = dot(head_t_high, columns[...]) + dot(head_t_low, columns[...])
    mid_pre_grad = (mid_grad * slope).astype(jnp.bfloat16)
    turned = jnp.transpose(mid_pre_grad)
    back[1, 1] = turned[:128]
    back[1, 2] = turned[128:]

    def keep(start, value):
        value = value.astype(jnp.bfloat16)
        rows = pl.ds(start, value.shape[0])
        part[0, rows] = value[:, :128]
        part[1, rows] = value[:, 128:]

    thirds = range(3)
    for tap in range(27):
        a, b, c = tap // 9, tap // 3 % 3, tap % 3
        cells = jnp.concatenate([low_moved[c, a, b], low_moved[c, a, b + 1]], axis=1)
        keep(tap * 256, dot(mid_pre_grad, cells, NT))
        if tap % 5 == 4:
            summing.send_other(tap // 5)
    keep(27 * 256, dot(columns[...], mid, NT))
    keep(27 * 256 + 512, jnp.zeros((256, 256), jnp.float32))
    summing.send_other(5)
    for k in thirds:
        summing.add_other(k)
        summing.open_ring(k)
    for k in thirds:
        summing.pass_ring(k)

    for k in thirds:
        summing.store_sum(k, 0)
        summing.open_level(k, 1)

    for k in thirds:
        summing.store_sum(k, 1)
        summing.open_level(k, 2)
    copies = exchange(3, back, back, brick_places)

    for k in thirds:
        summing.store_last(k, scale)
        summing.open_spread(k, 2)
    for k in thirds:
        summing.close_spread(k, 2)
        summing.open_spread(k, 1)
        summing.send_piece(k, 0)

    finish(copies, back)
    rows, cols = grid_of(256, 128)
    moves = table(cols == jnp.where(rows < 128, rows + 1, rows - 129))
    for x in range(3):
        for y in range(4):
            back_moved[x, y, :, pl.ds(256, 256)] = back[x, y]
            both = dot(moves, back[x, y]).astype(jnp.bfloat16)
            back_moved[x, y, :, pl.ds(0, 256)] = both[:128]
            back_moved[x, y, :, pl.ds(512, 256)] = both[128:]
    total = jnp.zeros((256, 256), jnp.float32)
    for a in range(3):
        for b in range(3):
            cells = jnp.concatenate(
                [back_moved[2 - a, 2 - b], back_moved[2 - a, 3 - b]], axis=0
            )
            total = total + dot(cells, w_mid[pl.ds((3 * a + b) * 768, 768), :])
    for distance in (1, 3, 2):
        for k in thirds:
            summing.send_piece(k, distance)
    for k in thirds:
        summing.hand_own(k)
    down_grad = (jnp.transpose(total) * silu_slope(down_pre[...])).astype(jnp.bfloat16)

    def finish_features(a):
        for b in (0, 1):
            weight = jnp.concatenate([w_down[4 * a + 2 * b], w_down[4 * a + 2 * b + 1]], axis=1)
            pieces = dot(weight, down_grad, TN)
            for cell in (0, 1):
                y = 2 * cell + b
                grad = jnp.concatenate(
                    [logit_grad[1 + a, 1 + y], jnp.zeros((8, 256), jnp.float32)], axis=0
                ).astype(jnp.bfloat16)
                hidden = dot(heads, grad, TN).astype(jnp.bfloat16).astype(jnp.float32)
                at = slice(cell * 128, cell * 128 + 128)
                whole = jnp.concatenate([pieces[:128, at], pieces[128:, at]], axis=1) + hidden
                grad_out[pl.ds((4 * a + y) * 128, 128), :] = dot(
                    whole.astype(jnp.bfloat16), apart, NT
                ).astype(jnp.bfloat16)

    finish_features(0)
    for distance in (0, 1, 3, 2):
        for k in thirds:
            summing.pass_piece(k, distance)
    finish_features(1)
    store_grad = pltpu.make_async_copy(grad_out, grad_hbm, load_sem.at[4])
    store_grad.start()
    for k in thirds:
        summing.hand_far(k)
    for copy in sent:
        copy.wait_send()
    summing.end()
    store_grad.wait()


def expand_kernel(sums, head_rows, mid_out, up_out, w_head, mixed, up, load_sem, mid_sem, up_sem):
    mid_copy = pltpu.make_async_copy(sums.at[pl.ds(0, 6912)], mid_out, mid_sem)
    load = pltpu.make_async_copy(sums.at[pl.ds(6912, 512)], mixed, load_sem)
    load.start()
    mid_copy.start()
    w_head[...] = jnp.zeros((16, 256), jnp.float32)
    w_head[pl.ds(0, 4), pl.ds(0, 128)] = head_rows[...].astype(jnp.float32)
    w_head[pl.ds(8, 4), pl.ds(128, 128)] = head_rows[...].astype(jnp.float32)
    heads = jnp.transpose(w_head[...]).astype(jnp.bfloat16)
    load.wait()
    stores = []
    for pair in range(32):
        pairs = dot(heads, mixed[pl.ds(pair * 16, 16), :])
        up[pl.ds(pair * 256, 256), :] = pairs.astype(jnp.bfloat16)
        if pair % 8 == 7:
            rows = pl.ds((pair - 7) * 256, 2048)
            store = pltpu.make_async_copy(up.at[rows], up_out.at[rows], up_sem.at[pair // 8])
            store.start()
            stores.append(store)
    for store in stores:
        store.wait()
    mid_copy.wait()


def expand(sums, w_head):
    vmem, hbm = pl.BlockSpec(memory_space=pltpu.VMEM), pl.BlockSpec(memory_space=pl.ANY)
    return pl.pallas_call(
        expand_kernel,
        out_shape=[
            jax.ShapeDtypeStruct((6912, 256), jnp.bfloat16),
            jax.ShapeDtypeStruct((8192, 256), jnp.bfloat16),
        ],
        in_specs=[hbm, vmem],
        out_specs=[hbm, hbm],
        scratch_shapes=[
            pltpu.VMEM((16, 256), jnp.float32),
            pltpu.VMEM((512, 256), jnp.bfloat16),
            pltpu.VMEM((8192, 256), jnp.bfloat16),
            pltpu.SemaphoreType.DMA(()),
            pltpu.SemaphoreType.DMA(()),
            pltpu.SemaphoreType.DMA((4,)),
        ],
        compiler_params=pltpu.CompilerParams(vmem_limit_bytes=32 * 2**20),
        cost_estimate=pl.CostEstimate(flops=10**8, bytes_accessed=12 * 10**6, transcendentals=0),
        name="expand",
    )(sums, w_head)


def window(features, labels, w_down, w_mid, w_up, w_head):
    half = lambda *shape: pltpu.VMEM(shape, jnp.bfloat16)
    full = lambda *shape: pltpu.VMEM(shape, jnp.float32)
    vmem, hbm = pl.BlockSpec(memory_space=pltpu.VMEM), pl.BlockSpec(memory_space=pl.ANY)
    return pl.pallas_call(
        functools.partial(window_kernel, 1.0 / math.sqrt(32768)),
        out_shape=[
            jax.ShapeDtypeStruct((1024, 256), jnp.bfloat16),
            jax.ShapeDtypeStruct((ROWS, 256), jnp.bfloat16),
        ],
        in_specs=[hbm, vmem, hbm, vmem, hbm, hbm],
        out_specs=[hbm, hbm],
        scratch_shapes=[
            half(1024, 256), half(8, 256, 128), half(1024, 256),
            full(16, 128), full(8, 256),
            half(27 * 256, 256), half(64 * 128, 256),
            half(3, 4, 256, 128), half(3, 3, 4, 256, 128),
            full(256, 256), full(256, 256),
            half(1024, 256), full(512, 256), full(256, 512),
            full(4, 6, 8, 256), full(8, 4, 6, 8, 256), full(4, 6, 8, 256), full(4, 6, 8, 256),
            half(512, 256), half(3, 4, 128, 256), half(3, 4, 128, 768),
            half(2, ROWS, 128), half(ROWS, 128), half(ROWS, 128),
            half(3, 2, 320, 128),
            half(3, 2, 640, 128), half(3, 3, 160, 128), half(3, 3, 48, 128),
            half(3 * 640, 128), half(3 * THIRD, 128), half(3 * THIRD, 128),
            half(ROWS, 128),
            pltpu.SemaphoreType.DMA((5,)),
            pltpu.SemaphoreType.DMA((32,)),
            pltpu.SemaphoreType.DMA((32,)),
            pltpu.SemaphoreType.DMA((200,)),
            pltpu.SemaphoreType.DMA((200,)),
        ],
        compiler_params=pltpu.CompilerParams(
            collective_id=8, has_side_effects=True, vmem_limit_bytes=60 * 2**20
        ),
        cost_estimate=pl.CostEstimate(flops=4 * 10**9, bytes_accessed=2 * 10**7, transcendentals=0),
        name="window",
    )(features, labels, w_down, w_head, w_mid, w_up)


def local(features, labels, w_down, w_mid, w_up, w_head):
    chans_up = features.shape[0]
    chans_mid = w_mid.shape[3]
    flat = features.transpose(1, 2, 0, 3).reshape(8 * chans_up, 256)
    grad, sums = window(
        flat, labels, w_down.reshape(8, chans_mid, chans_up),
        w_mid.reshape(27 * chans_mid, chans_mid), w_up.reshape(64 * chans_up, chans_mid), w_head,
    )
    feature_grad = grad.reshape(2, 4, chans_up, 256).transpose(2, 0, 1, 3)
    mid_out, up_out = expand(sums, w_head)
    return (
        feature_grad,
        mid_out.reshape(3, 3, 3, chans_mid, chans_mid),
        up_out.reshape(4, 4, 4, chans_up, chans_mid),
    )


def solution(mesh):
    return jax.shard_map(
        local,
        mesh=mesh,
        in_specs=(P(None, "gx", "gy", None), P("gx", "gy", None), P(), P(), P(), P()),
        out_specs=(P(None, "gx", "gy", None), P(), P()),
        check_vma=False,
    )
```
